32 devices in a mesh: dp: 8 (over z, x), narrow: 4 (over y, core).
Axes of the slice: x: 2, y: 2, z: 4, core: 2. Of those that a mesh axis runs over, the one named last changes fastest.
Arguments:
- view_maps: bfloat16 [2, 18816, 2048], P(None, ('dp', 'narrow')), may hold values from -33 to 33
- crop_maps: bfloat16 [2, 6912, 2048], P(None, ('dp', 'narrow')), may hold values from -33 to 33
- image_ids: int32 [2, 192], replicated, may hold values from 0 to 95
- w_reduce: bfloat16 [2048, 512], replicated, may hold values from -0.125 to 0.125
- gain_one: float32 [512], replicated, may hold values from 0.25 to 1.75
- shift_one: float32 [512], replicated, may hold values from -0.5 to 0.5
- w_spatial: bfloat16 [4608, 512], replicated, may hold values from -0.09375 to 0.09375
- gain_two: float32 [512], replicated, may hold values from 0.25 to 1.75
- shift_two: float32 [512], replicated, may hold values from -0.5 to 0.5
- w_expand: bfloat16 [512, 2048], replicated, may hold values from -0.25 to 0.25
- gain_three: float32 [2048], replicated, may hold values from 0.25 to 1.75
- shift_three: float32 [2048], replicated, may hold values from -0.5 to 0.5
- w_hidden: bfloat16 [2048, 2048], replicated, may hold values from -0.125 to 0.125
- gain_head: float32 [2048], replicated, may hold values from 0.25 to 1.75
- shift_head: float32 [2048], replicated, may hold values from -0.5 to 0.5
- w_embed: bfloat16 [2048, 128], replicated, may hold values from -0.125 to 0.125
Outputs:
- anchor_loss: float32 [2, 1152], P(None, ('dp', 'narrow'))
- grad_views: float32 [2, 18816, 2048], P(None, ('dp', 'narrow'))
- grad_crops: float32 [2, 6912, 2048], P(None, ('dp', 'narrow'))
- grad_w_reduce: float32 [2048, 512], P('dp')
- grad_gain_one: float32 [512], replicated
- grad_shift_one: float32 [512], replicated
- grad_w_spatial: float32 [4608, 512], P('dp')
- grad_gain_two: float32 [512], replicated
- grad_shift_two: float32 [512], replicated
- grad_w_expand: float32 [512, 2048], P('dp')
- grad_gain_three: float32 [2048], replicated
- grad_shift_three: float32 [2048], replicated
- grad_w_hidden: float32 [2048, 2048], P('dp')
- grad_gain_head: float32 [2048], replicated
- grad_shift_head: float32 [2048], replicated
- grad_w_embed: float32 [2048, 128], P('dp')
The draws below stay inside these ranges and needn't reach their ends.
Inputs may be any that keep to these rules, and one draw needn't show every extreme that they name: image_ids[m, i] is the id of image i of micro-batch m; embeddings of micro-batch m whose images have equal ids are positives of each other.
All inputs are finite; a program needn't handle non-finite values.
Results may differ from the reference program's by a relative error of at most 0.022.
Values may be sent and summed in bfloat16 or wider, within the bound.
No kernel may reach another device: no remote copies, remote signals or barrier semaphores. Data moves between devices by JAX's collectives and lax.ppermute only.
A program may use at most 256 MiB of HBM per device.

```python
import jax
import jax.numpy as jnp
from jax import lax

C = 2048
M = 512
H = 2048
E = 128
VIEWS = 2
CROPS = 4
VSIDE = 7
CSIDE = 3
MICRO = 2
IMAGES = 192
EMB = 1152


def image_scale(key):
    scale_key = jax.random.fold_in(key, 11)
    position = jnp.arange(IMAGES, dtype=jnp.float32) / IMAGES
    jitter = jax.random.uniform(scale_key, (MICRO, IMAGES), minval=0.0, maxval=1.2)
    return 0.4 * jnp.exp(jnp.log(3.0) * position + jitter)


def channel_scale(key):
    return jnp.exp(jax.random.uniform(jax.random.fold_in(key, 13), (C,), minval=-0.7, maxval=0.7))


def draw_maps(key, salt_value, pixels_each):
    noise_key = jax.random.fold_in(key, salt_value)
    full_shape = (MICRO, IMAGES, pixels_each, C)
    noise_draw = jnp.clip(jax.random.normal(noise_key, full_shape), -4.0, 4.0)
    values = noise_draw * image_scale(key)[:, :, None, None] * channel_scale(key)
    return values.reshape(MICRO, IMAGES * pixels_each, C)


def draw_view_maps(key, part):
    return draw_maps(key, 1, VIEWS * VSIDE * VSIDE).astype(jnp.bfloat16)


def draw_crop_maps(key, part):
    return draw_maps(key, 5, CROPS * CSIDE * CSIDE).astype(jnp.bfloat16)


def touch_ends(entries, stream_key, least, largest):
    shape = entries.shape
    place = [jax.random.randint(jax.random.fold_in(stream_key, axis), (), 0, shape[axis]) for axis in range(len(shape))]
    entries = entries.at[tuple(place)].set(least)
    longest = shape.index(max(shape))
    place[longest] = (place[longest] + 1) % shape[longest]
    return entries.at[tuple(place)].set(largest)


def gaussian(own_key, shape, deviation, limit, kind=jnp.bfloat16):
    drawn = deviation * jax.random.normal(own_key, shape, jnp.float32)
    return jnp.clip(drawn, min=-limit, max=limit).astype(kind)


def setup_inputs(seed: int = 0) -> dict:
    streams_of = jax.random.split(jax.random.key(seed), 17)
    return {
        "view_maps": draw_view_maps(jax.random.fold_in(streams_of[16], 71), 0),
        "crop_maps": draw_crop_maps(jax.random.fold_in(streams_of[16], 71), 0),
        "image_ids": touch_ends(jax.random.randint(streams_of[2], (MICRO, IMAGES), 0, IMAGES // 2), jax.random.fold_in(streams_of[2], 1), 0, (IMAGES // 2) - 1).astype(jnp.int32),
        "w_reduce": gaussian(streams_of[3], (C, M), C ** -0.5, 0.125),
        "gain_one": jnp.clip(1.0 + 0.15 * jax.random.normal(streams_of[4], (M,), jnp.float32), 0.25, 1.75),
        "shift_one": jnp.clip(jax.random.uniform(streams_of[5], (M,), jnp.float32, -0.5, 0.5), -0.5, 0.5),
        "w_spatial": gaussian(streams_of[6], (9 * M, M), (9 * M) ** -0.5, 0.09375),
        "gain_two": jnp.clip(1.0 + 0.15 * jax.random.normal(streams_of[7], (M,), jnp.float32), 0.25, 1.75),
        "shift_two": jnp.clip(jax.random.uniform(streams_of[8], (M,), jnp.float32, -0.5, 0.5), -0.5, 0.5),
        "w_expand": gaussian(streams_of[9], (M, C), M ** -0.5, 0.25),
        "gain_three": jnp.clip(1.0 + 0.15 * jax.random.normal(streams_of[10], (C,), jnp.float32), 0.25, 1.75),
        "shift_three": jnp.clip(jax.random.uniform(streams_of[11], (C,), jnp.float32, -0.5, 0.5), -0.5, 0.5),
        "w_hidden": gaussian(streams_of[12], (C, H), C ** -0.5, 0.125),
        "gain_head": jnp.clip(1.0 + 0.15 * jax.random.normal(streams_of[13], (H,), jnp.float32), 0.25, 1.75),
        "shift_head": jnp.clip(jax.random.uniform(streams_of[14], (H,), jnp.float32, -0.5, 0.5), -0.5, 0.5),
        "w_embed": gaussian(streams_of[15], (H, E), H ** -0.5, 0.125),
    }


logit_divisor_tau = 0.1
epsilon = 1e-05

@jax.custom_vjp
def low(v):
    return lax.optimization_barrier(v.astype(jnp.bfloat16)).astype(jnp.float32)

@jax.custom_vjp
def low_back(v):
    return v

def low_keep(v):
    return (low(v), None)

def low_pass(kept, grad):
    return (grad,)

def back_keep(v):
    return (v, None)

def back_low(kept, grad):
    return (low(grad),)
low.defvjp(low_keep, low_pass)
low_back.defvjp(back_keep, back_low)

def exact_matmul_result(left, right):
    return jnp.dot(left, right, precision=lax.Precision.HIGHEST, preferred_element_type=jnp.float32)

def batch_norm(tensor, gain_vec, shift_vec):
    means = lax.optimization_barrier(jnp.mean(tensor, axis=0))
    variance = lax.optimization_barrier(jnp.mean(tensor * tensor, axis=0)) - means * means
    return (tensor - means) * lax.rsqrt(variance + epsilon) * gain_vec + shift_vec

def spread_taps(hidden, map_side):
    padded = jnp.pad(hidden, ((0, 0), (1, 1), (1, 1), (0, 0)))
    pieces = [padded[:, tap_row:tap_row + map_side, tap_col:tap_col + map_side, :] for tap_row in range(3) for tap_col in range(3)]
    return jnp.concatenate(pieces, axis=-1).reshape(-1, 9 * hidden.shape[-1])

def micro_loss(view_pix, crop_pix, ids_row, weights):
    w_reduce, gain_one, shift_one, w_spatial, gain_two, shift_two, w_expand, gain_three, shift_three, w_hidden, gain_head, shift_head, w_embed = weights
    pixels = jnp.concatenate([view_pix, crop_pix], axis=0)
    view_rows = view_pix.shape[0]
    act_one = low_back(exact_matmul_result(pixels, w_reduce))
    hid_one = low(jax.nn.silu(batch_norm(act_one, gain_one, shift_one)))
    tap_cols = jnp.concatenate([spread_taps(hid_one[:view_rows].reshape(-1, VSIDE, VSIDE, M), VSIDE), spread_taps(hid_one[view_rows:].reshape(-1, CSIDE, CSIDE, M), CSIDE)], axis=0)
    act_two = low_back(exact_matmul_result(tap_cols, w_spatial))
    hid_two = low(jax.nn.silu(batch_norm(act_two, gain_two, shift_two)))
    act_three = low_back(exact_matmul_result(hid_two, w_expand))
    block_out = jax.nn.silu(batch_norm(act_three, gain_three, shift_three) + pixels)
    pooled_views = lax.optimization_barrier(jnp.mean(block_out[:view_rows].reshape(IMAGES, VIEWS, VSIDE * VSIDE, C), axis=2))
    pooled_crops = lax.optimization_barrier(jnp.mean(block_out[view_rows:].reshape(IMAGES, CROPS, CSIDE * CSIDE, C), axis=2))
    pooled = low(jnp.concatenate([pooled_views, pooled_crops], axis=1).reshape(EMB, C))
    head_act = low_back(exact_matmul_result(pooled, w_hidden))
    head_hid = low(jax.nn.silu(batch_norm(head_act, gain_head, shift_head)))
    embedding = low_back(exact_matmul_result(head_hid, w_embed))
    unit_length_features = low(embedding * lax.rsqrt(lax.optimization_barrier(jnp.sum(embedding * embedding, axis=1, keepdims=True)) + 1e-06))
    cosine_logit_matrix = low_back(exact_matmul_result(unit_length_features, unit_length_features.T) / logit_divisor_tau)
    ids_emb = jnp.repeat(ids_row, VIEWS + CROPS)
    emb_order = jnp.arange(EMB, dtype=jnp.int32)
    self_mask = emb_order[:, None] == emb_order[None, :]
    positive = (ids_emb[:, None] == ids_emb[None, :]) & jnp.logical_not(self_mask)
    counts = lax.optimization_barrier(jnp.sum(positive.astype(jnp.float32), axis=1))
    diagonal_excluded = jnp.where(self_mask, -1e+30, cosine_logit_matrix)
    log_total = jax.nn.logsumexp(diagonal_excluded, axis=1)
    pos_sum = lax.optimization_barrier(jnp.sum(jnp.where(positive, cosine_logit_matrix, 0.0), axis=1))
    per_anchor = log_total - pos_sum / counts
    return (jnp.sum(per_anchor), per_anchor)

def reference(view_maps, crop_maps, image_ids, w_reduce, gain_one, shift_one, w_spatial, gain_two, shift_two, w_expand, gain_three, shift_three, w_hidden, gain_head, shift_head, w_embed):

    def overall_objective(view_float, crop_float, weights):
        accum = jnp.zeros((), jnp.float32)
        anchor_terms = []
        for micro_index in range(MICRO):
            total, per_anchor = micro_loss(view_float[micro_index], crop_float[micro_index], image_ids[micro_index], weights)
            accum = accum + total
            anchor_terms.append(per_anchor)
        return (accum / (MICRO * EMB), jnp.stack(anchor_terms, axis=0))
    weights = (w_reduce.astype(jnp.float32), gain_one, shift_one, w_spatial.astype(jnp.float32), gain_two, shift_two, w_expand.astype(jnp.float32), gain_three, shift_three, w_hidden.astype(jnp.float32), gain_head, shift_head, w_embed.astype(jnp.float32))
    loss, backward, anchor_loss = jax.vjp(overall_objective, view_maps.astype(jnp.float32), crop_maps.astype(jnp.float32), weights, has_aux=True)
    grad_views, grad_crops, grads = backward(jnp.ones_like(loss))
    return (anchor_loss, grad_views, grad_crops, grads[0], grads[1], grads[2], grads[3], grads[4], grads[5], grads[6], grads[7], grads[8], grads[9], grads[10], grads[11], grads[12])
```

```python
import functools
import math

import jax
import jax.numpy as jnp
import numpy as np
from jax import lax
from jax.experimental import pallas as pl
from jax.experimental.pallas import tpu as pltpu
from jax.sharding import PartitionSpec as P

VIEWS = 2
CROPS = 4
VSIDE = 7
CSIDE = 3
TAU_INV = 10.0
EPS = 1e-05
LEN_EPS = 1e-06
BOTH = ("dp", "narrow")
F32 = jnp.float32
BF16 = jnp.bfloat16
MIB = 1 << 20


def round_up(value, step):
    return -(-value // step) * step


def xor_permute(array, offset, count):
    return lax.ppermute(array, BOTH, [(i, i ^ offset) for i in range(count)])


def bit_stages(first, last):
    bits = [1 << b for b in range(first, last)]
    stages = [bits[:1]] if bits else []
    rest = bits[1:]
    while rest:
        stages.append(rest[:2])
        rest = rest[2:]
    return stages


def all_sum(array, count):
    for stage in bit_stages(0, count.bit_length() - 1):
        if len(stage) == 1:
            array = array + xor_permute(array, stage[0], count)
        else:
            low, high = stage
            near = xor_permute(array, low, count)
            far = xor_permute(array, high, count)
            across = xor_permute(array, low ^ high, count)
            array = (array + near) + (far + across)
    return array


def gather_all(array, count):
    parts = [array]
    stages = bit_stages(0, count.bit_length() - 1)
    for stage in stages[:0:-1] + stages[:1]:
        offsets = stage if len(stage) == 1 else [stage[0], stage[1], stage[0] ^ stage[1]]
        block = jnp.stack(parts) if len(parts) > 1 else parts[0][None]
        arrived = [xor_permute(block, off, count) for off in offsets]
        parts = [p for p in parts]
        for got in arrived:
            parts.extend(got[k] for k in range(got.shape[0]))
    return jnp.stack(parts)


def gather_order(count):
    order = [0]
    stages = bit_stages(0, count.bit_length() - 1)
    for stage in stages[:0:-1] + stages[:1]:
        offsets = stage if len(stage) == 1 else [stage[0], stage[1], stage[0] ^ stage[1]]
        order = order + [o ^ off for off in offsets for o in order]
    return np.array(order, np.int32)


def dot(left, right):
    return jnp.dot(left, right, preferred_element_type=F32)


def dot_nt(left, right):
    return lax.dot_general(left, right, (((1,), (1,)), ((), ())), preferred_element_type=F32)


def sigmoid(values):
    return 0.5 * jnp.tanh(0.5 * values) + 0.5


def silu_slope(values):
    sigma = sigmoid(values)
    return sigma * (1.0 + values * (1.0 - sigma))


def norm_terms(totals, rows):
    means = totals[0:1] / rows
    variance = totals[1:2] / rows - means * means
    return means, lax.rsqrt(variance + EPS)


def halves(values):
    high = values.astype(BF16)
    return high, (values - high.astype(F32)).astype(BF16)


def col_sums(first, second):
    return jnp.sum(first, axis=0, keepdims=True), jnp.sum(second, axis=0, keepdims=True)


class Sizes:
    def __init__(self, view_rows, crop_rows):
        self.views, self.crops = view_rows, crop_rows
        self.crop_at = round_up(view_rows, 16)
        self.rows = self.crop_at + round_up(crop_rows, 16)

    def zero_pads(self, ref, lead, cols):
        zero = jnp.zeros((self.crop_at - self.views, cols), ref.dtype)
        ref[lead, self.views : self.crop_at, :] = zero
        tail = self.rows - self.crop_at - self.crops
        ref[lead, self.crop_at + self.crops :, :] = jnp.zeros((tail, cols), ref.dtype)

    def row_mask(self):
        row = lax.broadcasted_iota(jnp.int32, (self.rows, 128), 0)
        inside = (row < self.views) | ((row >= self.crop_at) & (row < self.crop_at + self.crops))
        return inside


def wide(mask, cols):
    return jnp.concatenate([mask] * (cols // 128), axis=1)


def fill_edges(edges_ref, sizes):
    for start, stop, at, side in (
        (0, sizes.crop_at, sizes.views, VSIDE),
        (sizes.crop_at, sizes.rows, sizes.crop_at + sizes.crops, CSIDE),
    ):
        count = stop - start
        row = lax.broadcasted_iota(jnp.int32, (count, 128), 0)
        real = row < (at - start)
        rowf = row.astype(F32) + 0.5
        line = jnp.floor(rowf * (1.0 / side))
        col = rowf - 0.5 - line * side
        in_map = line - jnp.floor((line + 0.5) * (1.0 / side)) * side
        keep = (col > 0.5, col < side - 1.5, in_map > 0.5, in_map < side - 1.5)
        for k in range(4):
            edges_ref[k, start:stop, :] = jnp.where(real & keep[k], 1.0, 0.0)
        edges_ref[4, start:stop, :] = jnp.where(real, 1.0, 0.0)


PAD = 16


def tap_block(source_ref, edges_ref, sizes, tap, width):
    dy, dx = tap // 3 - 1, tap % 3 - 1
    pieces = []
    for start, stop, side in ((0, sizes.crop_at, VSIDE), (sizes.crop_at, sizes.rows, CSIDE)):
        shift = dy * side + dx
        values = source_ref[PAD + start + shift : PAD + stop + shift, :]
        mask = None
        for cond, plane in ((dx < 0, 0), (dx > 0, 1), (dy < 0, 2), (dy > 0, 3)):
            if cond:
                edge = edges_ref[plane, start:stop, :]
                mask = edge if mask is None else mask * edge
        if mask is None:
            mask = edges_ref[4, start:stop, :]
        pieces.append((values * wide(mask, width)).astype(BF16))
    return jnp.concatenate(pieces, axis=0)


def k_reduce(xv, xc, w, act, stats, *, sizes):
    views = dot(xv[0], w[...])
    crops = dot(xc[0], w[...])
    act[0, : sizes.views, :] = views
    act[0, sizes.crop_at : sizes.crop_at + sizes.crops, :] = crops
    sizes.zero_pads(act, 0, act.shape[2])
    a, b = col_sums(views, views * views)
    c, d = col_sums(crops, crops * crops)
    stats[0, 0:1, :] = a + c
    stats[0, 1:2, :] = b + d


def k_spatial(act, totals, gain, shift, w, hid, act_two, stats, source, edges, *, sizes, rows):
    width = act.shape[2]

    @pl.when(pl.program_id(0) == 0)
    def _():
        fill_edges(edges, sizes)
        source[:PAD, :] = jnp.zeros((PAD, width), F32)
        source[PAD + sizes.rows :, :] = jnp.zeros((PAD, width), F32)

    means, inv = norm_terms(totals[0], rows)
    pre = (act[0] - means) * (inv * gain[...]) + shift[...]
    hidden = (pre * sigmoid(pre)).astype(BF16)
    hid[0] = hidden
    source[PAD : PAD + sizes.rows, :] = hidden.astype(F32)
    for tap in range(9):
        cols = tap_block(source, edges, sizes, tap, width)
        part = dot(cols, w[tap * width : (tap + 1) * width, :])
        if tap == 0:
            act_two[0] = part
        else:
            act_two[0] += part
    out = act_two[0]
    a, b = col_sums(out, out * out)
    stats[0, 0:1, :] = a
    stats[0, 1:2, :] = b


def k_expand(act, totals, gain, shift, w, hid, act_three, stats, *, sizes, rows):
    @pl.when(pl.program_id(1) == 0)
    def _():
        means, inv = norm_terms(totals[0], rows)
        pre = (act[0] - means) * (inv * gain[...]) + shift[...]
        keep = wide(sizes.row_mask(), act.shape[2])
        hid[0] = jnp.where(keep, pre * sigmoid(pre), 0.0).astype(BF16)

    out = dot(hid[0], w[...])
    act_three[0] = out
    a, b = col_sums(out, out * out)
    stats[0, 0:1, :] = a
    stats[0, 1:2, :] = b


def k_pool(act, totals, gain, shift, xv, xc, pool_v, pool_c, inv_count, w, pooled, head, stats, *, sizes, rows, steps):
    step, micro = pl.program_id(0), pl.program_id(1)
    means, inv = norm_terms(totals[0], rows)
    scale = inv * gain[...]

    def block_sum(start, count, x, pool):
        resid = (act[0, start : start + count, :] - means) * scale + shift[...] + x[0].astype(F32)
        high, low = halves(resid * sigmoid(resid))
        return dot(pool[...], high) + dot(pool[...], low)

    total = block_sum(0, sizes.views, xv, pool_v) + block_sum(sizes.crop_at, sizes.crops, xc, pool_c)
    low_pooled = (total * inv_count[...]).astype(BF16)
    pooled[0] = low_pooled
    part = dot(low_pooled, w[...])

    @pl.when(step == 0)
    def _():
        head[micro] = part

    @pl.when(step > 0)
    def _():
        head[micro] += part

    @pl.when(step == steps - 1)
    def _():
        out = head[micro]
        a, b = col_sums(out, out * out)
        stats[micro, 0:1, :] = a
        stats[micro, 1:2, :] = b


def head_forward(head, totals, gain, shift, w_embed, count):
    means, inv = norm_terms(totals, count)
    normed = (head - means) * inv
    pre = normed * gain + shift
    hidden = (pre * sigmoid(pre)).astype(BF16)
    embedding = dot(hidden, w_embed)
    inv_len = lax.rsqrt(jnp.sum(embedding * embedding, axis=1, keepdims=True) + LEN_EPS)
    return normed, pre, inv, hidden, embedding * inv_len, inv_len


def k_embed(head, totals, gain, shift, w_embed, hidden, unit_low, *, count):
    _, _, _, hid, unit, _ = head_forward(head[0], totals[0], gain[...], shift[...], w_embed[...], count)
    hidden[0] = hid
    unit_low[0] = unit.astype(BF16)


def k_loss(
    units, ids_all, ids_own, pos_all, pos_own, head, totals, gain, shift, w_embed,
    loss, slopes, grad_embed, stats, *, count, loss_scale, block,
):
    everyone = units[0]
    n_all = everyone.shape[0]
    n_own = head.shape[1]

    def add_rows(k, sums):
        start = k * block
        rows = units[0, pl.ds(pl.multiple_of(start, block), block), :]
        scores = dot_nt(rows, everyone) * TAU_INV
        mine = lax.broadcasted_iota(jnp.int32, (block, n_all), 0) + start
        other = lax.broadcasted_iota(jnp.int32, (block, n_all), 1)
        terms = jnp.where(mine == other, 0.0, jnp.exp(scores - TAU_INV))
        return sums + jnp.sum(terms, axis=0, keepdims=True)

    sums = lax.fori_loop(0, n_all // block, add_rows, jnp.zeros((1, n_all), F32))
    log_all = jnp.log(sums) + TAU_INV
    normed, pre, inv, hid, unit, inv_len = head_forward(
        head[0], totals[0], gain[...], shift[...], w_embed[...], count
    )
    low = unit.astype(BF16)
    scores = dot_nt(low, everyone) * TAU_INV
    itself = lax.broadcasted_iota(jnp.int32, (n_own, n_all), 0) == lax.broadcasted_iota(
        jnp.int32, (n_own, n_all), 1
    )
    own_sum = jnp.sum(jnp.where(itself, 0.0, jnp.exp(scores - TAU_INV)), axis=1, keepdims=True)
    log_own = jnp.log(own_sum) + TAU_INV
    positive = (ids_own[0] == ids_all[0]) & jnp.logical_not(itself)
    pos_sum = jnp.sum(jnp.where(positive, scores, 0.0), axis=1, keepdims=True)
    loss[0] = log_own - pos_sum * pos_own[0]
    by_row = jnp.where(itself, 0.0, jnp.exp(scores - log_own)) - jnp.where(positive, pos_own[0], 0.0)
    by_col = jnp.where(itself, 0.0, jnp.exp(scores - log_all)) - jnp.where(positive, pos_all[0], 0.0)
    grad_unit = (
        dot((by_row * loss_scale).astype(BF16), everyone)
        + dot((by_col * loss_scale).astype(BF16), everyone)
    ) * TAU_INV
    grad = inv_len * (grad_unit - unit * jnp.sum(unit * grad_unit, axis=1, keepdims=True))
    grad_low = grad.astype(BF16)
    grad_embed[0] = grad_low
    slope = dot_nt(grad_low, w_embed[...]) * silu_slope(pre)
    slopes[0] = slope
    a, b = col_sums(slope, slope * normed)
    stats[0, 0:1, :] = a
    stats[0, 1:2, :] = b


def norm_back(slopes, normed, sums, gain, inv, rows):
    return (gain * inv) * (slopes - sums[0:1] / rows - normed * (sums[1:2] / rows))


def k_back_pool(
    slopes, head, tot_head, sum_head, gain_head, act, totals, gain, shift, xv, xc,
    spread_v, spread_c, inv_count, w, grad_head, grad_resid, stats, held, *, sizes, rows, count,
):
    micro = pl.program_id(1)

    @pl.when(pl.program_id(0) == 0)
    def _():
        means, inv = norm_terms(tot_head[micro], count)
        normed = (head[micro] - means) * inv
        out = norm_back(slopes[micro], normed, sum_head[micro], gain_head[...], inv, count)
        held[micro] = out.astype(BF16)
        grad_head[micro] = out.astype(BF16)

    high, low = halves(dot_nt(held[micro], w[...]) * inv_count[...])
    means, inv = norm_terms(totals[0], rows)
    tot = []
    for start, n, x, spread in (
        (0, sizes.views, xv, spread_v),
        (sizes.crop_at, sizes.crops, xc, spread_c),
    ):
        normed = (act[0, start : start + n, :] - means) * inv
        resid = normed * gain[...] + shift[...] + x[0].astype(F32)
        back = dot(spread[...], high) + dot(spread[...], low)
        slope = back * silu_slope(resid)
        grad_resid[0, start : start + n, :] = slope
        tot.append(col_sums(slope, slope * normed))
    sizes.zero_pads(grad_resid, 0, grad_resid.shape[2])
    stats[0, 0:1, :] = tot[0][0] + tot[1][0]
    stats[0, 1:2, :] = tot[0][1] + tot[1][1]


def k_back_expand(
    grad_resid, act_three, tot_three, sum_three, gain_three, w, act_two, tot_two, gain_two, shift_two,
    grad_three, slopes, stats, acc, *, sizes, rows, steps,
):
    step = pl.program_id(1)
    means, inv = norm_terms(tot_three[0], rows)
    normed = (act_three[0] - means) * inv
    grad = norm_back(grad_resid[0], normed, sum_three[0], gain_three[...], inv, rows)
    low = jnp.where(wide(sizes.row_mask(), grad.shape[1]), grad, 0.0).astype(BF16)
    grad_three[0] = low
    part = dot_nt(low, w[...])

    @pl.when(step == 0)
    def _():
        acc[...] = part

    @pl.when(step > 0)
    def _():
        acc[...] += part

    @pl.when(step == steps - 1)
    def _():
        means, inv = norm_terms(tot_two[0], rows)
        normed = (act_two[0] - means) * inv
        slope = acc[...] * silu_slope(normed * gain_two[...] + shift_two[...])
        slopes[0] = slope
        a, b = col_sums(slope, slope * normed)
        stats[0, 0:1, :] = a
        stats[0, 1:2, :] = b


def k_back_spatial(
    slopes, act_two, tot_two, sum_two, gain_two, w, act_one, tot_one, gain_one, shift_one,
    grad_cols, slopes_one, stats, source, edges, *, sizes, rows,
):
    width = act_two.shape[2]

    @pl.when(pl.program_id(0) == 0)
    def _():
        fill_edges(edges, sizes)
        source[:PAD, :] = jnp.zeros((PAD, width), F32)
        source[PAD + sizes.rows :, :] = jnp.zeros((PAD, width), F32)

    means, inv = norm_terms(tot_two[0], rows)
    normed = (act_two[0] - means) * inv
    source[PAD : PAD + sizes.rows, :] = norm_back(slopes[0], normed, sum_two[0], gain_two[...], inv, rows)
    for tap in range(9):
        cols = tap_block(source, edges, sizes, tap, width)
        other = 8 - tap
        grad_cols[0, :, other * width : (other + 1) * width] = cols
        part = dot_nt(cols, w[other * width : (other + 1) * width, :])
        if tap == 0:
            slopes_one[0] = part
        else:
            slopes_one[0] += part
    means, inv = norm_terms(tot_one[0], rows)
    normed = (act_one[0] - means) * inv
    slope = slopes_one[0] * silu_slope(normed * gain_one[...] + shift_one[...])
    slopes_one[0] = slope
    a, b = col_sums(slope, slope * normed)
    stats[0, 0:1, :] = a
    stats[0, 1:2, :] = b


def k_back_reduce(
    slopes, act_one, tot_one, sum_one, gain_one, w, grad_resid, grad_one, grad_v, grad_c, *, sizes, rows
):
    @pl.when(pl.program_id(1) == 0)
    def _():
        means, inv = norm_terms(tot_one[0], rows)
        normed = (act_one[0] - means) * inv
        grad = norm_back(slopes[0], normed, sum_one[0], gain_one[...], inv, rows)
        grad_one[0] = jnp.where(wide(sizes.row_mask(), grad.shape[1]), grad, 0.0).astype(BF16)

    back = dot_nt(grad_one[0], w[...])
    grad_v[0] = grad_resid[0, : sizes.views, :] + back[: sizes.views]
    at = sizes.crop_at
    grad_c[0] = grad_resid[0, at : at + sizes.crops, :] + back[at : at + sizes.crops]


def call(kernel, name, grid, ins, outs, scratch=(), flops=0, vmem=56):
    spec = lambda block, index: pl.BlockSpec(block, index)
    moved = sum(a.size * a.dtype.itemsize for a, _, _ in ins) + sum(
        math.prod(s) * jnp.dtype(t).itemsize for s, t, _, _ in outs
    )
    return pl.pallas_call(
        kernel,
        grid=grid,
        in_specs=[spec(b, i) for _, b, i in ins],
        out_specs=[spec(b, i) for _, _, b, i in outs],
        out_shape=[jax.ShapeDtypeStruct(s, t) for s, t, _, _ in outs],
        scratch_shapes=list(scratch),
        compiler_params=pltpu.CompilerParams(vmem_limit_bytes=vmem * MIB),
        cost_estimate=pl.CostEstimate(flops=int(flops), bytes_accessed=int(moved), transcendentals=0),
        name=name,
    )(*[a for a, _, _ in ins])


def exact(array):
    return lax.optimization_barrier(array)


def add_low(*parts):
    total = parts[0].astype(F32)
    for part in parts[1:]:
        total = total + part.astype(F32)
    return total.astype(BF16)


def reduce_weight(grad, count, data_size, narrow_size):
    rows, cols = grad.shape
    me = lax.axis_index("dp")
    core = lax.axis_index("narrow") % 2
    blocks = grad.reshape(data_size, rows // data_size, cols)
    blocks = jnp.stack(
        [lax.dynamic_index_in_dim(blocks, me ^ j, axis=0, keepdims=False) for j in range(data_size)]
    )
    half = cols // 2
    low, high = blocks[:, :, :half], blocks[:, :, half:]
    keep = jnp.where(core == 0, low, high)
    send = jnp.where(core == 0, high, low)
    part = add_low(keep, xor_permute(send, 1, count))
    size = data_size
    for stage in bit_stages(0, data_size.bit_length() - 1):
        if len(stage) == 1:
            split = part.reshape((size // 2, 2) + part.shape[1:])
            part = add_low(split[:, 0], xor_permute(split[:, 1], stage[0] * narrow_size, count))
            size //= 2
        else:
            split = part.reshape((size // 4, 4) + part.shape[1:])
            got = [
                xor_permute(split[:, k], off * narrow_size, count)
                for k, off in ((1, stage[0]), (2, stage[1]), (3, stage[0] ^ stage[1]))
            ]
            part = add_low(split[:, 0], *got)
            size //= 4
    part = exact(part[0])
    off = 2
    while off < narrow_size:
        part = exact(add_low(part, xor_permute(part, off, count)))
        off *= 2
    other = xor_permute(part, 1, count)
    both = jnp.where(
        core == 0, jnp.concatenate([part, other], axis=1), jnp.concatenate([other, part], axis=1)
    )
    return both.astype(F32)


def body(
    view_maps, crop_maps, image_ids, w_reduce, gain_one, shift_one, w_spatial, gain_two, shift_two,
    w_expand, gain_three, shift_three, w_hidden, gain_head, shift_head, w_embed,
):
    micros, view_rows, channels = view_maps.shape
    crop_rows = crop_maps.shape[1]
    mid = w_reduce.shape[1]
    hidden_width = w_hidden.shape[1]
    emb_width = w_embed.shape[1]
    images_dev = view_rows // (VIEWS * VSIDE * VSIDE)
    each = VIEWS + CROPS
    own = images_dev * each
    data_size, narrow_size = lax.axis_size("dp"), lax.axis_size("narrow")
    count = data_size * narrow_size
    emb_total = own * count
    pixel_count = (view_rows + crop_rows) * count
    loss_scale = 1.0 / (micros * emb_total)
    device = lax.axis_index("dp") * narrow_size + lax.axis_index("narrow")
    sizes = Sizes(view_rows, crop_rows)
    rows = sizes.rows

    pool_v = np.zeros((own, view_rows), np.float32)
    pool_c = np.zeros((own, crop_rows), np.float32)
    area_v, area_c = VSIDE * VSIDE, CSIDE * CSIDE
    for r in range(view_rows):
        image, view = divmod(r // area_v, VIEWS)
        pool_v[image * each + view, r] = 1
    for r in range(crop_rows):
        image, crop = divmod(r // area_c, CROPS)
        pool_c[image * each + VIEWS + crop, r] = 1
    inv_count = np.where(np.arange(own) % each < VIEWS, 1.0 / area_v, 1.0 / area_c)
    inv_count = jnp.asarray(inv_count[:, None], F32)
    spread_v, spread_c = jnp.asarray(pool_v.T, BF16), jnp.asarray(pool_c.T, BF16)
    pool_v, pool_c = jnp.asarray(pool_v, BF16), jnp.asarray(pool_c, BF16)

    place = jnp.asarray(gather_order(count)) ^ device
    same = jnp.sum((image_ids[:, :, None] == image_ids[:, None, :]).astype(F32), axis=2)
    inv_pos = 1.0 / (same * each - 1.0)

    from_device = place[:, None] == jnp.arange(count, dtype=jnp.int32)[None, :]

    def by_place(values):
        blocks = values.reshape(micros, 1, count, images_dev)
        moved = jnp.sum(jnp.where(from_device[None, :, :, None], blocks, 0), axis=2)
        return jnp.repeat(moved.reshape(micros, -1), each, axis=1)

    ids_all, pos_all = by_place(image_ids), by_place(inv_pos)
    ids_own, pos_own = ids_all[:, :own, None], pos_all[:, :own, None]
    ids_all, pos_all = ids_all[:, None, :], pos_all[:, None, :]

    row = lambda v: v.reshape(1, -1)
    g1, b1, g2, b2 = row(gain_one), row(shift_one), row(gain_two), row(shift_two)
    g3, b3, gh, bh = row(gain_three), row(shift_three), row(gain_head), row(shift_head)
    reduce_all = lambda stats: all_sum(stats, count)
    flops = 2.0 * micros * rows * channels * mid

    m0 = lambda m: (m, 0, 0)
    fix2 = lambda *_: (0, 0)
    fix3 = lambda *_: (0, 0, 0)
    act_one, st = call(
        functools.partial(k_reduce, sizes=sizes), "reduce", (micros,),
        [
            (view_maps, (1, view_rows, channels), m0),
            (crop_maps, (1, crop_rows, channels), m0),
            (w_reduce, (channels, mid), fix2),
        ],
        [
            ((micros, rows, mid), F32, (1, rows, mid), m0),
            ((micros, 2, mid), F32, (1, 2, mid), m0),
        ],
        flops=flops,
    )
    tot_one = reduce_all(st)
    hid_one, act_two, st = call(
        functools.partial(k_spatial, sizes=sizes, rows=pixel_count), "spatial", (micros,),
        [
            (act_one, (1, rows, mid), m0),
            (tot_one, (1, 2, mid), m0),
            (g1, (1, mid), fix2),
            (b1, (1, mid), fix2),
            (w_spatial, (9 * mid, mid), fix2),
        ],
        [
            ((micros, rows, mid), BF16, (1, rows, mid), m0),
            ((micros, rows, mid), F32, (1, rows, mid), m0),
            ((micros, 2, mid), F32, (1, 2, mid), m0),
        ],
        scratch=[pltpu.VMEM((rows + 2 * PAD, mid), F32), pltpu.VMEM((5, rows, 128), F32)],
        flops=flops * 9 * mid / channels,
    )
    tot_two = reduce_all(st)
    mn0 = lambda m, n: (m, 0, 0)
    mn = lambda m, n: (m, 0, n)
    blk = 512
    steps = channels // blk
    hid_two, act_three, st = call(
        functools.partial(k_expand, sizes=sizes, rows=pixel_count), "expand", (micros, steps),
        [
            (act_two, (1, rows, mid), mn0),
            (tot_two, (1, 2, mid), mn0),
            (g2, (1, mid), fix2),
            (b2, (1, mid), fix2),
            (w_expand, (mid, blk), lambda m, n: (0, n)),
        ],
        [
            ((micros, rows, mid), BF16, (1, rows, mid), mn0),
            ((micros, rows, channels), F32, (1, rows, blk), mn),
            ((micros, 2, channels), F32, (1, 2, blk), mn),
        ],
        flops=flops,
    )
    tot_three = reduce_all(st)
    cblk = 256
    csteps = channels // cblk
    nm = lambda n, m: (m, 0, n)
    vec = lambda n, m: (0, n)
    wrow = lambda n, m: (n, 0)
    pooled, head, st = call(
        functools.partial(k_pool, sizes=sizes, rows=pixel_count, steps=csteps), "pool", (csteps, micros),
        [
            (act_three, (1, rows, cblk), nm),
            (tot_three, (1, 2, cblk), nm),
            (g3, (1, cblk), vec),
            (b3, (1, cblk), vec),
            (view_maps, (1, view_rows, cblk), nm),
            (crop_maps, (1, crop_rows, cblk), nm),
            (pool_v, (own, view_rows), fix2),
            (pool_c, (own, crop_rows), fix2),
            (inv_count, (own, 1), fix2),
            (w_hidden, (cblk, hidden_width), wrow),
        ],
        [
            ((micros, own, channels), BF16, (1, own, cblk), nm),
            ((micros, own, hidden_width), F32, (micros, own, hidden_width), fix3),
            ((micros, 2, hidden_width), F32, (micros, 2, hidden_width), fix3),
        ],
        flops=flops / 10,
    )
    tot_head = reduce_all(st)
    head_in = [
        (head, (1, own, hidden_width), m0),
        (tot_head, (1, 2, hidden_width), m0),
        (gh, (1, hidden_width), fix2),
        (bh, (1, hidden_width), fix2),
        (w_embed, (hidden_width, emb_width), fix2),
    ]
    head_hid, unit_low = call(
        functools.partial(k_embed, count=emb_total), "embed", (micros,), head_in,
        [
            ((micros, own, hidden_width), BF16, (1, own, hidden_width), m0),
            ((micros, own, emb_width), BF16, (1, own, emb_width), m0),
        ],
    )
    units = gather_all(unit_low, count)
    units = jnp.transpose(units, (1, 0, 2, 3)).reshape(micros, emb_total, emb_width)
    loss, slopes, grad_embed, st = call(
        functools.partial(k_loss, count=emb_total, loss_scale=loss_scale, block=128), "loss", (micros,),
        [
            (units, (1, emb_total, emb_width), m0),
            (ids_all, (1, 1, emb_total), m0),
            (ids_own, (1, own, 1), m0),
            (pos_all, (1, 1, emb_total), m0),
            (pos_own, (1, own, 1), m0),
        ]
        + head_in,
        [
            ((micros, own, 1), F32, (1, own, 1), m0),
            ((micros, own, hidden_width), F32, (1, own, hidden_width), m0),
            ((micros, own, emb_width), BF16, (1, own, emb_width), m0),
            ((micros, 2, hidden_width), F32, (1, 2, hidden_width), m0),
        ],
    )
    sum_head = reduce_all(st)

    grad_head, grad_resid, st = call(
        functools.partial(k_back_pool, sizes=sizes, rows=pixel_count, count=emb_total), "back_pool",
        (csteps, micros),
        [
            (slopes, (micros, own, hidden_width), fix3),
            (head, (micros, own, hidden_width), fix3),
            (tot_head, (micros, 2, hidden_width), fix3),
            (sum_head, (micros, 2, hidden_width), fix3),
            (gh, (1, hidden_width), fix2),
            (act_three, (1, rows, cblk), nm),
            (tot_three, (1, 2, cblk), nm),
            (g3, (1, cblk), vec),
            (b3, (1, cblk), vec),
            (view_maps, (1, view_rows, cblk), nm),
            (crop_maps, (1, crop_rows, cblk), nm),
            (spread_v, (view_rows, own), fix2),
            (spread_c, (crop_rows, own), fix2),
            (inv_count, (own, 1), fix2),
            (w_hidden, (cblk, hidden_width), wrow),
        ],
        [
            ((micros, own, hidden_width), BF16, (micros, own, hidden_width), fix3),
            ((micros, rows, channels), F32, (1, rows, cblk), nm),
            ((micros, 2, channels), F32, (1, 2, cblk), nm),
        ],
        scratch=[pltpu.VMEM((micros, own, hidden_width), BF16)],
        flops=flops / 10,
    )
    sum_three = reduce_all(st)
    grad_three, slopes_two, st = call(
        functools.partial(k_back_expand, sizes=sizes, rows=pixel_count, steps=steps), "back_expand",
        (micros, steps),
        [
            (grad_resid, (1, rows, blk), mn),
            (act_three, (1, rows, blk), mn),
            (tot_three, (1, 2, blk), mn),
            (sum_three, (1, 2, blk), mn),
            (g3, (1, blk), lambda m, n: (0, n)),
            (w_expand, (mid, blk), lambda m, n: (0, n)),
            (act_two, (1, rows, mid), mn0),
            (tot_two, (1, 2, mid), mn0),
            (g2, (1, mid), fix2),
            (b2, (1, mid), fix2),
        ],
        [
            ((micros, rows, channels), BF16, (1, rows, blk), mn),
            ((micros, rows, mid), F32, (1, rows, mid), mn0),
            ((micros, 2, mid), F32, (1, 2, mid), mn0),
        ],
        scratch=[pltpu.VMEM((rows, mid), F32)],
        flops=flops,
    )
    sum_two = reduce_all(st)
    grad_cols, slopes_one, st = call(
        functools.partial(k_back_spatial, sizes=sizes, rows=pixel_count), "back_spatial", (micros,),
        [
            (slopes_two, (1, rows, mid), m0),
            (act_two, (1, rows, mid), m0),
            (tot_two, (1, 2, mid), m0),
            (sum_two, (1, 2, mid), m0),
            (g2, (1, mid), fix2),
            (w_spatial, (9 * mid, mid), fix2),
            (act_one, (1, rows, mid), m0),
            (tot_one, (1, 2, mid), m0),
            (g1, (1, mid), fix2),
            (b1, (1, mid), fix2),
        ],
        [
            ((micros, rows, 9 * mid), BF16, (1, rows, 9 * mid), m0),
            ((micros, rows, mid), F32, (1, rows, mid), m0),
            ((micros, 2, mid), F32, (1, 2, mid), m0),
        ],
        scratch=[pltpu.VMEM((rows + 2 * PAD, mid), F32), pltpu.VMEM((5, rows, 128), F32)],
        flops=flops * 9 * mid / channels,
    )
    sum_one = reduce_all(st)
    grad_one, grad_views, grad_crops = call(
        functools.partial(k_back_reduce, sizes=sizes, rows=pixel_count), "back_reduce", (micros, steps),
        [
            (slopes_one, (1, rows, mid), mn0),
            (act_one, (1, rows, mid), mn0),
            (tot_one, (1, 2, mid), mn0),
            (sum_one, (1, 2, mid), mn0),
            (g1, (1, mid), fix2),
            (w_reduce, (blk, mid), lambda m, n: (n, 0)),
            (grad_resid, (1, rows, blk), mn),
        ],
        [
            ((micros, rows, mid), BF16, (1, rows, mid), mn0),
            (view_maps.shape, F32, (1, view_rows, blk), mn),
            (crop_maps.shape, F32, (1, crop_rows, blk), mn),
        ],
        flops=flops,
    )

    over = lambda a, b: jnp.einsum("mri,mrj->ij", a, b, preferred_element_type=F32)
    reduce_w = lambda g: reduce_weight(g.astype(BF16), count, data_size, narrow_size)
    gw_embed = reduce_w(over(head_hid, grad_embed))
    gw_hidden = reduce_w(over(pooled, grad_head))
    gw_expand = reduce_w(over(hid_two, grad_three))
    by_tap = jnp.einsum(
        "mri,mrtj->tij", hid_one, grad_cols.reshape(micros, rows, 9, mid), preferred_element_type=F32
    )
    gw_spatial = reduce_w(by_tap.reshape(9 * mid, mid))
    at = sizes.crop_at
    gw_reduce = reduce_w(
        over(view_maps, grad_one[:, :view_rows]) + over(crop_maps, grad_one[:, at : at + crop_rows])
    )
    gain_grad = lambda sums: jnp.sum(sums[:, 1], axis=0)
    shift_grad = lambda sums: jnp.sum(sums[:, 0], axis=0)
    return (
        loss.reshape(micros, own), grad_views, grad_crops,
        gw_reduce, gain_grad(sum_one), shift_grad(sum_one),
        gw_spatial, gain_grad(sum_two), shift_grad(sum_two),
        gw_expand, gain_grad(sum_three), shift_grad(sum_three),
        gw_hidden, gain_grad(sum_head), shift_grad(sum_head),
        gw_embed,
    )


def solution(mesh):
    rows = P(None, BOTH, None)
    return jax.shard_map(
        body,
        mesh=mesh,
        in_specs=(rows, rows) + (P(),) * 14,
        out_specs=(
            P(None, BOTH), rows, rows,
            P("dp", None), P(), P(),
            P("dp", None), P(), P(),
            P("dp", None), P(), P(),
            P("dp", None), P(), P(),
            P("dp", None),
        ),
        check_vma=False,
    )
```

```python
import functools
import math

import jax
import jax.numpy as jnp
import numpy as np
from jax import lax
from jax.experimental import pallas as pl
from jax.experimental.pallas import tpu as pltpu
from jax.sharding import PartitionSpec as P

VIEWS = 2
CROPS = 4
VSIDE = 7
CSIDE = 3
TAU_INV = 10.0
EPS = 1e-05
LEN_EPS = 1e-06
BOTH = ("dp", "narrow")
F32 = jnp.float32
BF16 = jnp.bfloat16
MIB = 1 << 20


def round_up(value, step):
    return -(-value // step) * step


def xor_permute(array, offset, count):
    return lax.ppermute(array, BOTH, [(i, i ^ offset) for i in range(count)])


def bit_stages(first, last):
    bits = [1 << b for b in range(first, last)]
    stages = [bits[:1]] if bits else []
    rest = bits[1:]
    while rest:
        stages.append(rest[:2])
        rest = rest[2:]
    return stages


def all_sum(array, count, begun=None):
    for stage in bit_stages(0, count.bit_length() - 1):
        if len(stage) == 1:
            array = array + xor_permute(array, stage[0], count)
            if begun is not None:
                begun(array)
                begun = None
        else:
            low, high = stage
            near = xor_permute(array, low, count)
            far = xor_permute(array, high, count)
            across = xor_permute(array, low ^ high, count)
            array = (array + near) + (far + across)
    return array


def gather_all(array, count):
    parts = [array]
    stages = bit_stages(0, count.bit_length() - 1)
    for stage in stages[:0:-1] + stages[:1]:
        offsets = stage if len(stage) == 1 else [stage[0], stage[1], stage[0] ^ stage[1]]
        block = jnp.stack(parts) if len(parts) > 1 else parts[0][None]
        arrived = [xor_permute(block, off, count) for off in offsets]
        parts = [p for p in parts]
        for got in arrived:
            parts.extend(got[k] for k in range(got.shape[0]))
    return jnp.stack(parts)


def gather_order(count):
    order = [0]
    stages = bit_stages(0, count.bit_length() - 1)
    for stage in stages[:0:-1] + stages[:1]:
        offsets = stage if len(stage) == 1 else [stage[0], stage[1], stage[0] ^ stage[1]]
        order = order + [o ^ off for off in offsets for o in order]
    return np.array(order, np.int32)


def dot(left, right):
    return jnp.dot(left, right, preferred_element_type=F32)


def dot_tn(left, right):
    return lax.dot_general(left, right, (((0,), (0,)), ((), ())), preferred_element_type=F32)


def dot_nt(left, right):
    return lax.dot_general(left, right, (((1,), (1,)), ((), ())), preferred_element_type=F32)


def norm_terms(totals, rows):
    means = totals[0:1] / rows
    variance = totals[1:2] / rows - means * means
    return means, lax.rsqrt(variance + EPS)


def halves(values):
    high = values.astype(BF16)
    return high, (values - high.astype(F32)).astype(BF16)


def col_sums(first, second):
    return jnp.sum(first, axis=0, keepdims=True), jnp.sum(second, axis=0, keepdims=True)


class Sizes:
    def __init__(self, view_rows, crop_rows):
        self.views, self.crops = view_rows, crop_rows
        self.crop_at = round_up(view_rows, 16)
        self.rows = self.crop_at + round_up(crop_rows, 16)

    def row_mask(self):
        row = lax.broadcasted_iota(jnp.int32, (self.rows, 128), 0)
        inside = (row < self.views) | ((row >= self.crop_at) & (row < self.crop_at + self.crops))
        return inside


def wide(mask, cols):
    return jnp.concatenate([mask] * (cols // 128), axis=1)


def fill_edges(edges_ref, sizes):
    for start, stop, at, side in (
        (0, sizes.crop_at, sizes.views, VSIDE),
        (sizes.crop_at, sizes.rows, sizes.crop_at + sizes.crops, CSIDE),
    ):
        count = stop - start
        row = lax.broadcasted_iota(jnp.int32, (count, 128), 0)
        real = row < (at - start)
        rowf = row.astype(F32) + 0.5
        line = jnp.floor(rowf * (1.0 / side))
        col = rowf - 0.5 - line * side
        in_map = line - jnp.floor((line + 0.5) * (1.0 / side)) * side
        keep = (col > 0.5, col < side - 1.5, in_map > 0.5, in_map < side - 1.5)
        for k in range(4):
            edges_ref[k, start:stop, :] = jnp.where(real & keep[k], 1.0, 0.0)
        edges_ref[4, start:stop, :] = jnp.where(real, 1.0, 0.0)


PAD = 16


def tap_block(source_ref, edges_ref, sizes, tap, width):
    dy, dx = tap // 3 - 1, tap % 3 - 1
    pieces = []
    for start, stop, side in ((0, sizes.crop_at, VSIDE), (sizes.crop_at, sizes.rows, CSIDE)):
        shift = dy * side + dx
        values = source_ref[PAD + start + shift : PAD + stop + shift, :]
        mask = None
        for cond, plane in ((dx < 0, 0), (dx > 0, 1), (dy < 0, 2), (dy > 0, 3)):
            if cond:
                edge = edges_ref[plane, start:stop, :]
                mask = edge if mask is None else mask * edge
        if mask is None:
            mask = edges_ref[4, start:stop, :]
        pieces.append((values * wide(mask, width)).astype(BF16))
    return jnp.concatenate(pieces, axis=0)


def k_reduce(xi, xc, w, x, act, stats, flat, *, sizes, steps):
    step = pl.program_id(0)
    micros, _, cols = xc.shape
    views, at = sizes.views, sizes.crop_at
    tiles = cols // 128
    flat[...] = xi[...].astype(F32).reshape(views * micros * tiles, 128)
    for m in range(micros):
        part = [flat[pl.ds(micros * t + m, views, stride=micros * tiles), :] for t in range(tiles)]
        x[m, :at, :] = jnp.concatenate(
            [jnp.concatenate(part, axis=1).astype(BF16), jnp.zeros((at - views, cols), BF16)], axis=0
        )
        tail = sizes.rows - at - sizes.crops
        x[m, at:, :] = jnp.concatenate([xc[m], jnp.zeros((tail, cols), BF16)], axis=0)
    out = dot(together(x), w[...]).reshape(act.shape)

    @pl.when(step == 0)
    def _():
        act[...] = out

    @pl.when(step > 0)
    def _():
        act[...] += out

    @pl.when(step == steps - 1)
    def _():
        put_stats(stats, act, act)


def together(ref):
    return ref[...].reshape(ref.shape[0] * ref.shape[1], ref.shape[2])


def put_stats(stats, first, second):
    for m in range(first.shape[0]):
        a, b = col_sums(first[m], first[m] * second[m])
        stats[m, 0:1, :] = a
        stats[m, 1:2, :] = b


def affine(totals, m, gain, shift, rows):
    means, inv = norm_terms(totals[m], rows)
    scale = inv * gain[...]
    return scale, shift[...] - means * scale, inv, -means * inv


def silu(values):
    half = 0.5 * values
    return half + half * jnp.tanh(half)


def twice_slope(values):
    half = 0.5 * values
    turn = jnp.tanh(half)
    return (1.0 + turn) * (1.0 + half * (1.0 - turn))


def back_terms(totals, sums, m, gain, rows):
    means, inv = norm_terms(totals[m], rows)
    a = gain[...] * inv
    mean_s, mean_sn = sums[m, 0:1] / rows, sums[m, 1:2] / rows
    b = -(a * inv) * mean_sn
    return a, b, -(a * mean_s) - b * means


def set_source(source, edges, sizes):
    micros, _, width = source.shape
    fill_edges(edges, sizes)
    for m in range(micros):
        source[m, :PAD, :] = jnp.zeros((PAD, width), F32)
        source[m, PAD + sizes.rows :, :] = jnp.zeros((PAD, width), F32)


def tap_rows(source, edges, sizes, tap):
    micros, _, width = source.shape
    return jnp.concatenate([tap_block(source.at[m], edges, sizes, tap, width) for m in range(micros)], axis=0)


def k_spatial(act, totals, gain, shift, w, hid, act_two, stats, source, edges, *, sizes, rows):
    step = pl.program_id(0)
    micros, _, width = act.shape

    @pl.when(step == 0)
    def _():
        set_source(source, edges, sizes)
        for m in range(micros):
            scale, bias, _, _ = affine(totals, m, gain, shift, rows)
            hidden = silu(act[m] * scale + bias).astype(BF16)
            hid[m] = hidden
            source[m, PAD : PAD + sizes.rows, :] = hidden.astype(F32)

    for dy in range(3):

        @pl.when(step == dy)
        def _(dy=dy):
            for k in range(3):
                tap = 3 * dy + k
                part = dot(tap_rows(source, edges, sizes, tap), w[k * width : (k + 1) * width, :]).reshape(act_two.shape)
                if tap == 0:
                    act_two[...] = part
                else:
                    act_two[...] += part
            if dy == 2:
                put_stats(stats, act_two, act_two)


def k_expand(act, totals, gain, shift, w, hid, stats, *, sizes, rows):
    micros, n, width = act.shape

    @pl.when(pl.program_id(0) == 0)
    def _():
        keep = wide(sizes.row_mask(), width)
        for m in range(micros):
            scale, bias, _, _ = affine(totals, m, gain, shift, rows)
            hid[m] = jnp.where(keep, silu(act[m] * scale + bias), 0.0).astype(BF16)

    out = dot(together(hid), w[...]).reshape(micros, n, -1)
    put_stats(stats, out, out)


def k_pool(hid, w_expand, totals, gain, shift, x, pool, inv_count, w, pooled, head, stats, *, rows, steps):
    step = pl.program_id(0)
    micros, own, _ = head.shape
    act = dot(together(hid), w_expand[...]).reshape(x.shape)
    low = []
    for m in range(micros):
        scale, bias, _, _ = affine(totals, m, gain, shift, rows)
        low.append(silu((act[m] * scale + bias) + x[m].astype(F32)).astype(BF16))
    low_pooled = (dot(pool[...], jnp.concatenate(low, axis=0)) * inv_count[...]).astype(BF16)
    pooled[...] = low_pooled
    part = dot(low_pooled, w[...])

    @pl.when(step == 0)
    def _():
        for m in range(micros):
            head[m] = part[m * own : (m + 1) * own]

    @pl.when(step > 0)
    def _():
        for m in range(micros):
            head[m] += part[m * own : (m + 1) * own]

    @pl.when(step == steps - 1)
    def _():
        put_stats(stats, head, head)


def head_forward(head, totals, gain, shift, w_embed, count):
    means, inv = norm_terms(totals, count)
    normed = (head - means) * inv
    pre = normed * gain + shift
    hidden = silu(pre).astype(BF16)
    embedding = dot(hidden, w_embed)
    inv_len = lax.rsqrt(jnp.sum(embedding * embedding, axis=1, keepdims=True) + LEN_EPS)
    return normed, pre, inv, hidden, embedding * inv_len, inv_len


def k_embed(where, head, totals, gain, shift, w_embed, pooled, unit_low, *packs_held, count, lines):
    packs, held = packs_held[:-1], packs_held[-1]
    micros, own, width = head.shape
    shard = 4 * lines
    hidden = []
    for m in range(micros):
        _, _, _, hid, unit, _ = head_forward(head[m], totals[m], gain[...], shift[...], w_embed[...], count)
        unit_low[m] = unit.astype(BF16)
        hidden.append(hid.astype(F32))
    both = jnp.concatenate(hidden, axis=0)
    for n in range(4):
        picked = [both[:, s * shard + n * lines : s * shard + (n + 1) * lines] for s in range(width // shard)]
        held[n] = jnp.concatenate(picked, axis=1).astype(BF16)
    chan, sub = pooled.shape[1], held.shape[2]
    for pack, places in zip(packs, ((0,), (1,), (2, 3))):
        pack[:, :chan] = pooled[...]
        for k, place in enumerate(places):
            pack[:, chan + k * sub : chan + (k + 1) * sub] = held[place ^ where[1]]


def k_embed_only(head, totals, gain, shift, w_embed, hidden, unit_low, *, count):
    for m in range(head.shape[0]):
        _, _, _, hid, unit, _ = head_forward(head[m], totals[m], gain[...], shift[...], w_embed[...], count)
        hidden[m] = hid
        unit_low[m] = unit.astype(BF16)


def k_loss(
    units, ids_all, ids_own, pos_all, pos_own, head, totals, gain, shift, w_embed,
    loss, slopes, grad_embed, stats, *, count, loss_scale, block,
):
    everyone = units[0]
    n_all = everyone.shape[0]
    n_own = head.shape[1]

    def add_rows(k, sums):
        start = k * block
        rows = units[0, pl.ds(pl.multiple_of(start, block), block), :]
        scores = dot_nt(rows, everyone) * TAU_INV
        mine = lax.broadcasted_iota(jnp.int32, (block, n_all), 0) + start
        other = lax.broadcasted_iota(jnp.int32, (block, n_all), 1)
        terms = jnp.where(mine == other, 0.0, jnp.exp(scores - TAU_INV))
        return sums + jnp.sum(terms, axis=0, keepdims=True)

    sums = lax.fori_loop(0, n_all // block, add_rows, jnp.zeros((1, n_all), F32))
    log_all = jnp.log(sums) + TAU_INV
    normed, pre, inv, hid, unit, inv_len = head_forward(
        head[0], totals[0], gain[...], shift[...], w_embed[...], count
    )
    low = unit.astype(BF16)
    scores = dot_nt(low, everyone) * TAU_INV
    itself = lax.broadcasted_iota(jnp.int32, (n_own, n_all), 0) == lax.broadcasted_iota(
        jnp.int32, (n_own, n_all), 1
    )
    own_sum = jnp.sum(jnp.where(itself, 0.0, jnp.exp(scores - TAU_INV)), axis=1, keepdims=True)
    log_own = jnp.log(own_sum) + TAU_INV
    positive = (ids_own[0] == ids_all[0]) & jnp.logical_not(itself)
    pos_sum = jnp.sum(jnp.where(positive, scores, 0.0), axis=1, keepdims=True)
    loss[0] = log_own - pos_sum * pos_own[0]
    by_row = jnp.where(itself, 0.0, jnp.exp(scores - log_own)) - jnp.where(positive, pos_own[0], 0.0)
    by_col = jnp.where(itself, 0.0, jnp.exp(scores - log_all)) - jnp.where(positive, pos_all[0], 0.0)
    grad_unit = (
        dot((by_row * loss_scale).astype(BF16), everyone)
        + dot((by_col * loss_scale).astype(BF16), everyone)
    ) * TAU_INV
    grad = inv_len * (grad_unit - unit * jnp.sum(unit * grad_unit, axis=1, keepdims=True))
    grad_low = grad.astype(BF16)
    grad_embed[0] = grad_low
    slope = dot_nt(grad_low, w_embed[...]) * (0.5 * twice_slope(pre))
    slopes[0] = slope
    a, b = col_sums(slope, slope * normed)
    stats[0, 0:1, :] = a
    stats[0, 1:2, :] = b


def k_head_back(where, slopes, head, totals, sums, gain, embed, grad, *packs, count):
    micros, own, width = head.shape
    rows = []
    for m in range(micros):
        a, b, c = back_terms(totals, sums, m, gain, count)
        rows.append(slopes[m] * a + head[m] * b + c)
    grad[...] = jnp.concatenate(rows, axis=0).astype(BF16)
    if packs:
        emb = jnp.concatenate([embed[m].astype(F32) for m in range(micros)], axis=0).astype(BF16)
        quarter = width // 4
        for place, pack in enumerate(packs):
            at = pl.multiple_of((place ^ where[1]) * quarter, quarter)
            pack[:, :quarter] = grad[:, pl.ds(at, quarter)]
            pack[:, quarter:] = emb


def k_back_pool(grad_head, hid, w_expand, totals, gain, shift, x, spread, half_count, w, grad_resid, stats, *, rows):
    micros, n, cols = x.shape
    pair = jnp.concatenate(halves(dot_nt(grad_head[...], w[...]) * half_count[...]), axis=0)
    act = dot(together(hid), w_expand[...])
    back = dot(spread[...], pair)
    for m in range(micros):
        scale, bias, inv, offset = affine(totals, m, gain, shift, rows)
        mine = act[m * n : (m + 1) * n]
        slope = back[m * n : (m + 1) * n] * twice_slope((mine * scale + bias) + x[m].astype(F32))
        grad_resid[m] = slope.astype(BF16)
        a, b = col_sums(slope, slope * (mine * inv + offset))
        stats[m, 0:1, :] = a
        stats[m, 1:2, :] = b


def k_back_expand(
    grad_resid, hid, tot_three, sum_three, gain_three, w, act_two, tot_two, gain_two, shift_two,
    grad_three, slopes, stats, *, sizes, rows, steps,
):
    step = pl.program_id(0)
    micros, n, cols = grad_resid.shape
    act = dot(together(hid), w[...])
    low = []
    for m in range(micros):
        a, b, c = back_terms(tot_three, sum_three, m, gain_three, rows)
        low.append((grad_resid[m].astype(F32) * a + (act[m * n : (m + 1) * n] * b + c)).astype(BF16))
        grad_three[m] = low[m]
    part = dot_nt(jnp.concatenate(low, axis=0), w[...]).reshape(slopes.shape)

    @pl.when(step == 0)
    def _():
        slopes[...] = part

    @pl.when(step > 0)
    def _():
        slopes[...] += part

    @pl.when(step == steps - 1)
    def _():
        finish_slopes(slopes, stats, act_two, tot_two, gain_two, shift_two, rows, wide(sizes.row_mask(), slopes.shape[2]))


def finish_slopes(slopes, stats, act, totals, gain, shift, rows, keep=None):
    for m in range(slopes.shape[0]):
        scale, bias, inv, offset = affine(totals, m, gain, shift, rows)
        slope = slopes[m] * (0.5 * twice_slope(act[m] * scale + bias))
        if keep is not None:
            slope = jnp.where(keep, slope, 0.0)
        slopes[m] = slope
        a, b = col_sums(slope, slope * (act[m] * inv + offset))
        stats[m, 0:1, :] = a
        stats[m, 1:2, :] = b


UNIT = 64
UNITS_A = 5


def k_back_spatial(
    where, slopes, act_two, tot_two, sum_two, gain_two, w, act_one, tot_one, gain_one, shift_one, hid,
    slopes_one, stats, *rest, sizes, rows, shares,
):
    if shares:
        keep_a, send_a, keep_b, send_b, source, edges, turned, block = rest
        core, line = where[1] % 2, where[1] // 2
    else:
        grad_two, source, edges = rest
    step = pl.program_id(0)
    micros, n, mid = act_two.shape

    @pl.when(step == 0)
    def _():
        set_source(source, edges, sizes)
        for m in range(micros):
            a, b, c = back_terms(tot_two, sum_two, m, gain_two, rows)
            low = (slopes[m] * a + (act_two[m] * b + c)).astype(BF16)
            source[m, PAD : PAD + sizes.rows, :] = low.astype(F32)
            if shares:
                turned[:, m * n : (m + 1) * n] = hid[m].T
            else:
                grad_two[m] = low

    def share(tap, here):
        part = dot(turned[...], here)
        for q in range(4):
            block[q] = part[:, 128 * q : 128 * (q + 1)].astype(BF16)
        for unit in range(8 * (8 - tap), 8 * (9 - tap)):
            shard, k = divmod(unit, 9)
            place = shard ^ where[0]
            lines = slice(UNIT * (unit % 8), UNIT * (unit % 8 + 1))
            for y in range(2):
                for out_a, out_b, c in ((keep_a, keep_b, core), (send_a, send_b, 1 - core)):
                    piece = block[2 * y + c, lines, :]
                    if k < UNITS_A:
                        out_a[place % 2, place // 2, y ^ line, k * UNIT : (k + 1) * UNIT, :] = piece
                    else:
                        at = (k - UNITS_A) * UNIT
                        out_b[y ^ line, place % 2, place // 2, at : at + UNIT, :] = piece

    for dy in range(3):

        @pl.when(step == dy)
        def _(dy=dy):
            for k in range(3):
                tap = 3 * dy + k
                here = tap_rows(source, edges, sizes, tap)
                part = dot_nt(here, w[(2 - k) * mid : (3 - k) * mid, :]).reshape(slopes_one.shape)
                if tap == 0:
                    slopes_one[...] = part
                else:
                    slopes_one[...] += part
                if shares:
                    share(tap, here)
            if dy == 2:
                finish_slopes(slopes_one, stats, act_one, tot_one, gain_one, shift_one, rows)


def k_weight_hidden(where, *refs):
    rows, packs = refs[:4], refs[4:8]
    subs = refs[8:12]
    send, keep, grads, extra = refs[12:]
    step = pl.program_id(0)
    quarter = keep.shape[2]

    @pl.when(step == 0)
    def _():
        total = None
        for k in range(4):
            n = packs[k].shape[0]
            grads[k * n : (k + 1) * n, :] = packs[k][:, :quarter].astype(F32)
            part = dot_tn(subs[k][...], packs[k][:, quarter:])
            total = part if total is None else total + part
        extra[...] = total.astype(BF16).reshape(extra.shape)

    pooled = jnp.concatenate([r[...].astype(F32) for r in rows], axis=0).astype(BF16)
    block = dot_tn(pooled, grads[...].astype(BF16)).astype(BF16)
    place = 2 * (step % 4) + 1 - step // 4
    more = extra[place ^ where[0]]
    lines = more.shape[0] // 4

    def store(ref):
        ref[0, : block.shape[0], :] = block
        for k in range(4):
            ref[0, block.shape[0] :, 128 * k : 128 * (k + 1)] = more[lines * k : lines * (k + 1), :]

    @pl.when(step < 4)
    def _():
        store(send)

    @pl.when(step >= 4)
    def _():
        store(keep)


def k_weight_expand(where, hid, grad, keep, send, turned, *, shards):
    micros, rows, mid = hid.shape
    step = pl.program_id(0)

    @pl.when(step == 0)
    def _():
        for m in range(micros):
            turned[:, m * rows : (m + 1) * rows] = hid[m].T

    low = dot(turned[...], together(grad)).astype(BF16)
    each = mid // shards

    def store(out):
        for shard in range(shards):
            place = shard ^ where[0]
            out[place % 2, place // 2, 0] = low[shard * each : (shard + 1) * each]

    @pl.when(step % 2 == 0)
    def _():
        store(keep)

    @pl.when(step % 2 == 1)
    def _():
        store(send)


def k_weight_reduce(
    where, x, slopes, act, totals, sums, gain, grad, keep_a, send_a, keep_b, send_b, turned, block, *, rows
):
    micros, n, mid = slopes.shape
    core, line = where[1] % 2, where[1] // 2

    @pl.when(pl.program_id(0) == 0)
    def _():
        for m in range(micros):
            a, b, c = back_terms(totals, sums, m, gain, rows)
            low = (slopes[m] * a + (act[m] * b + c)).astype(BF16)
            grad[m] = low
            turned[:, m * n : (m + 1) * n] = low.T

    total = dot(turned[...], together(x)).astype(BF16).T
    half = total.shape[0] // 2
    for q in range(4):
        block[q] = total[:, 128 * q : 128 * (q + 1)]
    for y in range(2):
        for out_a, out_b, c in ((keep_a, keep_b, core), (send_a, send_b, 1 - core)):
            out_a[0, 0, y ^ line] = block[2 * y + c, :half, :]
            out_b[y ^ line, 0, 0] = block[2 * y + c, half:, :]


def k_grad_one(slopes, act, totals, sums, gain, grad, *, rows):
    for m in range(slopes.shape[0]):
        a, b, c = back_terms(totals, sums, m, gain, rows)
        grad[m] = (slopes[m] * a + (act[m] * b + c)).astype(BF16)


def k_back_reduce(grad_one, w, grad_resid, *refs, sizes):
    grad_v, grad_c, done = refs[-3:]
    done[...] = jnp.zeros_like(done)
    views, lines, _ = grad_v.shape
    micros = grad_one.shape[0]
    flat = grad_v.reshape(views * lines, 128)
    at = sizes.crop_at
    n = sizes.rows
    back = dot_nt(together(grad_one), w[...])
    for m in range(micros):
        both = grad_resid[m].astype(F32) + back[m * n : (m + 1) * n]
        grad_c[m] = both[at : at + sizes.crops]
        for t in range(lines // micros):
            flat[pl.ds(micros * t + m, views, stride=lines), :] = both[:views, 128 * t : 128 * (t + 1)]


def call(kernel, name, grid, ins, outs, scratch=(), flops=0, vmem=56, where=None, aliases=None):
    spec = lambda block, index: pl.BlockSpec(block, index) if block else pl.BlockSpec(memory_space=pl.ANY)
    scalars = [] if where is None else [where]
    moved = sum(a.size * a.dtype.itemsize for a, _, _ in ins) + sum(
        math.prod(s) * jnp.dtype(t).itemsize for s, t, _, _ in outs
    )
    return pl.pallas_call(
        kernel,
        grid_spec=pltpu.PrefetchScalarGridSpec(
            num_scalar_prefetch=len(scalars),
            grid=grid,
            in_specs=[spec(b, i) for _, b, i in ins],
            out_specs=[spec(b, i) for _, _, b, i in outs],
            scratch_shapes=list(scratch),
        ),
        out_shape=[jax.ShapeDtypeStruct(s, t) for s, t, _, _ in outs],
        compiler_params=pltpu.CompilerParams(vmem_limit_bytes=vmem * MIB),
        cost_estimate=pl.CostEstimate(flops=1000, bytes_accessed=1000, transcendentals=0),
        name=name,
        input_output_aliases=aliases or {},
    )(*scalars, *[a for a, _, _ in ins])


def exact(array):
    return lax.optimization_barrier(array)


def add_low(*parts):
    total = parts[0].astype(F32)
    for part in parts[1:]:
        total = total + part.astype(F32)
    return total.astype(BF16)


def reduce_weight(grad, count, data_size, narrow_size):
    rows, cols = grad.shape
    me = lax.axis_index("dp")
    core = lax.axis_index("narrow") % 2
    blocks = grad.reshape(data_size, rows // data_size, cols)
    blocks = jnp.stack(
        [lax.dynamic_index_in_dim(blocks, me ^ j, axis=0, keepdims=False) for j in range(data_size)]
    )
    half = cols // 2
    low, high = blocks[:, :, :half], blocks[:, :, half:]
    keep = jnp.where(core == 0, low, high)
    send = jnp.where(core == 0, high, low)
    part = add_low(keep, xor_permute(send, 1, count))
    size = data_size
    for stage in bit_stages(0, data_size.bit_length() - 1):
        if len(stage) == 1:
            split = part.reshape((size // 2, 2) + part.shape[1:])
            part = add_low(split[:, 0], xor_permute(split[:, 1], stage[0] * narrow_size, count))
            size //= 2
        else:
            split = part.reshape((size // 4, 4) + part.shape[1:])
            got = [
                xor_permute(split[:, k], off * narrow_size, count)
                for k, off in ((1, stage[0]), (2, stage[1]), (3, stage[0] ^ stage[1]))
            ]
            part = add_low(split[:, 0], *got)
            size //= 4
    part = exact(part[0])
    off = 2
    while off < narrow_size:
        part = exact(add_low(part, xor_permute(part, off, count)))
        off *= 2
    other = xor_permute(part, 1, count)
    both = jnp.where(
        core == 0, jnp.concatenate([part, other], axis=1), jnp.concatenate([other, part], axis=1)
    )
    return both.astype(F32)


class Mesh84:
    core, line, x, z = 1, 2, 4, 8

    def __init__(self, count):
        self.count = count

    def send(self, array, offset):
        return xor_permute(array, offset, self.count)

    def split(self, keep, got):
        return [add_low(keep[k], got[k]) for k in range(keep.shape[0])]

    def across_z(self, parts, *others):
        sent = [after(p, *others) if others else p for p in parts[1:]]
        return [parts[0]] + [self.send(sent[k - 1], self.z * k) for k in (1, 2, 3)]

    def quarters(self, near, far, narrow):
        places = (near[0], far[0], near[1], far[1])
        pick = lambda q: lax.select_n(narrow, *(places[q ^ n] for n in range(4)))
        return jnp.concatenate([pick(q) for q in range(4)], axis=-1)


def after(value, *others):
    return lax.optimization_barrier((value, *others))[0]


def finish_a(net, got, narrow):
    part = exact(add_low(*got))
    part = exact(add_low(part, net.send(part, net.line)[::-1]))
    return net.quarters(part, net.send(part, net.core), narrow)


def finish_b(net, got, narrow):
    part = exact(add_low(*got))
    pair = jnp.stack([part, net.send(part, net.line)])
    return net.quarters(pair, net.send(pair, net.core), narrow)


def expand_share(hid, grad, where):
    micros, rows, mid = hid.shape
    quarter = grad.shape[2] // 4
    each = mid // 8
    shape = (2, 4, 2, each, quarter)
    block = (2, 4, 1, each, quarter)
    at = lambda q, w: (0, 0, q // 2, 0, 0)
    return call(
        functools.partial(k_weight_expand, shards=8), "weight_expand", (4,),
        [
            (hid, (micros, rows, mid), lambda q, w: (0, 0, 0)),
            (grad, (micros, rows, quarter), lambda q, w: (0, 0, q ^ w[1])),
        ],
        [(shape, BF16, block, at), (shape, BF16, block, at)],
        scratch=[pltpu.VMEM((mid, micros * rows), BF16)],
        flops=2 * micros * rows * mid * grad.shape[2],
        where=where,
    )


def hidden_share(rows, packs, where):
    total, wide_cols = rows[0].shape
    chan = wide_cols * 4 // 5
    sub = wide_cols - chan
    emb = packs[0].shape[1] - sub
    shard = chan // 8
    extra = sub // 8 * emb // sub
    place = lambda i: 2 * (i % 4) + 1 - i // 4
    fix = lambda i, w: (0, 0)
    out = ((4, shard + extra, sub), BF16, (1, shard + extra, sub))
    return call(
        k_weight_hidden, "weight_hidden", (8,),
        [(r, (total, shard), lambda i, w: (0, place(i) ^ w[0])) for r in rows]
        + [(p, p.shape, fix) for p in packs]
        + [(r, (total, sub), lambda i, w: (0, chan // sub)) for r in rows],
        [
            out + (lambda i, w: (jnp.minimum(i, 3), 0, 0),),
            out + (lambda i, w: (jnp.maximum(i - 4, 0), 0, 0),),
        ],
        scratch=[pltpu.VMEM((4 * total, sub), F32), pltpu.VMEM((8, sub // 8, emb), BF16)],
        flops=8 * total * chan * sub,
        where=where,
    )[::-1]


def spread_taps(hidden, side):
    padded = jnp.pad(hidden, ((0, 0), (1, 1), (1, 1), (0, 0)))
    pieces = [padded[:, dy : dy + side, dx : dx + side, :] for dy in range(3) for dx in range(3)]
    return jnp.concatenate(pieces, axis=-1)


def body(
    view_maps, crop_maps, image_ids, w_reduce, gain_one, shift_one, w_spatial, gain_two, shift_two,
    w_expand, gain_three, shift_three, w_hidden, gain_head, shift_head, w_embed,
):
    micros, view_rows, channels = view_maps.shape
    crop_rows = crop_maps.shape[1]
    mid = w_reduce.shape[1]
    hidden_width = w_hidden.shape[1]
    emb_width = w_embed.shape[1]
    images_dev = view_rows // (VIEWS * VSIDE * VSIDE)
    each = VIEWS + CROPS
    own = images_dev * each
    data_size, narrow_size = lax.axis_size("dp"), lax.axis_size("narrow")
    count = data_size * narrow_size
    emb_total = own * count
    pixel_count = (view_rows + crop_rows) * count
    loss_scale = 1.0 / (micros * emb_total)
    device = lax.axis_index("dp") * narrow_size + lax.axis_index("narrow")
    sizes = Sizes(view_rows, crop_rows)
    rows = sizes.rows

    pool = np.zeros((micros, own, micros, rows), np.float32)
    for m in range(micros):
        for r in range(view_rows):
            image, view = divmod(r // (VSIDE * VSIDE), VIEWS)
            pool[m, image * each + view, m, r] = 1
        for r in range(crop_rows):
            image, crop = divmod(r // (CSIDE * CSIDE), CROPS)
            pool[m, image * each + VIEWS + crop, m, sizes.crop_at + r] = 1
    pool = pool.reshape(micros * own, micros * rows)
    inv_count = np.where(np.arange(micros * own) % each < VIEWS, 1.0 / VSIDE**2, 1.0 / CSIDE**2)[:, None]
    spread = jnp.asarray(np.concatenate([pool.T, pool.T], axis=1), BF16)
    pool = jnp.asarray(pool, BF16)
    half_count = jnp.asarray(0.5 * inv_count, F32)
    inv_count = jnp.asarray(inv_count, F32)

    place = jnp.asarray(gather_order(count)) ^ device
    same = jnp.sum((image_ids[:, :, None] == image_ids[:, None, :]).astype(F32), axis=2)
    inv_pos = 1.0 / (same * each - 1.0)

    from_device = place[:, None] == jnp.arange(count, dtype=jnp.int32)[None, :]

    def by_place(values):
        blocks = values.reshape(micros, 1, count, images_dev)
        moved = jnp.sum(jnp.where(from_device[None, :, :, None], blocks, 0), axis=2)
        return jnp.repeat(moved.reshape(micros, -1), each, axis=1)

    ids_all, pos_all = by_place(image_ids), by_place(inv_pos)
    ids_own, pos_own = ids_all[:, :own, None], pos_all[:, :own, None]
    ids_all, pos_all = ids_all[:, None, :], pos_all[:, None, :]

    row = lambda v: v.reshape(1, -1)
    g1, b1, g2, b2 = row(gain_one), row(shift_one), row(gain_two), row(shift_two)
    g3, b3, gh, bh = row(gain_three), row(shift_three), row(gain_head), row(shift_head)
    reduce_all = lambda stats: all_sum(stats, count)
    flops = 2.0 * micros * rows * channels * mid

    fast = data_size == 8 and narrow_size == 4 and mid == 512 and micros == 2
    dp, narrow = lax.axis_index("dp"), lax.axis_index("narrow")
    where = jnp.stack([dp, narrow]).astype(jnp.int32)
    net = Mesh84(count)
    blk = 512
    steps = channels // blk
    fix2 = lambda *_: (0, 0)
    fix3 = lambda *_: (0, 0, 0)
    col = lambda n, *_: (0, n)
    col3 = lambda n, *_: (0, 0, n)
    row = lambda n, *_: (n, 0)
    m0 = lambda m, *_: (m, 0, 0)
    act_mid = (micros, rows, mid)
    two = lambda array: (array, array.shape, fix3)
    vec = lambda array: (array, array.shape, fix2)
    vec_block = lambda array: (array, (1, blk), col)
    tot_block = lambda array: (array, (micros, 2, blk), col3)
    stats_of = lambda width: ((micros, 2, width), F32, (micros, 2, width), fix3)

    tiles = channels // 128
    mixed = jnp.transpose(view_maps.reshape(micros, view_rows, tiles, 128), (1, 2, 0, 3))
    mixed = mixed.reshape(view_rows, micros * tiles, 128)
    lines = micros * blk // 128
    pixels, act_one, st = call(
        functools.partial(k_reduce, sizes=sizes, steps=steps), "reduce", (steps,),
        [
            (mixed, (view_rows, lines, 128), lambda n: (0, n, 0)),
            (crop_maps, (micros, crop_rows, blk), col3),
            (w_reduce, (blk, mid), row),
        ],
        [
            ((micros, rows, channels), BF16, (micros, rows, blk), col3),
            (act_mid, F32, act_mid, fix3),
            stats_of(mid),
        ],
        scratch=[pltpu.VMEM((view_rows * lines, 128), F32)],
        flops=flops,
    )
    tot_one = reduce_all(st)
    taps_scratch = [
        pltpu.VMEM((micros, rows + 2 * PAD, mid), F32),
        pltpu.VMEM((5, rows, 128), F32),
    ]
    hid_one, act_two, st = call(
        functools.partial(k_spatial, sizes=sizes, rows=pixel_count), "spatial", (3,),
        [two(act_one), two(tot_one), vec(g1), vec(b1), (w_spatial, (3 * mid, mid), row)],
        [(act_mid, BF16, act_mid, fix3), (act_mid, F32, act_mid, fix3), stats_of(mid)],
        scratch=taps_scratch,
        flops=flops * 9 * mid / channels,
    )
    tot_two = reduce_all(st)
    hid_two, st = call(
        functools.partial(k_expand, sizes=sizes, rows=pixel_count), "expand", (steps,),
        [two(act_two), two(tot_two), vec(g2), vec(b2), (w_expand, (mid, blk), col)],
        [(act_mid, BF16, act_mid, fix3), ((micros, 2, channels), F32, (micros, 2, blk), col3)],
        flops=flops,
    )
    tot_three = reduce_all(st)
    flat_own = micros * own
    pooled, head, st = call(
        functools.partial(k_pool, rows=pixel_count, steps=steps), "pool", (steps,),
        [
            two(hid_two),
            (w_expand, (mid, blk), col),
            tot_block(tot_three),
            vec_block(g3),
            vec_block(b3),
            (pixels, (micros, rows, blk), col3),
            vec(pool),
            vec(inv_count),
            (w_hidden, (blk, hidden_width), row),
        ],
        [
            ((flat_own, channels), BF16, (flat_own, blk), col),
            ((micros, own, hidden_width), F32, (micros, own, hidden_width), fix3),
            stats_of(hidden_width),
        ],
        flops=flops,
    )
    tot_head = reduce_all(st)
    head_in = [two(head), two(tot_head), vec(gh), vec(bh), vec(w_embed)]
    unit_shape = (micros, own, emb_width)
    if fast:
        sub = hidden_width // 4
        pack = (flat_own, channels + sub)
        unit_low, *rows_packs = call(
            functools.partial(k_embed, count=emb_total, lines=sub // 8), "embed", (1,), head_in + [vec(pooled)],
            [(unit_shape, BF16, unit_shape, fix3)] + [(pack, BF16, pack, fix2)] * 2
            + [((flat_own, channels + 2 * sub), BF16, (flat_own, channels + 2 * sub), fix2)],
            scratch=[pltpu.VMEM((4, flat_own, sub), BF16)],
            where=where,
        )
    else:
        head_hid, unit_low = call(
            functools.partial(k_embed_only, count=emb_total), "embed", (1,), head_in,
            [
                ((micros, own, hidden_width), BF16, (micros, own, hidden_width), fix3),
                (unit_shape, BF16, unit_shape, fix3),
            ],
        )
    units = gather_all(unit_low, count)
    units = jnp.transpose(units, (1, 0, 2, 3)).reshape(micros, emb_total, emb_width)
    if fast:
        pack_own, pack_core, pack_line = (after(p, units) for p in rows_packs)
        got_core = net.send(pack_core, net.core)
        got_line = net.send(pack_line, net.line)
    loss, slopes, grad_embed, st = call(
        functools.partial(k_loss, count=emb_total, loss_scale=loss_scale, block=128), "loss", (micros,),
        [
            (units, (1, emb_total, emb_width), m0),
            (ids_all, (1, 1, emb_total), m0),
            (ids_own, (1, own, 1), m0),
            (pos_all, (1, 1, emb_total), m0),
            (pos_own, (1, own, 1), m0),
            (head, (1, own, hidden_width), m0),
            (tot_head, (1, 2, hidden_width), m0),
            vec(gh),
            vec(bh),
            vec(w_embed),
        ],
        [
            ((micros, own, 1), F32, (1, own, 1), m0),
            ((micros, own, hidden_width), F32, (1, own, hidden_width), m0),
            (unit_shape, BF16, (1, own, emb_width), m0),
            ((micros, 2, hidden_width), F32, (1, 2, hidden_width), m0),
        ],
    )
    if fast:
        got_core, got_line = (after(g, st) for g in (got_core, got_line))
        st = after(st, got_line)
        wide_cols = channels + sub
        pass_on = jnp.concatenate([got_line[:, :channels], got_line[:, wide_cols:]], axis=1)
        rows_packs = [pack_own, got_core, got_line[:, :wide_cols], net.send(pass_on, net.core)]
    sum_head = reduce_all(st)

    grad_head, *packs = call(
        functools.partial(k_head_back, count=emb_total), "head_back", (1,),
        [two(slopes), two(head), two(tot_head), two(sum_head), vec(gh), two(grad_embed)],
        [((flat_own, hidden_width), BF16, (flat_own, hidden_width), fix2)]
        + [((flat_own, hidden_width // 4 + emb_width), BF16, (flat_own, hidden_width // 4 + emb_width), fix2)]
        * (4 if fast else 0),
        where=where,
    )
    if fast:
        packs = packs[:1] + [net.send(packs[k], k) for k in (1, 2, 3)]
    grad_resid, st = call(
        functools.partial(k_back_pool, rows=pixel_count), "back_pool", (steps,),
        [
            vec(grad_head),
            two(hid_two),
            (w_expand, (mid, blk), col),
            tot_block(tot_three),
            vec_block(g3),
            vec_block(b3),
            (pixels, (micros, rows, blk), col3),
            vec(spread),
            vec(half_count),
            (w_hidden, (blk, hidden_width), row),
        ],
        [
            ((micros, rows, channels), BF16, (micros, rows, blk), col3),
            ((micros, 2, channels), F32, (micros, 2, blk), col3),
        ],
        flops=flops,
    )
    if fast:
        packs = packs[:1] + [after(g, st) for g in packs[1:]]
        wh_keep, wh_send = hidden_share(rows_packs, packs, where)
    sum_three = reduce_all(st)
    if fast:
        wh_got = net.send(after(wh_send, sum_three), net.x)
        grad_resid = after(grad_resid, wh_send, wh_keep)
    grad_three, slopes_two, st = call(
        functools.partial(k_back_expand, sizes=sizes, rows=pixel_count, steps=steps), "back_expand", (steps,),
        [
            (grad_resid, (micros, rows, blk), col3),
            two(hid_two),
            tot_block(tot_three),
            tot_block(sum_three),
            vec_block(g3),
            (w_expand, (mid, blk), col),
            two(act_two),
            two(tot_two),
            vec(g2),
            vec(b2),
        ],
        [
            ((micros, rows, channels), BF16, (micros, rows, blk), col3),
            (act_mid, F32, act_mid, fix3),
            stats_of(mid),
        ],
        flops=2 * flops,
    )
    if fast:
        w3_keep, w3_send = expand_share(hid_two, grad_three, where)
        w3_got = net.send(w3_send, net.core)
        wh_z = net.split(wh_keep, after(wh_got, st, w3_send))
        w3_x = net.split(w3_keep, w3_got)
        st = after(st, wh_got)
    sum_two = reduce_all(st)
    if fast:
        wh_got = net.across_z(wh_z, sum_two)
        w3_got = net.send(after(w3_x[1], sum_two), net.x)
        slopes_two = after(slopes_two, *wh_z, *w3_x)
    shapes = [(2, 4, 2, UNITS_A * UNIT, 128)] * 2 + [(2, 2, 4, (9 - UNITS_A) * UNIT, 128)] * 2
    slopes_one, st, *rest = call(
        functools.partial(k_back_spatial, sizes=sizes, rows=pixel_count, shares=fast), "back_spatial", (3,),
        [
            two(slopes_two),
            two(act_two),
            two(tot_two),
            two(sum_two),
            vec(g2),
            (w_spatial, (3 * mid, mid), lambda n, *_: (2 - n, 0)),
            two(act_one),
            two(tot_one),
            vec(g1),
            vec(b1),
            two(hid_one),
        ],
        [(act_mid, F32, act_mid, fix3), stats_of(mid)]
        + ([(t, BF16, t, lambda *_: (0,) * 5) for t in shapes] if fast else [(act_mid, BF16, act_mid, fix3)]),
        scratch=taps_scratch
        + ([pltpu.VMEM((mid, micros * rows), BF16), pltpu.VMEM((4, mid, 128), BF16)] if fast else []),
        flops=2 * flops * 9 * mid / channels,
        where=where,
    )
    if fast:
        w2_keep_a, w2_send_a, w2_keep_b, w2_send_b = rest
        wh_part = exact(add_low(*(after(g, st) for g in wh_got)))
        w3_z = net.split(w3_x[0], after(w3_got, st))
        st = after(st, *wh_got, w3_got)
        first = []
        sum_one = all_sum(st, count, first.append)
        w2_got_a, w2_got_b = (net.send(after(g, *first), net.core) for g in (w2_send_a, w2_send_b))
        w2_x = net.split(w2_keep_a, w2_got_a)
        w2_y = net.split(w2_keep_b, w2_got_b)
        w2_got_a = net.send(after(w2_x[1], sum_one), net.x)
        w2_got_b = net.send(after(w2_y[1], sum_one), net.line)
        w3_got = net.across_z(w3_z, sum_one)
    else:
        sum_one = reduce_all(st)
    one_in = [two(slopes_one), two(act_one), two(tot_one), two(sum_one), vec(g1)]
    if fast:
        one_in[0] = two(after(slopes_one, *w3_z, *w2_x, *w2_y, wh_part))
        shard = channels // 8
        half = shard // 2
        at_a = lambda j, w: (j % 2, j // 2, 0, 0, 0)
        at_b = lambda j, w: (0, j % 2, j // 2, 0, 0)
        out_a = ((2, 4, 2, half, 128), BF16, (1, 1, 2, half, 128), at_a)
        out_b = ((2, 2, 4, half, 128), BF16, (2, 1, 1, half, 128), at_b)
        grad_one, w1_keep_a, w1_send_a, w1_keep_b, w1_send_b = call(
            functools.partial(k_weight_reduce, rows=pixel_count), "weight_reduce", (8,),
            [(pixels, (micros, rows, shard), lambda j, w: (0, 0, j ^ w[0]))] + one_in,
            [(act_mid, BF16, act_mid, fix3), out_a, out_a, out_b, out_b],
            scratch=[pltpu.VMEM((mid, micros * rows), BF16), pltpu.VMEM((4, shard, 128), BF16)],
            flops=flops,
            where=where,
        )
        w1_got_a, w1_got_b = net.send(w1_send_a, net.core), net.send(w1_send_b, net.core)
        late = lambda g: after(g, w1_send_a)
        w2_z = net.split(w2_x[0], late(w2_got_a))
        w2_x = net.split(w2_y[0], late(w2_got_b))
        w3_part = exact(add_low(*map(late, w3_got)))
        w2_got_a = net.across_z(w2_z)
        w2_got_b = net.send(w2_x[1], net.x)
        w3_line = net.send(w3_part, net.line)
        grad_one = after(grad_one, *w2_z, *w2_x, w3_part)
    else:
        (grad_one,) = call(
            functools.partial(k_grad_one, rows=pixel_count), "grad_one", (1,), one_in, [(act_mid, BF16, act_mid, fix3)]
        )
    def back_reduce(first, grads, before=()):
        at = lambda n: n + first
        return call(
            functools.partial(k_back_reduce, sizes=sizes), "back_reduce", (steps // 2,),
            [
                two(grads),
                (w_reduce, (blk, mid), lambda n: (at(n), 0)),
                (grad_resid, (micros, rows, blk), lambda n: (0, 0, at(n))),
            ]
            + [(b, None, None) for b in before],
            [
                ((view_rows, micros * tiles, 128), F32, (view_rows, lines, 128), lambda n: (0, at(n), 0)),
                (crop_maps.shape, F32, (micros, crop_rows, blk), lambda n: (0, 0, at(n))),
                ((8, 128), F32, (8, 128), fix2),
            ],
            flops=flops / 2,
            aliases={3 + k: k for k in range(len(before))},
        )

    grad_views, grad_crops, done = back_reduce(0, grad_one)
    if fast:
        late = lambda g: after(g, done)
        w1_x = net.split(w1_keep_a, late(w1_got_a))
        w1_y = net.split(w1_keep_b, late(w1_got_b))
        w1_got_a, w1_got_b = net.send(w1_x[1], net.x), net.send(w1_y[1], net.line)
        wh_line = net.send(after(wh_part, done), net.line)
        grad_one = after(grad_one, *w1_x, *w1_y)
    grad_views, grad_crops, done = back_reduce(steps // 2, grad_one, (grad_views, grad_crops))
    grad_views = jnp.transpose(grad_views.reshape(view_rows, tiles, micros, 128), (2, 0, 1, 3)).reshape(view_maps.shape)

    if fast:
        late = lambda g: after(g, done)
        lines = w_hidden.shape[0] // data_size
        wh_pair = jnp.stack([wh_part, late(wh_line)])
        far = net.send(wh_pair, net.core)
        gw_hidden = net.quarters(wh_pair[:, :lines], far[:, :lines], narrow).astype(F32)
        extra = net.quarters(wh_pair[:, lines:], far[:, lines:], narrow)
        extra = extra.reshape(-1, 4, 4, emb_width)
        gw_embed = jnp.transpose(extra, (1, 2, 0, 3)).reshape(-1, emb_width).astype(F32)
        w2_b = net.across_z(net.split(w2_x[0], late(w2_got_b)))
        w1_z = net.split(w1_x[0], late(w1_got_a))
        w1_x = net.split(w1_y[0], late(w1_got_b))
        w1_a = net.across_z(w1_z)
        w1_b = net.across_z(net.split(w1_x[0], net.send(w1_x[1], net.x)))
        w2_b = finish_b(net, w2_b, narrow)
        w2_a = finish_a(net, [late(g) for g in w2_got_a], narrow)
        w1_a = finish_a(net, w1_a, narrow)
        w1_b = finish_b(net, w1_b, narrow)
        gw_spatial = jnp.concatenate([w2_a, w2_b], axis=0).astype(F32)
        w3_part = exact(add_low(w3_part, late(w3_line)[::-1]))
        gw_expand = net.quarters(w3_part, net.send(w3_part, net.core), narrow).astype(F32)
        gw_reduce = jnp.concatenate([w1_a, w1_b], axis=0).astype(F32)
    else:
        over = lambda a, b: jnp.einsum("mri,mrj->ij", a, b, preferred_element_type=F32)
        reduce_w = lambda g: reduce_weight(g.astype(BF16), count, data_size, narrow_size)
        gw_embed = reduce_w(over(head_hid, grad_embed))
        gw_hidden = reduce_w(jnp.dot(pooled.T, grad_head, preferred_element_type=F32))
        gw_expand = reduce_w(over(hid_two, grad_three))
        at = sizes.crop_at
        real = lambda t: (t[:, :view_rows], t[:, at : at + crop_rows])
        cols = [
            spread_taps(part.reshape(-1, side, side, mid), side).reshape(micros, -1, 9, mid)
            for part, side in zip(real(rest[0]), (VSIDE, CSIDE))
        ]
        by_tap = jnp.einsum(
            "mri,mrtj->tij", jnp.concatenate(real(hid_one), axis=1), jnp.concatenate(cols, axis=1),
            preferred_element_type=F32,
        )[::-1]
        gw_spatial = reduce_w(by_tap.reshape(9 * mid, mid))
        gw_reduce = reduce_w(over(pixels, grad_one))
    gain_grad = lambda sums: jnp.sum(sums[:, 1], axis=0)
    shift_grad = lambda sums: jnp.sum(sums[:, 0], axis=0)
    return (
        loss.reshape(micros, own), grad_views, grad_crops,
        gw_reduce, gain_grad(sum_one), shift_grad(sum_one),
        gw_spatial, gain_grad(sum_two), shift_grad(sum_two),
        gw_expand, gain_grad(sum_three), shift_grad(sum_three),
        gw_hidden, gain_grad(sum_head), shift_grad(sum_head),
        gw_embed,
    )


def solution(mesh):
    rows = P(None, BOTH, None)
    return jax.shard_map(
        body,
        mesh=mesh,
        in_specs=(rows, rows) + (P(),) * 14,
        out_specs=(
            P(None, BOTH), rows, rows,
            P("dp", None), P(), P(),
            P("dp", None), P(), P(),
            P("dp", None), P(), P(),
            P("dp", None), P(), P(),
            P("dp", None),
        ),
        check_vma=False,
    )
```

```python
import functools
import math

import jax
import jax.numpy as jnp
import numpy as np
from jax import lax
from jax.experimental import pallas as pl
from jax.experimental.pallas import tpu as pltpu
from jax.sharding import PartitionSpec as P

VIEWS = 2
CROPS = 4
VSIDE = 7
CSIDE = 3
TAU_INV = 10.0
LOG2E = math.log2(math.e)
EPS = 1e-05
LEN_EPS = 1e-06
BOTH = ("dp", "narrow")
F32 = jnp.float32
BF16 = jnp.bfloat16
MIB = 1 << 20


def round_up(value, step):
    return -(-value // step) * step


def xor_permute(array, offset, count):
    return lax.ppermute(array, BOTH, [(i, i ^ offset) for i in range(count)])


def bit_stages(first, last):
    bits = [1 << b for b in range(first, last)]
    stages = [bits[:1]] if bits else []
    rest = bits[1:]
    while rest:
        stages.append(rest[:2])
        rest = rest[2:]
    return stages


def all_sum(array, count, begun=None):
    for stage in bit_stages(0, count.bit_length() - 1):
        if len(stage) == 1:
            array = array + xor_permute(array, stage[0], count)
            if begun is not None:
                begun(array)
                begun = None
        else:
            low, high = stage
            near = xor_permute(array, low, count)
            far = xor_permute(array, high, count)
            across = xor_permute(array, low ^ high, count)
            array = (array + near) + (far + across)
    return array


def gather_all(array, count):
    parts = [array]
    stages = bit_stages(0, count.bit_length() - 1)
    for stage in stages[:0:-1] + stages[:1]:
        offsets = stage if len(stage) == 1 else [stage[0], stage[1], stage[0] ^ stage[1]]
        block = jnp.stack(parts) if len(parts) > 1 else parts[0][None]
        arrived = [xor_permute(block, off, count) for off in offsets]
        parts = [p for p in parts]
        for got in arrived:
            parts.extend(got[k] for k in range(got.shape[0]))
    return jnp.stack(parts)


def gather_order(count):
    order = [0]
    stages = bit_stages(0, count.bit_length() - 1)
    for stage in stages[:0:-1] + stages[:1]:
        offsets = stage if len(stage) == 1 else [stage[0], stage[1], stage[0] ^ stage[1]]
        order = order + [o ^ off for off in offsets for o in order]
    return np.array(order, np.int32)


def dot(left, right):
    return jnp.dot(left, right, preferred_element_type=F32)


def dot_tn(left, right):
    return lax.dot_general(left, right, (((0,), (0,)), ((), ())), preferred_element_type=F32)


def dot_nt(left, right):
    return lax.dot_general(left, right, (((1,), (1,)), ((), ())), preferred_element_type=F32)


def norm_terms(totals, rows):
    means = totals[0:1] / rows
    variance = totals[1:2] / rows - means * means
    return means, lax.rsqrt(variance + EPS)


def halves(values):
    high = values.astype(BF16)
    return high, (values - high.astype(F32)).astype(BF16)


def col_sums(first, second):
    return jnp.sum(first, axis=0, keepdims=True), jnp.sum(second, axis=0, keepdims=True)


class Sizes:
    def __init__(self, view_rows, crop_rows):
        self.views, self.crops = view_rows, crop_rows
        self.crop_at = round_up(view_rows, 16)
        self.rows = self.crop_at + round_up(crop_rows, 16)

    def row_mask(self):
        row = lax.broadcasted_iota(jnp.int32, (self.rows, 128), 0)
        inside = (row < self.views) | ((row >= self.crop_at) & (row < self.crop_at + self.crops))
        return inside


def wide(mask, cols):
    return jnp.concatenate([mask] * (cols // 128), axis=1)


def fill_edges(edges_ref, sizes):
    for start, stop, at, side in (
        (0, sizes.crop_at, sizes.views, VSIDE),
        (sizes.crop_at, sizes.rows, sizes.crop_at + sizes.crops, CSIDE),
    ):
        count = stop - start
        row = lax.broadcasted_iota(jnp.int32, (count, 128), 0)
        real = row < (at - start)
        rowf = row.astype(F32) + 0.5
        line = jnp.floor(rowf * (1.0 / side))
        col = rowf - 0.5 - line * side
        in_map = line - jnp.floor((line + 0.5) * (1.0 / side)) * side
        keep = (col > 0.5, col < side - 1.5, in_map > 0.5, in_map < side - 1.5)
        for k in range(4):
            edges_ref[k, start:stop, :] = jnp.where(real & keep[k], 1.0, 0.0)
        edges_ref[4, start:stop, :] = jnp.where(real, 1.0, 0.0)


PAD = 16


def tap_block(source_ref, edges_ref, sizes, tap, width):
    dy, dx = tap // 3 - 1, tap % 3 - 1
    pieces = []
    for start, stop, side in ((0, sizes.crop_at, VSIDE), (sizes.crop_at, sizes.rows, CSIDE)):
        shift = dy * side + dx
        values = source_ref[PAD + start + shift : PAD + stop + shift, :]
        mask = None
        for cond, plane in ((dx < 0, 0), (dx > 0, 1), (dy < 0, 2), (dy > 0, 3)):
            if cond:
                edge = edges_ref[plane, start:stop, :]
                mask = edge if mask is None else mask * edge
        if mask is None:
            mask = edges_ref[4, start:stop, :]
        pieces.append((values * wide(mask, width)).astype(BF16))
    return jnp.concatenate(pieces, axis=0)


def k_reduce(xi, xc, w, x, act, stats, flat, *, sizes, steps):
    step = pl.program_id(0)
    micros, _, cols = xc.shape
    views, at = sizes.views, sizes.crop_at
    tiles = cols // 128
    flat[...] = xi[...].astype(F32).reshape(views * micros * tiles, 128)
    for m in range(micros):
        part = [flat[pl.ds(micros * t + m, views, stride=micros * tiles), :] for t in range(tiles)]
        x[m, :at, :] = jnp.concatenate(
            [jnp.concatenate(part, axis=1).astype(BF16), jnp.zeros((at - views, cols), BF16)], axis=0
        )
        tail = sizes.rows - at - sizes.crops
        x[m, at:, :] = jnp.concatenate([xc[m], jnp.zeros((tail, cols), BF16)], axis=0)
    out = dot(together(x), w[...]).reshape(act.shape)

    @pl.when(step == 0)
    def _():
        act[...] = out

    @pl.when(step > 0)
    def _():
        act[...] += out

    @pl.when(step == steps - 1)
    def _():
        put_stats(stats, act, act)


def together(ref):
    return ref[...].reshape(ref.shape[0] * ref.shape[1], ref.shape[2])


def put_stats(stats, first, second):
    for m in range(first.shape[0]):
        a, b = col_sums(first[m], first[m] * second[m])
        stats[m, 0:1, :] = a
        stats[m, 1:2, :] = b


def chunks(rows):
    step = rows // 3 if rows % 48 == 0 else rows
    return [slice(at, at + step) for at in range(0, rows, step)]


def affine(totals, m, gain, shift, rows):
    means, inv = norm_terms(totals[m], rows)
    scale = inv * gain[...]
    return scale, shift[...] - means * scale, inv, -means * inv


def silu(values):
    half = 0.5 * values
    return half + half * jnp.tanh(half)


def twice_slope(values):
    half = 0.5 * values
    turn = jnp.tanh(half)
    return (1.0 + turn) * (1.0 + half * (1.0 - turn))


def back_terms(totals, sums, m, gain, rows):
    means, inv = norm_terms(totals[m], rows)
    a = gain[...] * inv
    mean_s, mean_sn = sums[m, 0:1] / rows, sums[m, 1:2] / rows
    b = -(a * inv) * mean_sn
    return a, b, -(a * mean_s) - b * means


def set_source(source, edges, sizes):
    micros, _, width = source.shape
    fill_edges(edges, sizes)
    for m in range(micros):
        source[m, :PAD, :] = jnp.zeros((PAD, width), F32)
        source[m, PAD + sizes.rows :, :] = jnp.zeros((PAD, width), F32)


def tap_rows(source, edges, sizes, tap):
    micros, _, width = source.shape
    return jnp.concatenate([tap_block(source.at[m], edges, sizes, tap, width) for m in range(micros)], axis=0)


def k_spatial(act, totals, gain, shift, w, hid, act_two, stats, source, edges, *, sizes, rows):
    step = pl.program_id(0)
    micros, _, width = act.shape

    @pl.when(step == 0)
    def _():
        set_source(source, edges, sizes)
        for m in range(micros):
            scale, bias, _, _ = affine(totals, m, gain, shift, rows)
            hidden = silu(act[m] * scale + bias).astype(BF16)
            hid[m] = hidden
            source[m, PAD : PAD + sizes.rows, :] = hidden.astype(F32)

    for dy in range(3):

        @pl.when(step == dy)
        def _(dy=dy):
            for k in range(3):
                tap = 3 * dy + k
                part = dot(tap_rows(source, edges, sizes, tap), w[k * width : (k + 1) * width, :]).reshape(act_two.shape)
                if tap == 0:
                    act_two[...] = part
                else:
                    act_two[...] += part
            if dy == 2:
                put_stats(stats, act_two, act_two)


def k_expand(act, totals, gain, shift, w, hid, stats, *, sizes, rows):
    micros, n, width = act.shape

    @pl.when(pl.program_id(0) == 0)
    def _():
        keep = wide(sizes.row_mask(), width)
        for m in range(micros):
            scale, bias, _, _ = affine(totals, m, gain, shift, rows)
            hid[m] = jnp.where(keep, silu(act[m] * scale + bias), 0.0).astype(BF16)

    out = dot(together(hid), w[...]).reshape(micros, n, -1)
    put_stats(stats, out, out)


def k_pool(hid, w_expand, totals, gain, shift, x, pool, inv_count, w, pooled, head, stats, low, *, rows, steps):
    step = pl.program_id(0)
    micros, own, _ = head.shape
    n = x.shape[1]
    for m in range(micros):
        scale, bias, _, _ = affine(totals, m, gain, shift, rows)
        for part in chunks(n):
            act = dot(hid[m, part, :], w_expand[...])
            low[m, part, :] = silu((act * scale + bias) + x[m, part, :].astype(F32)).astype(BF16)
    low_pooled = (dot(pool[...], together(low)) * inv_count[...]).astype(BF16)
    pooled[...] = low_pooled
    part = dot(low_pooled, w[...])

    @pl.when(step == 0)
    def _():
        for m in range(micros):
            head[m] = part[m * own : (m + 1) * own]

    @pl.when(step > 0)
    def _():
        for m in range(micros):
            head[m] += part[m * own : (m + 1) * own]

    @pl.when(step == steps - 1)
    def _():
        put_stats(stats, head, head)


def head_forward(head, totals, gain, shift, w_embed, count):
    means, inv = norm_terms(totals, count)
    normed = (head - means) * inv
    pre = normed * gain + shift
    hidden = silu(pre).astype(BF16)
    embedding = dot(hidden, w_embed)
    inv_len = lax.rsqrt(jnp.sum(embedding * embedding, axis=1, keepdims=True) + LEN_EPS)
    return normed, pre, inv, hidden, embedding * inv_len, inv_len


def k_embed(where, head, totals, gain, shift, w_embed, pooled, unit_low, *packs_held, count, lines):
    packs, held = packs_held[:-1], packs_held[-1]
    micros, own, width = head.shape
    shard = 4 * lines
    hidden = []
    for m in range(micros):
        _, _, _, hid, unit, _ = head_forward(head[m], totals[m], gain[...], shift[...], w_embed[...], count)
        unit_low[m] = unit.astype(BF16)
        hidden.append(hid.astype(F32))
    both = jnp.concatenate(hidden, axis=0)
    for n in range(4):
        picked = [both[:, s * shard + n * lines : s * shard + (n + 1) * lines] for s in range(width // shard)]
        held[n] = jnp.concatenate(picked, axis=1).astype(BF16)
    chan, sub = pooled.shape[1], held.shape[2]
    for pack, places in zip(packs, ((0,), (1,), (2, 3))):
        pack[:, :chan] = pooled[...]
        for k, place in enumerate(places):
            pack[:, chan + k * sub : chan + (k + 1) * sub] = held[place ^ where[1]]


def k_embed_only(head, totals, gain, shift, w_embed, hidden, unit_low, *, count):
    for m in range(head.shape[0]):
        _, _, _, hid, unit, _ = head_forward(head[m], totals[m], gain[...], shift[...], w_embed[...], count)
        hidden[m] = hid
        unit_low[m] = unit.astype(BF16)


def k_loss(
    units, ids_all, ids_own, pos_all, pos_own, head, totals, gain, shift, w_embed,
    loss, slopes, grad_embed, stats, *, count, loss_scale, block,
):
    everyone = units[0]
    n_all = everyone.shape[0]
    n_own = head.shape[1]

    def terms(start):
        scores = dot_nt(units[0, pl.ds(start, block), :], everyone)
        return jnp.exp2((scores - 1.0) * (TAU_INV * LOG2E))

    if n_all <= 16 * block:
        total = None
        apart = lax.broadcasted_iota(jnp.int32, (block, block), 0) != lax.broadcasted_iota(jnp.int32, (block, block), 1)
        for k in range(n_all // block):
            row = terms(k * block)
            here = slice(k * block, (k + 1) * block)
            pieces = [row[:, : here.start], jnp.where(apart, row[:, here], 0.0), row[:, here.stop :]]
            row = jnp.concatenate([p for p in pieces if p.shape[1]], axis=1)
            row = jnp.sum(row.reshape(block // 8, 8, n_all), axis=0)
            total = row if total is None else total + row
        sums = jnp.sum(total, axis=0, keepdims=True)
    else:

        def add_rows(k, sums):
            start = pl.multiple_of(k * block, block)
            mine = lax.broadcasted_iota(jnp.int32, (block, n_all), 0) + start
            other = lax.broadcasted_iota(jnp.int32, (block, n_all), 1)
            return sums + jnp.sum(jnp.where(mine == other, 0.0, terms(start)), axis=0, keepdims=True)

        sums = lax.fori_loop(0, n_all // block, add_rows, jnp.zeros((1, n_all), F32))
    log_all = jnp.log(sums) + TAU_INV
    normed, pre, inv, hid, unit, inv_len = head_forward(
        head[0], totals[0], gain[...], shift[...], w_embed[...], count
    )
    low = unit.astype(BF16)
    scores = dot_nt(low, everyone) * TAU_INV
    itself = lax.broadcasted_iota(jnp.int32, (n_own, n_all), 0) == lax.broadcasted_iota(
        jnp.int32, (n_own, n_all), 1
    )
    own_sum = jnp.sum(jnp.where(itself, 0.0, jnp.exp(scores - TAU_INV)), axis=1, keepdims=True)
    log_own = jnp.log(own_sum) + TAU_INV
    positive = (ids_own[0] == ids_all[0]) & jnp.logical_not(itself)
    pos_sum = jnp.sum(jnp.where(positive, scores, 0.0), axis=1, keepdims=True)
    loss[0] = log_own - pos_sum * pos_own[0]
    by_row = jnp.where(itself, 0.0, jnp.exp(scores - log_own)) - jnp.where(positive, pos_own[0], 0.0)
    by_col = jnp.where(itself, 0.0, jnp.exp(scores - log_all)) - jnp.where(positive, pos_all[0], 0.0)
    grad_unit = (
        dot((by_row * loss_scale).astype(BF16), everyone)
        + dot((by_col * loss_scale).astype(BF16), everyone)
    ) * TAU_INV
    grad = inv_len * (grad_unit - unit * jnp.sum(unit * grad_unit, axis=1, keepdims=True))
    grad_low = grad.astype(BF16)
    grad_embed[0] = grad_low
    slope = dot_nt(grad_low, w_embed[...]) * (0.5 * twice_slope(pre))
    slopes[0] = slope
    a, b = col_sums(slope, slope * normed)
    stats[0, 0:1, :] = a
    stats[0, 1:2, :] = b


def k_head_back(where, slopes, head, totals, sums, gain, embed, grad, *packs, count):
    micros, own, width = head.shape
    rows = []
    for m in range(micros):
        a, b, c = back_terms(totals, sums, m, gain, count)
        rows.append(slopes[m] * a + head[m] * b + c)
    grad[...] = jnp.concatenate(rows, axis=0).astype(BF16)
    if packs:
        emb = jnp.concatenate([embed[m].astype(F32) for m in range(micros)], axis=0).astype(BF16)
        quarter = width // 4
        for place, pack in enumerate(packs):
            at = pl.multiple_of((place ^ where[1]) * quarter, quarter)
            pack[:, :quarter] = grad[:, pl.ds(at, quarter)]
            pack[:, quarter:] = emb


def k_back_pool(grad_head, hid, w_expand, totals, gain, shift, x, spread, half_count, w, grad_resid, stats, *, rows):
    micros, n, cols = x.shape
    pair = jnp.concatenate(halves(dot_nt(grad_head[...], w[...]) * half_count[...]), axis=0)
    for m in range(micros):
        scale, bias, inv, offset = affine(totals, m, gain, shift, rows)
        sums = None
        for part in chunks(n):
            act = dot(hid[m, part, :], w_expand[...])
            back = dot(spread[m * n + part.start : m * n + part.stop, :], pair)
            slope = back * twice_slope((act * scale + bias) + x[m, part, :].astype(F32))
            grad_resid[m, part, :] = slope.astype(BF16)
            more = col_sums(slope, slope * (act * inv + offset))
            sums = more if sums is None else (sums[0] + more[0], sums[1] + more[1])
        stats[m, 0:1, :] = sums[0]
        stats[m, 1:2, :] = sums[1]


def k_back_expand(
    where, grad_resid, hid, tot_three, sum_three, gain_three, w, act_two, tot_two, gain_two, shift_two,
    slopes, stats, *rest, sizes, rows, steps, shares,
):
    step = pl.program_id(0)
    micros, n, mid = hid.shape
    if shares:
        keep, send, low, turned = rest

        @pl.when(step == 0)
        def _():
            for m in range(micros):
                turned[:, m * n : (m + 1) * n] = hid[m].T

    else:
        (low,) = rest

    @pl.when(step == 0)
    def _():
        slopes[...] = jnp.zeros(slopes.shape, F32)

    for m in range(micros):
        a, b, c = back_terms(tot_three, sum_three, m, gain_three, rows)
        for part in chunks(n):
            act = dot(hid[m, part, :], w[...])
            grad = (grad_resid[m, part, :].astype(F32) * a + (act * b + c)).astype(BF16)
            low[m, part, :] = grad
            slopes[m, part, :] += dot_nt(grad, w[...])

    if shares:
        share = dot(turned[...], together(low)).astype(BF16)
        each = mid // 8
        for out, even in ((keep, 0), (send, 1)):

            @pl.when(step % 2 == even)
            def _(out=out):
                for shard in range(8):
                    place = shard ^ where[0]
                    out[place % 2, place // 2, 0] = share[shard * each : (shard + 1) * each]

    @pl.when(step == steps - 1)
    def _():
        finish_slopes(slopes, stats, act_two, tot_two, gain_two, shift_two, rows, wide(sizes.row_mask(), mid))


def finish_slopes(slopes, stats, act, totals, gain, shift, rows, keep=None):
    for m in range(slopes.shape[0]):
        scale, bias, inv, offset = affine(totals, m, gain, shift, rows)
        slope = slopes[m] * (0.5 * twice_slope(act[m] * scale + bias))
        if keep is not None:
            slope = jnp.where(keep, slope, 0.0)
        slopes[m] = slope
        a, b = col_sums(slope, slope * (act[m] * inv + offset))
        stats[m, 0:1, :] = a
        stats[m, 1:2, :] = b


UNIT = 64
UNITS_A = 5


def k_back_spatial(
    where, slopes, act_two, tot_two, sum_two, gain_two, w, act_one, tot_one, gain_one, shift_one, hid,
    slopes_one, stats, *rest, sizes, rows, shares,
):
    if shares:
        keep_a, send_a, keep_b, send_b, source, edges, turned, block = rest
        core, line = where[1] % 2, where[1] // 2
    else:
        grad_two, source, edges = rest
    step = pl.program_id(0)
    micros, n, mid = act_two.shape

    @pl.when(step == 0)
    def _():
        set_source(source, edges, sizes)
        for m in range(micros):
            a, b, c = back_terms(tot_two, sum_two, m, gain_two, rows)
            low = (slopes[m] * a + (act_two[m] * b + c)).astype(BF16)
            source[m, PAD : PAD + sizes.rows, :] = low.astype(F32)
            if shares:
                turned[:, m * n : (m + 1) * n] = hid[m].T
            else:
                grad_two[m] = low

    def share(tap, here):
        part = dot(turned[...], here)
        for q in range(4):
            block[q] = part[:, 128 * q : 128 * (q + 1)].astype(BF16)
        for unit in range(8 * (8 - tap), 8 * (9 - tap)):
            shard, k = divmod(unit, 9)
            place = shard ^ where[0]
            lines = slice(UNIT * (unit % 8), UNIT * (unit % 8 + 1))
            for y in range(2):
                for out_a, out_b, c in ((keep_a, keep_b, core), (send_a, send_b, 1 - core)):
                    piece = block[2 * y + c, lines, :]
                    if k < UNITS_A:
                        out_a[place % 2, place // 2, y ^ line, k * UNIT : (k + 1) * UNIT, :] = piece
                    else:
                        at = (k - UNITS_A) * UNIT
                        out_b[y ^ line, place % 2, place // 2, at : at + UNIT, :] = piece

    for dy in range(3):

        @pl.when(step == dy)
        def _(dy=dy):
            for k in range(3):
                tap = 3 * dy + k
                here = tap_rows(source, edges, sizes, tap)
                part = dot_nt(here, w[(2 - k) * mid : (3 - k) * mid, :]).reshape(slopes_one.shape)
                if tap == 0:
                    slopes_one[...] = part
                else:
                    slopes_one[...] += part
                if shares:
                    share(tap, here)
            if dy == 2:
                finish_slopes(slopes_one, stats, act_one, tot_one, gain_one, shift_one, rows)


def k_weight_hidden(where, *refs):
    rows, packs = refs[:4], refs[4:8]
    subs = refs[8:12]
    keep, send, grads, extra, held = refs[12:]
    step = pl.program_id(0)
    quarter = keep.shape[2]

    @pl.when(step == 0)
    def _():
        total = None
        for k in range(4):
            n = packs[k].shape[0]
            grads[k * n : (k + 1) * n, :] = packs[k][:, :quarter].astype(F32)
            part = dot_tn(subs[k][...], packs[k][:, quarter:])
            total = part if total is None else total + part
        extra[...] = total.astype(BF16).reshape(extra.shape)

    pooled = jnp.concatenate([r[...].astype(F32) for r in rows], axis=0).astype(BF16)
    held[...] = dot_tn(pooled, grads[...].astype(BF16)).astype(BF16).reshape(held.shape)
    shard = held.shape[1]
    for x, ref in ((0, keep), (1, send)):
        more = extra[(2 * step + x) ^ where[0]]
        lines = more.shape[0] // 4
        ref[0, :shard, :] = held[x ^ (where[0] % 2)]
        for k in range(4):
            ref[0, shard:, 128 * k : 128 * (k + 1)] = more[lines * k : lines * (k + 1), :]


def k_weight_reduce(
    where, x, slopes, act, totals, sums, gain, grad, keep, send, turned, block, *, rows
):
    micros, n, mid = slopes.shape
    core, line = where[1] % 2, where[1] // 2

    @pl.when(pl.program_id(0) == 0)
    def _():
        for m in range(micros):
            a, b, c = back_terms(totals, sums, m, gain, rows)
            low = (slopes[m] * a + (act[m] * b + c)).astype(BF16)
            grad[m] = low
            turned[:, m * n : (m + 1) * n] = low.T

    total = dot(turned[...], together(x)).astype(BF16).T
    for q in range(4):
        block[q] = total[:, 128 * q : 128 * (q + 1)]
    for y in range(2):
        for out, c in ((keep, core), (send, 1 - core)):
            out[0, 0, y ^ line] = block[2 * y + c]


def k_grad_one(slopes, act, totals, sums, gain, grad, *, rows):
    for m in range(slopes.shape[0]):
        a, b, c = back_terms(totals, sums, m, gain, rows)
        grad[m] = (slopes[m] * a + (act[m] * b + c)).astype(BF16)


def k_back_reduce(grad_one, w, grad_resid, *refs, sizes):
    grad_v, grad_c = refs[-2:]
    views, lines, _ = grad_v.shape
    micros = grad_one.shape[0]
    flat = grad_v.reshape(views * lines, 128)
    at = sizes.crop_at
    n = sizes.rows
    back = dot_nt(together(grad_one), w[...])
    for m in range(micros):
        both = grad_resid[m].astype(F32) + back[m * n : (m + 1) * n]
        grad_c[m] = both[at : at + sizes.crops]
        for t in range(lines // micros):
            flat[pl.ds(micros * t + m, views, stride=lines), :] = both[:views, 128 * t : 128 * (t + 1)]


def call(kernel, name, grid, ins, outs, scratch=(), flops=0, vmem=56, where=None, aliases=None):
    spec = lambda block, index: pl.BlockSpec(block, index) if block else pl.BlockSpec(memory_space=pl.ANY)
    scalars = [] if where is None else [where]
    moved = sum(a.size * a.dtype.itemsize for a, _, _ in ins) + sum(
        math.prod(s) * jnp.dtype(t).itemsize for s, t, _, _ in outs
    )
    return pl.pallas_call(
        kernel,
        grid_spec=pltpu.PrefetchScalarGridSpec(
            num_scalar_prefetch=len(scalars),
            grid=grid,
            in_specs=[spec(b, i) for _, b, i in ins],
            out_specs=[spec(b, i) for _, _, b, i in outs],
            scratch_shapes=list(scratch),
        ),
        out_shape=[jax.ShapeDtypeStruct(s, t) for s, t, _, _ in outs],
        compiler_params=pltpu.CompilerParams(vmem_limit_bytes=vmem * MIB),
        cost_estimate=pl.CostEstimate(flops=1000, bytes_accessed=1000, transcendentals=0),
        name=name,
        input_output_aliases=aliases or {},
    )(*scalars, *[a for a, _, _ in ins])


def exact(array):
    return lax.optimization_barrier(array)


def add_low(*parts):
    total = parts[0].astype(F32)
    for part in parts[1:]:
        total = total + part.astype(F32)
    return total.astype(BF16)


def reduce_weight(grad, count, data_size, narrow_size):
    rows, cols = grad.shape
    me = lax.axis_index("dp")
    core = lax.axis_index("narrow") % 2
    blocks = grad.reshape(data_size, rows // data_size, cols)
    blocks = jnp.stack(
        [lax.dynamic_index_in_dim(blocks, me ^ j, axis=0, keepdims=False) for j in range(data_size)]
    )
    half = cols // 2
    low, high = blocks[:, :, :half], blocks[:, :, half:]
    keep = jnp.where(core == 0, low, high)
    send = jnp.where(core == 0, high, low)
    part = add_low(keep, xor_permute(send, 1, count))
    size = data_size
    for stage in bit_stages(0, data_size.bit_length() - 1):
        if len(stage) == 1:
            split = part.reshape((size // 2, 2) + part.shape[1:])
            part = add_low(split[:, 0], xor_permute(split[:, 1], stage[0] * narrow_size, count))
            size //= 2
        else:
            split = part.reshape((size // 4, 4) + part.shape[1:])
            got = [
                xor_permute(split[:, k], off * narrow_size, count)
                for k, off in ((1, stage[0]), (2, stage[1]), (3, stage[0] ^ stage[1]))
            ]
            part = add_low(split[:, 0], *got)
            size //= 4
    part = exact(part[0])
    off = 2
    while off < narrow_size:
        part = exact(add_low(part, xor_permute(part, off, count)))
        off *= 2
    other = xor_permute(part, 1, count)
    both = jnp.where(
        core == 0, jnp.concatenate([part, other], axis=1), jnp.concatenate([other, part], axis=1)
    )
    return both.astype(F32)


class Mesh84:
    core, line, x, z = 1, 2, 4, 8

    def __init__(self, count):
        self.count = count

    def send(self, array, offset):
        return xor_permute(array, offset, self.count)

    def split(self, keep, got):
        return [add_low(keep[k], got[k]) for k in range(keep.shape[0])]

    def across_z(self, parts, *others):
        sent = [after(p, *others) if others else p for p in parts[1:]]
        return [parts[0]] + [self.send(sent[k - 1], self.z * k) for k in (1, 2, 3)]

    def quarters(self, near, far, narrow):
        places = (near[0], far[0], near[1], far[1])
        pick = lambda q: lax.select_n(narrow, *(places[q ^ n] for n in range(4)))
        return jnp.concatenate([pick(q) for q in range(4)], axis=-1)


def after(value, *others):
    return lax.optimization_barrier((value, *others))[0]


def hidden_share(rows, packs, where):
    total, wide_cols = rows[0].shape
    chan = wide_cols * 4 // 5
    sub = wide_cols - chan
    emb = packs[0].shape[1] - sub
    shard = chan // 8
    extra = sub // 8 * emb // sub
    fix = lambda i, w: (0, 0)
    out = ((4, shard + extra, sub), BF16, (1, shard + extra, sub), lambda i, w: (i, 0, 0))
    return call(
        k_weight_hidden, "weight_hidden", (4,),
        [(r, (total, 2 * shard), lambda i, w: (0, i ^ (w[0] // 2))) for r in rows]
        + [(p, p.shape, fix) for p in packs]
        + [(r, (total, sub), lambda i, w: (0, chan // sub)) for r in rows],
        [out, out],
        scratch=[
            pltpu.VMEM((4 * total, sub), F32),
            pltpu.VMEM((8, sub // 8, emb), BF16),
            pltpu.VMEM((2, shard, sub), BF16),
        ],
        flops=8 * total * chan * sub,
        where=where,
    )


def spread_taps(hidden, side):
    padded = jnp.pad(hidden, ((0, 0), (1, 1), (1, 1), (0, 0)))
    pieces = [padded[:, dy : dy + side, dx : dx + side, :] for dy in range(3) for dx in range(3)]
    return jnp.concatenate(pieces, axis=-1)


def body(
    view_maps, crop_maps, image_ids, w_reduce, gain_one, shift_one, w_spatial, gain_two, shift_two,
    w_expand, gain_three, shift_three, w_hidden, gain_head, shift_head, w_embed,
):
    micros, view_rows, channels = view_maps.shape
    crop_rows = crop_maps.shape[1]
    mid = w_reduce.shape[1]
    hidden_width = w_hidden.shape[1]
    emb_width = w_embed.shape[1]
    images_dev = view_rows // (VIEWS * VSIDE * VSIDE)
    each = VIEWS + CROPS
    own = images_dev * each
    data_size, narrow_size = lax.axis_size("dp"), lax.axis_size("narrow")
    count = data_size * narrow_size
    emb_total = own * count
    pixel_count = (view_rows + crop_rows) * count
    loss_scale = 1.0 / (micros * emb_total)
    device = lax.axis_index("dp") * narrow_size + lax.axis_index("narrow")
    sizes = Sizes(view_rows, crop_rows)
    rows = sizes.rows

    pool = np.zeros((micros, own, micros, rows), np.float32)
    for m in range(micros):
        for r in range(view_rows):
            image, view = divmod(r // (VSIDE * VSIDE), VIEWS)
            pool[m, image * each + view, m, r] = 1
        for r in range(crop_rows):
            image, crop = divmod(r // (CSIDE * CSIDE), CROPS)
            pool[m, image * each + VIEWS + crop, m, sizes.crop_at + r] = 1
    pool = pool.reshape(micros * own, micros * rows)
    inv_count = np.where(np.arange(micros * own) % each < VIEWS, 1.0 / VSIDE**2, 1.0 / CSIDE**2)[:, None]
    spread = jnp.asarray(np.concatenate([pool.T, pool.T], axis=1), BF16)
    pool = jnp.asarray(pool, BF16)
    half_count = jnp.asarray(0.5 * inv_count, F32)
    inv_count = jnp.asarray(inv_count, F32)

    place = jnp.asarray(gather_order(count)) ^ device
    same = jnp.sum((image_ids[:, :, None] == image_ids[:, None, :]).astype(F32), axis=2)
    inv_pos = 1.0 / (same * each - 1.0)

    from_device = place[:, None] == jnp.arange(count, dtype=jnp.int32)[None, :]

    def by_place(values):
        blocks = values.reshape(micros, 1, count, images_dev)
        moved = jnp.sum(jnp.where(from_device[None, :, :, None], blocks, 0), axis=2)
        return jnp.repeat(moved.reshape(micros, -1), each, axis=1)

    ids_all, pos_all = by_place(image_ids), by_place(inv_pos)
    ids_own, pos_own = ids_all[:, :own, None], pos_all[:, :own, None]
    ids_all, pos_all = ids_all[:, None, :], pos_all[:, None, :]

    row = lambda v: v.reshape(1, -1)
    g1, b1, g2, b2 = row(gain_one), row(shift_one), row(gain_two), row(shift_two)
    g3, b3, gh, bh = row(gain_three), row(shift_three), row(gain_head), row(shift_head)
    reduce_all = lambda stats: all_sum(stats, count)
    flops = 2.0 * micros * rows * channels * mid

    fast = data_size == 8 and narrow_size == 4 and mid == 512 and micros == 2
    dp, narrow = lax.axis_index("dp"), lax.axis_index("narrow")
    where = jnp.stack([dp, narrow]).astype(jnp.int32)
    net = Mesh84(count)
    blk = 512
    steps = channels // blk
    fix2 = lambda *_: (0, 0)
    fix3 = lambda *_: (0, 0, 0)
    col = lambda n, *_: (0, n)
    col3 = lambda n, *_: (0, 0, n)
    row = lambda n, *_: (n, 0)
    m0 = lambda m, *_: (m, 0, 0)
    act_mid = (micros, rows, mid)
    two = lambda array: (array, array.shape, fix3)
    vec = lambda array: (array, array.shape, fix2)
    vec_block = lambda array: (array, (1, blk), col)
    tot_block = lambda array: (array, (micros, 2, blk), col3)
    stats_of = lambda width: ((micros, 2, width), F32, (micros, 2, width), fix3)

    tiles = channels // 128
    mixed = jnp.transpose(view_maps.reshape(micros, view_rows, tiles, 128), (1, 2, 0, 3))
    mixed = mixed.reshape(view_rows, micros * tiles, 128)
    lines = micros * blk // 128
    pixels, act_one, st = call(
        functools.partial(k_reduce, sizes=sizes, steps=steps), "reduce", (steps,),
        [
            (mixed, (view_rows, lines, 128), lambda n: (0, n, 0)),
            (crop_maps, (micros, crop_rows, blk), col3),
            (w_reduce, (blk, mid), row),
        ],
        [
            ((micros, rows, channels), BF16, (micros, rows, blk), col3),
            (act_mid, F32, act_mid, fix3),
            stats_of(mid),
        ],
        scratch=[pltpu.VMEM((view_rows * lines, 128), F32)],
        flops=flops,
    )
    tot_one = reduce_all(st)
    taps_scratch = [
        pltpu.VMEM((micros, rows + 2 * PAD, mid), F32),
        pltpu.VMEM((5, rows, 128), F32),
    ]
    hid_one, act_two, st = call(
        functools.partial(k_spatial, sizes=sizes, rows=pixel_count), "spatial", (3,),
        [two(act_one), two(tot_one), vec(g1), vec(b1), (w_spatial, (3 * mid, mid), row)],
        [(act_mid, BF16, act_mid, fix3), (act_mid, F32, act_mid, fix3), stats_of(mid)],
        scratch=taps_scratch,
        flops=flops * 9 * mid / channels,
    )
    tot_two = reduce_all(st)
    hid_two, st = call(
        functools.partial(k_expand, sizes=sizes, rows=pixel_count), "expand", (steps,),
        [two(act_two), two(tot_two), vec(g2), vec(b2), (w_expand, (mid, blk), col)],
        [(act_mid, BF16, act_mid, fix3), ((micros, 2, channels), F32, (micros, 2, blk), col3)],
        flops=flops,
    )
    tot_three = reduce_all(st)
    flat_own = micros * own
    pooled, head, st = call(
        functools.partial(k_pool, rows=pixel_count, steps=steps), "pool", (steps,),
        [
            two(hid_two),
            (w_expand, (mid, blk), col),
            tot_block(tot_three),
            vec_block(g3),
            vec_block(b3),
            (pixels, (micros, rows, blk), col3),
            vec(pool),
            vec(inv_count),
            (w_hidden, (blk, hidden_width), row),
        ],
        [
            ((flat_own, channels), BF16, (flat_own, blk), col),
            ((micros, own, hidden_width), F32, (micros, own, hidden_width), fix3),
            stats_of(hidden_width),
        ],
        scratch=[pltpu.VMEM((micros, rows, blk), BF16)],
        flops=flops,
    )
    tot_head = reduce_all(st)
    head_in = [two(head), two(tot_head), vec(gh), vec(bh), vec(w_embed)]
    unit_shape = (micros, own, emb_width)
    if fast:
        sub = hidden_width // 4
        pack = (flat_own, channels + sub)
        unit_low, *rows_packs = call(
            functools.partial(k_embed, count=emb_total, lines=sub // 8), "embed", (1,), head_in + [vec(pooled)],
            [(unit_shape, BF16, unit_shape, fix3)] + [(pack, BF16, pack, fix2)] * 2
            + [((flat_own, channels + 2 * sub), BF16, (flat_own, channels + 2 * sub), fix2)],
            scratch=[pltpu.VMEM((4, flat_own, sub), BF16)],
            where=where,
        )
    else:
        head_hid, unit_low = call(
            functools.partial(k_embed_only, count=emb_total), "embed", (1,), head_in,
            [
                ((micros, own, hidden_width), BF16, (micros, own, hidden_width), fix3),
                (unit_shape, BF16, unit_shape, fix3),
            ],
        )
    units = gather_all(unit_low, count)
    units = jnp.transpose(units, (1, 0, 2, 3)).reshape(micros, emb_total, emb_width)
    if fast:
        pack_own, pack_core, pack_line = (after(p, units) for p in rows_packs)
        got_core = net.send(pack_core, net.core)
        got_line = net.send(pack_line, net.line)
    loss, slopes, grad_embed, st = call(
        functools.partial(k_loss, count=emb_total, loss_scale=loss_scale, block=128), "loss", (micros,),
        [
            (units, (1, emb_total, emb_width), m0),
            (ids_all, (1, 1, emb_total), m0),
            (ids_own, (1, own, 1), m0),
            (pos_all, (1, 1, emb_total), m0),
            (pos_own, (1, own, 1), m0),
            (head, (1, own, hidden_width), m0),
            (tot_head, (1, 2, hidden_width), m0),
            vec(gh),
            vec(bh),
            vec(w_embed),
        ],
        [
            ((micros, own, 1), F32, (1, own, 1), m0),
            ((micros, own, hidden_width), F32, (1, own, hidden_width), m0),
            (unit_shape, BF16, (1, own, emb_width), m0),
            ((micros, 2, hidden_width), F32, (1, 2, hidden_width), m0),
        ],
    )
    if fast:
        got_core, got_line = (after(g, st) for g in (got_core, got_line))
        st = after(st, got_line)
        wide_cols = channels + sub
        pass_on = jnp.concatenate([got_line[:, :channels], got_line[:, wide_cols:]], axis=1)
        rows_packs = [pack_own, got_core, got_line[:, :wide_cols], net.send(pass_on, net.core)]
    sum_head = reduce_all(st)

    grad_head, *packs = call(
        functools.partial(k_head_back, count=emb_total), "head_back", (1,),
        [two(slopes), two(head), two(tot_head), two(sum_head), vec(gh), two(grad_embed)],
        [((flat_own, hidden_width), BF16, (flat_own, hidden_width), fix2)]
        + [((flat_own, hidden_width // 4 + emb_width), BF16, (flat_own, hidden_width // 4 + emb_width), fix2)]
        * (4 if fast else 0),
        where=where,
    )
    if fast:
        packs = packs[:1] + [net.send(packs[k], k) for k in (1, 2, 3)]
    grad_resid, st = call(
        functools.partial(k_back_pool, rows=pixel_count), "back_pool", (steps,),
        [
            vec(grad_head),
            two(hid_two),
            (w_expand, (mid, blk), col),
            tot_block(tot_three),
            vec_block(g3),
            vec_block(b3),
            (pixels, (micros, rows, blk), col3),
            vec(spread),
            vec(half_count),
            (w_hidden, (blk, hidden_width), row),
        ],
        [
            ((micros, rows, channels), BF16, (micros, rows, blk), col3),
            ((micros, 2, channels), F32, (micros, 2, blk), col3),
        ],
        flops=flops,
    )
    if fast:
        packs = packs[:1] + [after(g, st) for g in packs[1:]]
        wh_keep, wh_send = hidden_share(rows_packs, packs, where)
    sum_three = reduce_all(st)
    if fast:
        wh_got = net.send(after(wh_send, sum_three), net.x)
        grad_resid = after(grad_resid, wh_send, wh_keep)
    turn = (lambda n, w: n ^ w[1]) if fast else (lambda n, w: n)
    turn3 = lambda n, w: (0, 0, turn(n, w))
    turn2 = lambda n, w: (0, turn(n, w))
    w3_share = (2, 4, 2, mid // 8, blk)
    w3_out = (w3_share, BF16, (2, 4, 1, mid // 8, blk), lambda n, w: (0, 0, n // 2, 0, 0))
    slopes_two, st, *rest = call(
        functools.partial(k_back_expand, sizes=sizes, rows=pixel_count, steps=steps, shares=fast), "back_expand", (steps,),
        [
            (grad_resid, (micros, rows, blk), turn3),
            two(hid_two),
            (tot_three, (micros, 2, blk), turn3),
            (sum_three, (micros, 2, blk), turn3),
            (g3, (1, blk), turn2),
            (w_expand, (mid, blk), turn2),
            two(act_two),
            two(tot_two),
            vec(g2),
            vec(b2),
        ],
        [(act_mid, F32, act_mid, fix3), stats_of(mid)]
        + ([w3_out, w3_out] if fast else [((micros, rows, channels), BF16, (micros, rows, blk), turn3)]),
        scratch=[pltpu.VMEM((micros, rows, blk), BF16), pltpu.VMEM((mid, micros * rows), BF16)] if fast else [],
        flops=2 * flops,
        where=where,
    )
    if fast:
        w3_keep, w3_send = rest
        w3_got = net.send(w3_send, net.core)
        wh_z = net.split(wh_keep, after(wh_got, st, w3_send))
        w3_x = net.split(w3_keep, w3_got)
        st = after(st, wh_got)
    else:
        (w3_full,) = rest
    sum_two = reduce_all(st)
    if fast:
        wh_got = net.across_z(wh_z, sum_two)
        w3_got = net.send(after(w3_x[1], sum_two), net.x)
        slopes_two = after(slopes_two, *wh_z, *w3_x)
    shapes = [(2, 4, 2, UNITS_A * UNIT, 128)] * 2 + [(2, 2, 4, (9 - UNITS_A) * UNIT, 128)] * 2
    slopes_one, st, *rest = call(
        functools.partial(k_back_spatial, sizes=sizes, rows=pixel_count, shares=fast), "back_spatial", (3,),
        [
            two(slopes_two),
            two(act_two),
            two(tot_two),
            two(sum_two),
            vec(g2),
            (w_spatial, (3 * mid, mid), lambda n, *_: (2 - n, 0)),
            two(act_one),
            two(tot_one),
            vec(g1),
            vec(b1),
            two(hid_one),
        ],
        [(act_mid, F32, act_mid, fix3), stats_of(mid)]
        + ([(t, BF16, t, lambda *_: (0,) * 5) for t in shapes] if fast else [(act_mid, BF16, act_mid, fix3)]),
        scratch=taps_scratch
        + ([pltpu.VMEM((mid, micros * rows), BF16), pltpu.VMEM((4, mid, 128), BF16)] if fast else []),
        flops=2 * flops * 9 * mid / channels,
        where=where,
    )
    if fast:
        w2_keep_a, w2_send_a, w2_keep_b, w2_send_b = rest
        wh_part = exact(add_low(*(after(g, st) for g in wh_got)))
        w3_z = net.split(w3_x[0], after(w3_got, st))
        st = after(st, *wh_got, w3_got)
        first = []
        sum_one = all_sum(st, count, first.append)
        w2_got_a, w2_got_b = (net.send(after(g, *first), net.core) for g in (w2_send_a, w2_send_b))
        w2_x = net.split(w2_keep_a, w2_got_a)
        w2_y = net.split(w2_keep_b, w2_got_b)
        w2_got_a = net.send(after(w2_x[1], sum_one), net.x)
        w2_got_b = net.send(after(w2_y[1], sum_one), net.line)
        w3_got = net.across_z(w3_z, sum_one)
    else:
        sum_one = reduce_all(st)
    one_in = [two(slopes_one), two(act_one), two(tot_one), two(sum_one), vec(g1)]
    if fast:
        one_in[0] = two(after(slopes_one, *w3_z, *w2_x, *w2_y, wh_part))
        shard = channels // 8
        out = ((2, 4, 2, shard, 128), BF16, (1, 1, 2, shard, 128), lambda j, w: (j % 2, j // 2, 0, 0, 0))
        grad_one, w1_keep, w1_send = call(
            functools.partial(k_weight_reduce, rows=pixel_count), "weight_reduce", (8,),
            [(pixels, (micros, rows, shard), lambda j, w: (0, 0, j ^ w[0]))] + one_in,
            [(act_mid, BF16, act_mid, fix3), out, out],
            scratch=[pltpu.VMEM((mid, micros * rows), BF16), pltpu.VMEM((4, shard, 128), BF16)],
            flops=flops,
            where=where,
        )
        w1_got = net.send(w1_send, net.core)
        w2_got_a, w2_got_b, *w3_got, _ = exact((w2_got_a, w2_got_b, *w3_got, w1_send))
        w2_z = net.split(w2_x[0], w2_got_a)
        w2_x = net.split(w2_y[0], w2_got_b)
        w3_part = exact(add_low(*w3_got))
        w2_got_a = net.across_z(w2_z)
        w2_got_b = net.send(w2_x[1], net.x)
        w3_line = net.send(w3_part, net.line)
        grad_one = after(grad_one, *w2_z, *w2_x, w3_part)
    else:
        (grad_one,) = call(
            functools.partial(k_grad_one, rows=pixel_count), "grad_one", (1,), one_in, [(act_mid, BF16, act_mid, fix3)]
        )
    def back_reduce(first, grads, before=()):
        at = lambda n: n + first
        return call(
            functools.partial(k_back_reduce, sizes=sizes), "back_reduce", (steps // 2,),
            [
                two(grads),
                (w_reduce, (blk, mid), lambda n: (at(n), 0)),
                (grad_resid, (micros, rows, blk), lambda n: (0, 0, at(n))),
            ]
            + [(b, None, None) for b in before],
            [
                ((view_rows, micros * tiles, 128), F32, (view_rows, lines, 128), lambda n: (0, at(n), 0)),
                (crop_maps.shape, F32, (micros, crop_rows, blk), lambda n: (0, 0, at(n))),
            ],
            flops=flops / 2,
            aliases={3 + k: k for k in range(len(before))},
        )

    grad_views, grad_crops = back_reduce(0, grad_one)
    if fast:
        w1_got, w2_got_b, w3_line, *w2_got_a, grad_crops = exact((w1_got, w2_got_b, w3_line, *w2_got_a, grad_crops))
        w1_x = net.split(w1_keep, w1_got)
        w1_got = net.send(w1_x[1], net.x)
        w2_bz = net.split(w2_x[0], w2_got_b)
        w2_got_b = net.across_z(w2_bz)
        w2_a = exact(add_low(*w2_got_a))
        w2_got_a = net.send(w2_a, net.line)
        w3_part = exact(add_low(w3_part, w3_line[::-1]))
        w3_far = net.send(w3_part, net.core)
        wh_line = net.send(after(wh_part, grad_crops), net.line)
        grad_one = after(grad_one, *w1_x, *w2_bz, w2_a, w3_part)
    grad_views, grad_crops = back_reduce(steps // 2, grad_one, (grad_views, grad_crops))
    grad_views = jnp.transpose(grad_views.reshape(view_rows, tiles, micros, 128), (2, 0, 1, 3)).reshape(view_maps.shape)

    if fast:
        w1_got, w2_got_a, wh_line, w3_far, *w2_got_b, grad_crops = exact(
            (w1_got, w2_got_a, wh_line, w3_far, *w2_got_b, grad_crops)
        )
        w1_got = net.across_z(net.split(w1_x[0], w1_got))
        w2_b = exact(add_low(*w2_got_b))
        w2_a = exact(add_low(w2_a, w2_got_a[::-1]))
        wh_pair = jnp.stack([wh_part, wh_line])
        arrived = exact((*w1_got, net.send(w2_b, net.line), net.send(w2_a, net.core), net.send(wh_pair, net.core)))
        w1_part = exact(add_low(*arrived[:4]))
        w2_pair = jnp.stack([w2_b, arrived[4]])
        w2_a_far, wh_far = arrived[5:]
        w1_line, w2_b_far = exact((net.send(w1_part, net.line), net.send(w2_pair, net.core)))
        w1_part = exact(add_low(w1_part, w1_line[::-1]))
        w1_far = net.send(w1_part, net.core)
        lines = w_hidden.shape[0] // data_size
        gw_hidden = net.quarters(wh_pair[:, :lines], wh_far[:, :lines], narrow).astype(F32)
        extra = net.quarters(wh_pair[:, lines:], wh_far[:, lines:], narrow)
        extra = extra.reshape(-1, 4, 4, emb_width)
        gw_embed = jnp.transpose(extra, (1, 2, 0, 3)).reshape(-1, emb_width).astype(F32)
        gw_expand = net.quarters(w3_part, w3_far, narrow).astype(F32)
        w2 = [net.quarters(w2_a, w2_a_far, narrow), net.quarters(w2_pair, w2_b_far, narrow)]
        gw_spatial = jnp.concatenate(w2, axis=0).astype(F32)
        gw_reduce = net.quarters(w1_part, w1_far, narrow).astype(F32)
    else:
        over = lambda a, b: jnp.einsum("mri,mrj->ij", a, b, preferred_element_type=F32)
        reduce_w = lambda g: reduce_weight(g.astype(BF16), count, data_size, narrow_size)
        gw_embed = reduce_w(over(head_hid, grad_embed))
        gw_hidden = reduce_w(jnp.dot(pooled.T, grad_head, preferred_element_type=F32))
        gw_expand = reduce_w(over(hid_two, w3_full))
        at = sizes.crop_at
        real = lambda t: (t[:, :view_rows], t[:, at : at + crop_rows])
        cols = [
            spread_taps(part.reshape(-1, side, side, mid), side).reshape(micros, -1, 9, mid)
            for part, side in zip(real(rest[0]), (VSIDE, CSIDE))
        ]
        by_tap = jnp.einsum(
            "mri,mrtj->tij", jnp.concatenate(real(hid_one), axis=1), jnp.concatenate(cols, axis=1),
            preferred_element_type=F32,
        )[::-1]
        gw_spatial = reduce_w(by_tap.reshape(9 * mid, mid))
        gw_reduce = reduce_w(over(pixels, grad_one))
    gain_grad = lambda sums: jnp.sum(sums[:, 1], axis=0)
    shift_grad = lambda sums: jnp.sum(sums[:, 0], axis=0)
    return (
        loss.reshape(micros, own), grad_views, grad_crops,
        gw_reduce, gain_grad(sum_one), shift_grad(sum_one),
        gw_spatial, gain_grad(sum_two), shift_grad(sum_two),
        gw_expand, gain_grad(sum_three), shift_grad(sum_three),
        gw_hidden, gain_grad(sum_head), shift_grad(sum_head),
        gw_embed,
    )


def solution(mesh):
    rows = P(None, BOTH, None)
    return jax.shard_map(
        body,
        mesh=mesh,
        in_specs=(rows, rows) + (P(),) * 14,
        out_specs=(
            P(None, BOTH), rows, rows,
            P("dp", None), P(), P(),
            P("dp", None), P(), P(),
            P("dp", None), P(), P(),
            P("dp", None), P(), P(),
            P("dp", None),
        ),
        check_vma=False,
    )
```

```python
import functools
import math

import jax
import jax.numpy as jnp
import numpy as np
from jax import lax
from jax.experimental import pallas as pl
from jax.experimental.pallas import tpu as pltpu
from jax.sharding import PartitionSpec as P

VIEWS = 2
CROPS = 4
VSIDE = 7
CSIDE = 3
TAU_INV = 10.0
LOG2E = math.log2(math.e)
EPS = 1e-05
LEN_EPS = 1e-06
BOTH = ("dp", "narrow")
F32 = jnp.float32
BF16 = jnp.bfloat16
MIB = 1 << 20


def round_up(value, step):
    return -(-value // step) * step


def xor_permute(array, offset, count):
    return lax.ppermute(array, BOTH, [(i, i ^ offset) for i in range(count)])


def bit_stages(first, last):
    bits = [1 << b for b in range(first, last)]
    stages = [bits[:1]] if bits else []
    rest = bits[1:]
    while rest:
        stages.append(rest[:2])
        rest = rest[2:]
    return stages


def all_sum(array, count, begun=None):
    for stage in bit_stages(0, count.bit_length() - 1):
        if len(stage) == 1:
            array = array + xor_permute(array, stage[0], count)
            if begun is not None:
                begun(array)
                begun = None
        else:
            low, high = stage
            near = xor_permute(array, low, count)
            far = xor_permute(array, high, count)
            across = xor_permute(array, low ^ high, count)
            array = (array + near) + (far + across)
    return array


def gather_all(array, count):
    parts = [array]
    stages = bit_stages(0, count.bit_length() - 1)
    for stage in stages[:0:-1] + stages[:1]:
        offsets = stage if len(stage) == 1 else [stage[0], stage[1], stage[0] ^ stage[1]]
        block = jnp.stack(parts) if len(parts) > 1 else parts[0][None]
        arrived = [xor_permute(block, off, count) for off in offsets]
        parts = [p for p in parts]
        for got in arrived:
            parts.extend(got[k] for k in range(got.shape[0]))
    return jnp.stack(parts)


def gather_order(count):
    order = [0]
    stages = bit_stages(0, count.bit_length() - 1)
    for stage in stages[:0:-1] + stages[:1]:
        offsets = stage if len(stage) == 1 else [stage[0], stage[1], stage[0] ^ stage[1]]
        order = order + [o ^ off for off in offsets for o in order]
    return np.array(order, np.int32)


def dot(left, right):
    return jnp.dot(left, right, preferred_element_type=F32)


def dot_tn(left, right):
    return lax.dot_general(left, right, (((0,), (0,)), ((), ())), preferred_element_type=F32)


def dot_nt(left, right):
    return lax.dot_general(left, right, (((1,), (1,)), ((), ())), preferred_element_type=F32)


def norm_terms(totals, rows):
    means = totals[0:1] / rows
    variance = totals[1:2] / rows - means * means
    return means, lax.rsqrt(variance + EPS)


def halves(values):
    high = values.astype(BF16)
    return high, (values - high.astype(F32)).astype(BF16)


def col_sums(first, second):
    return jnp.sum(first, axis=0, keepdims=True), jnp.sum(second, axis=0, keepdims=True)


class Sizes:
    def __init__(self, view_rows, crop_rows):
        self.views, self.crops = view_rows, crop_rows
        self.crop_at = round_up(view_rows, 16)
        self.rows = self.crop_at + round_up(crop_rows, 16)

    def row_mask(self):
        row = lax.broadcasted_iota(jnp.int32, (self.rows, 128), 0)
        inside = (row < self.views) | ((row >= self.crop_at) & (row < self.crop_at + self.crops))
        return inside


def wide(mask, cols):
    return jnp.concatenate([mask] * (cols // 128), axis=1)


def fill_edges(edges_ref, sizes):
    for start, stop, at, side in (
        (0, sizes.crop_at, sizes.views, VSIDE),
        (sizes.crop_at, sizes.rows, sizes.crop_at + sizes.crops, CSIDE),
    ):
        count = stop - start
        row = lax.broadcasted_iota(jnp.int32, (count, 128), 0)
        real = row < (at - start)
        rowf = row.astype(F32) + 0.5
        line = jnp.floor(rowf * (1.0 / side))
        col = rowf - 0.5 - line * side
        in_map = line - jnp.floor((line + 0.5) * (1.0 / side)) * side
        keep = (col > 0.5, col < side - 1.5, in_map > 0.5, in_map < side - 1.5)
        for k in range(4):
            edges_ref[k, start:stop, :] = jnp.where(real & keep[k], 1.0, 0.0)
        edges_ref[4, start:stop, :] = jnp.where(real, 1.0, 0.0)


PAD = 16


def tap_block(source_ref, edges_ref, sizes, tap, width):
    dy, dx = tap // 3 - 1, tap % 3 - 1
    pieces = []
    for start, stop, side in ((0, sizes.crop_at, VSIDE), (sizes.crop_at, sizes.rows, CSIDE)):
        shift = dy * side + dx
        values = source_ref[PAD + start + shift : PAD + stop + shift, :]
        mask = None
        for cond, plane in ((dx < 0, 0), (dx > 0, 1), (dy < 0, 2), (dy > 0, 3)):
            if cond:
                edge = edges_ref[plane, start:stop, :]
                mask = edge if mask is None else mask * edge
        if mask is None:
            mask = edges_ref[4, start:stop, :]
        pieces.append((values * wide(mask, width)).astype(BF16))
    return jnp.concatenate(pieces, axis=0)


def k_reduce(xi, xc, w, x, act, stats, flat, *, sizes, steps):
    step = pl.program_id(0)
    micros, _, cols = xc.shape
    views, at = sizes.views, sizes.crop_at
    tiles = cols // 128
    flat[...] = xi[...].astype(F32).reshape(views * micros * tiles, 128)
    for m in range(micros):
        part = [flat[pl.ds(micros * t + m, views, stride=micros * tiles), :] for t in range(tiles)]
        x[m, :at, :] = jnp.concatenate(
            [jnp.concatenate(part, axis=1).astype(BF16), jnp.zeros((at - views, cols), BF16)], axis=0
        )
        tail = sizes.rows - at - sizes.crops
        x[m, at:, :] = jnp.concatenate([xc[m], jnp.zeros((tail, cols), BF16)], axis=0)
    out = dot(together(x), w[...]).reshape(act.shape)

    @pl.when(step == 0)
    def _():
        act[...] = out

    @pl.when(step > 0)
    def _():
        act[...] += out

    @pl.when(step == steps - 1)
    def _():
        put_stats(stats, act, act)


def together(ref):
    return ref[...].reshape(ref.shape[0] * ref.shape[1], ref.shape[2])


def put_stats(stats, first, second):
    for m in range(first.shape[0]):
        a, b = col_sums(first[m], first[m] * second[m])
        stats[m, 0:1, :] = a
        stats[m, 1:2, :] = b


def chunks(rows):
    step = rows // 3 if rows % 48 == 0 else rows
    return [slice(at, at + step) for at in range(0, rows, step)]


def affine(totals, m, gain, shift, rows):
    means, inv = norm_terms(totals[m], rows)
    scale = inv * gain[...]
    return scale, shift[...] - means * scale, inv, -means * inv


def silu(values):
    half = 0.5 * values
    return half + half * jnp.tanh(half)


def twice_slope(values):
    half = 0.5 * values
    turn = jnp.tanh(half)
    return (1.0 + turn) * (1.0 + half * (1.0 - turn))


def back_terms(totals, sums, m, gain, rows):
    means, inv = norm_terms(totals[m], rows)
    a = gain[...] * inv
    mean_s, mean_sn = sums[m, 0:1] / rows, sums[m, 1:2] / rows
    b = -(a * inv) * mean_sn
    return a, b, -(a * mean_s) - b * means


def set_source(source, edges, sizes):
    micros, _, width = source.shape
    fill_edges(edges, sizes)
    for m in range(micros):
        source[m, :PAD, :] = jnp.zeros((PAD, width), F32)
        source[m, PAD + sizes.rows :, :] = jnp.zeros((PAD, width), F32)


def tap_rows(source, edges, sizes, tap):
    micros, _, width = source.shape
    return jnp.concatenate([tap_block(source.at[m], edges, sizes, tap, width) for m in range(micros)], axis=0)


def k_spatial(act, totals, gain, shift, w, hid, act_two, stats, source, edges, *, sizes, rows):
    step = pl.program_id(0)
    micros, _, width = act.shape

    @pl.when(step == 0)
    def _():
        set_source(source, edges, sizes)
        for m in range(micros):
            scale, bias, _, _ = affine(totals, m, gain, shift, rows)
            hidden = silu(act[m] * scale + bias).astype(BF16)
            hid[m] = hidden
            source[m, PAD : PAD + sizes.rows, :] = hidden.astype(F32)

    for dy in range(3):

        @pl.when(step == dy)
        def _(dy=dy):
            for k in range(3):
                tap = 3 * dy + k
                part = dot(tap_rows(source, edges, sizes, tap), w[k * width : (k + 1) * width, :]).reshape(act_two.shape)
                if tap == 0:
                    act_two[...] = part
                else:
                    act_two[...] += part
            if dy == 2:
                put_stats(stats, act_two, act_two)


def k_expand(act, totals, gain, shift, w, hid, stats, *, sizes, rows):
    micros, n, width = act.shape

    @pl.when(pl.program_id(0) == 0)
    def _():
        keep = wide(sizes.row_mask(), width)
        for m in range(micros):
            scale, bias, _, _ = affine(totals, m, gain, shift, rows)
            hid[m] = jnp.where(keep, silu(act[m] * scale + bias), 0.0).astype(BF16)

    out = dot(together(hid), w[...]).reshape(micros, n, -1)
    put_stats(stats, out, out)


def k_pool(hid, w_expand, totals, gain, shift, x, pool, inv_count, w, pooled, head, stats, low, *, rows, steps):
    step = pl.program_id(0)
    micros, own, _ = head.shape
    n = x.shape[1]
    for m in range(micros):
        scale, bias, _, _ = affine(totals, m, gain, shift, rows)
        for part in chunks(n):
            act = dot(hid[m, part, :], w_expand[...])
            low[m, part, :] = silu((act * scale + bias) + x[m, part, :].astype(F32)).astype(BF16)
    low_pooled = (dot(pool[...], together(low)) * inv_count[...]).astype(BF16)
    pooled[...] = low_pooled
    part = dot(low_pooled, w[...])

    @pl.when(step == 0)
    def _():
        for m in range(micros):
            head[m] = part[m * own : (m + 1) * own]

    @pl.when(step > 0)
    def _():
        for m in range(micros):
            head[m] += part[m * own : (m + 1) * own]

    @pl.when(step == steps - 1)
    def _():
        put_stats(stats, head, head)


def head_forward(head, totals, gain, shift, w_embed, count):
    means, inv = norm_terms(totals, count)
    normed = (head - means) * inv
    pre = normed * gain + shift
    hidden = silu(pre).astype(BF16)
    embedding = dot(hidden, w_embed)
    inv_len = lax.rsqrt(jnp.sum(embedding * embedding, axis=1, keepdims=True) + LEN_EPS)
    return normed, pre, inv, hidden, embedding * inv_len, inv_len


def k_embed(where, head, totals, gain, shift, w_embed, pooled, unit_low, *packs_held, count, lines):
    packs, held = packs_held[:-1], packs_held[-1]
    micros, own, width = head.shape
    shard = 4 * lines
    hidden = []
    for m in range(micros):
        _, _, _, hid, unit, _ = head_forward(head[m], totals[m], gain[...], shift[...], w_embed[...], count)
        unit_low[m] = unit.astype(BF16)
        hidden.append(hid.astype(F32))
    both = jnp.concatenate(hidden, axis=0)
    for n in range(4):
        picked = [both[:, s * shard + n * lines : s * shard + (n + 1) * lines] for s in range(width // shard)]
        held[n] = jnp.concatenate(picked, axis=1).astype(BF16)
    chan, sub = pooled.shape[1], held.shape[2]
    for pack, places in zip(packs, ((0,), (1,), (2, 3))):
        pack[:, :chan] = pooled[...]
        for k, place in enumerate(places):
            pack[:, chan + k * sub : chan + (k + 1) * sub] = held[place ^ where[1]]


def k_embed_only(head, totals, gain, shift, w_embed, hidden, unit_low, *, count):
    for m in range(head.shape[0]):
        _, _, _, hid, unit, _ = head_forward(head[m], totals[m], gain[...], shift[...], w_embed[...], count)
        hidden[m] = hid
        unit_low[m] = unit.astype(BF16)


def k_loss(
    units, ids_all, ids_own, pos_all, pos_own, head, totals, gain, shift, w_embed,
    loss, slopes, grad_embed, stats, *, count, loss_scale, block,
):
    everyone = units[0]
    n_all = everyone.shape[0]
    n_own = head.shape[1]

    def terms(start):
        scores = dot_nt(units[0, pl.ds(start, block), :], everyone)
        return jnp.exp2((scores - 1.0) * (TAU_INV * LOG2E))

    if n_all <= 16 * block:
        total = None
        apart = lax.broadcasted_iota(jnp.int32, (block, block), 0) != lax.broadcasted_iota(jnp.int32, (block, block), 1)
        for k in range(n_all // block):
            row = terms(k * block)
            here = slice(k * block, (k + 1) * block)
            pieces = [row[:, : here.start], jnp.where(apart, row[:, here], 0.0), row[:, here.stop :]]
            row = jnp.concatenate([p for p in pieces if p.shape[1]], axis=1)
            row = jnp.sum(row.reshape(block // 8, 8, n_all), axis=0)
            total = row if total is None else total + row
        sums = jnp.sum(total, axis=0, keepdims=True)
    else:

        def add_rows(k, sums):
            start = pl.multiple_of(k * block, block)
            mine = lax.broadcasted_iota(jnp.int32, (block, n_all), 0) + start
            other = lax.broadcasted_iota(jnp.int32, (block, n_all), 1)
            return sums + jnp.sum(jnp.where(mine == other, 0.0, terms(start)), axis=0, keepdims=True)

        sums = lax.fori_loop(0, n_all // block, add_rows, jnp.zeros((1, n_all), F32))
    log_all = jnp.log(sums) + TAU_INV
    normed, pre, inv, hid, unit, inv_len = head_forward(
        head[0], totals[0], gain[...], shift[...], w_embed[...], count
    )
    low = unit.astype(BF16)
    scores = dot_nt(low, everyone) * TAU_INV
    itself = lax.broadcasted_iota(jnp.int32, (n_own, n_all), 0) == lax.broadcasted_iota(
        jnp.int32, (n_own, n_all), 1
    )
    own_sum = jnp.sum(jnp.where(itself, 0.0, jnp.exp(scores - TAU_INV)), axis=1, keepdims=True)
    log_own = jnp.log(own_sum) + TAU_INV
    positive = (ids_own[0] == ids_all[0]) & jnp.logical_not(itself)
    pos_sum = jnp.sum(jnp.where(positive, scores, 0.0), axis=1, keepdims=True)
    loss[0] = log_own - pos_sum * pos_own[0]
    by_row = jnp.where(itself, 0.0, jnp.exp(scores - log_own)) - jnp.where(positive, pos_own[0], 0.0)
    by_col = jnp.where(itself, 0.0, jnp.exp(scores - log_all)) - jnp.where(positive, pos_all[0], 0.0)
    grad_unit = (
        dot((by_row * loss_scale).astype(BF16), everyone)
        + dot((by_col * loss_scale).astype(BF16), everyone)
    ) * TAU_INV
    grad = inv_len * (grad_unit - unit * jnp.sum(unit * grad_unit, axis=1, keepdims=True))
    grad_low = grad.astype(BF16)
    grad_embed[0] = grad_low
    slope = dot_nt(grad_low, w_embed[...]) * (0.5 * twice_slope(pre))
    slopes[0] = slope
    a, b = col_sums(slope, slope * normed)
    stats[0, 0:1, :] = a
    stats[0, 1:2, :] = b


def k_head_back(where, slopes, head, totals, sums, gain, embed, grad, *packs, count):
    micros, own, width = head.shape
    rows = []
    for m in range(micros):
        a, b, c = back_terms(totals, sums, m, gain, count)
        rows.append(slopes[m] * a + head[m] * b + c)
    grad[...] = jnp.concatenate(rows, axis=0).astype(BF16)
    if packs:
        emb = jnp.concatenate([embed[m].astype(F32) for m in range(micros)], axis=0).astype(BF16)
        quarter = width // 4
        for place, pack in enumerate(packs):
            at = pl.multiple_of((place ^ where[1]) * quarter, quarter)
            pack[:, :quarter] = grad[:, pl.ds(at, quarter)]
            pack[:, quarter:] = emb


def k_back_pool(grad_head, hid, w_expand, totals, gain, shift, x, spread, half_count, w, grad_resid, stats, *, rows):
    micros, n, cols = x.shape
    pair = jnp.concatenate(halves(dot_nt(grad_head[...], w[...]) * half_count[...]), axis=0)
    for m in range(micros):
        scale, bias, inv, offset = affine(totals, m, gain, shift, rows)
        sums = None
        for part in chunks(n):
            act = dot(hid[m, part, :], w_expand[...])
            back = dot(spread[m * n + part.start : m * n + part.stop, :], pair)
            slope = back * twice_slope((act * scale + bias) + x[m, part, :].astype(F32))
            grad_resid[m, part, :] = slope.astype(BF16)
            more = col_sums(slope, slope * (act * inv + offset))
            sums = more if sums is None else (sums[0] + more[0], sums[1] + more[1])
        stats[m, 0:1, :] = sums[0]
        stats[m, 1:2, :] = sums[1]


def k_back_expand(
    where, grad_resid, hid, tot_three, sum_three, gain_three, w, act_two, tot_two, gain_two, shift_two,
    slopes, stats, *rest, sizes, rows, steps, shares,
):
    step = pl.program_id(0)
    micros, n, mid = hid.shape
    if shares:
        keep, send, low, turned = rest

        @pl.when(step == 0)
        def _():
            for m in range(micros):
                turned[:, m * n : (m + 1) * n] = hid[m].T

    else:
        (low,) = rest

    @pl.when(step == 0)
    def _():
        slopes[...] = jnp.zeros(slopes.shape, F32)

    for m in range(micros):
        a, b, c = back_terms(tot_three, sum_three, m, gain_three, rows)
        for part in chunks(n):
            act = dot(hid[m, part, :], w[...])
            grad = (grad_resid[m, part, :].astype(F32) * a + (act * b + c)).astype(BF16)
            low[m, part, :] = grad
            slopes[m, part, :] += dot_nt(grad, w[...])

    if shares:
        share = dot(turned[...], together(low)).astype(BF16)
        each = mid // 8
        for out, even in ((keep, 0), (send, 1)):

            @pl.when(step % 2 == even)
            def _(out=out):
                for shard in range(8):
                    place = shard ^ where[0]
                    out[place % 2, place // 2, 0] = share[shard * each : (shard + 1) * each]

    @pl.when(step == steps - 1)
    def _():
        finish_slopes(slopes, stats, act_two, tot_two, gain_two, shift_two, rows, wide(sizes.row_mask(), mid))


def finish_slopes(slopes, stats, act, totals, gain, shift, rows, keep=None):
    for m in range(slopes.shape[0]):
        scale, bias, inv, offset = affine(totals, m, gain, shift, rows)
        slope = slopes[m] * (0.5 * twice_slope(act[m] * scale + bias))
        if keep is not None:
            slope = jnp.where(keep, slope, 0.0)
        slopes[m] = slope
        a, b = col_sums(slope, slope * (act[m] * inv + offset))
        stats[m, 0:1, :] = a
        stats[m, 1:2, :] = b


UNIT = 64
UNITS_A = 5


def k_back_spatial(
    where, slopes, act_two, tot_two, sum_two, gain_two, w, act_one, tot_one, gain_one, shift_one, hid,
    slopes_one, stats, *rest, sizes, rows, shares,
):
    if shares:
        keep_a, send_a, keep_b, send_b, source, edges, turned, block = rest
        core, line = where[1] % 2, where[1] // 2
    else:
        grad_two, source, edges = rest
    step = pl.program_id(0)
    micros, n, mid = act_two.shape

    @pl.when(step == 0)
    def _():
        set_source(source, edges, sizes)
        for m in range(micros):
            a, b, c = back_terms(tot_two, sum_two, m, gain_two, rows)
            low = (slopes[m] * a + (act_two[m] * b + c)).astype(BF16)
            source[m, PAD : PAD + sizes.rows, :] = low.astype(F32)
            if shares:
                turned[:, m * n : (m + 1) * n] = hid[m].T
            else:
                grad_two[m] = low

    def share(tap, here):
        part = dot(turned[...], here)
        for q in range(4):
            block[q] = part[:, 128 * q : 128 * (q + 1)].astype(BF16)
        for unit in range(8 * (8 - tap), 8 * (9 - tap)):
            shard, k = divmod(unit, 9)
            place = shard ^ where[0]
            lines = slice(UNIT * (unit % 8), UNIT * (unit % 8 + 1))
            for y in range(2):
                for out_a, out_b, c in ((keep_a, keep_b, core), (send_a, send_b, 1 - core)):
                    piece = block[2 * y + c, lines, :]
                    if k < UNITS_A:
                        out_a[place % 2, place // 2, y ^ line, k * UNIT : (k + 1) * UNIT, :] = piece
                    else:
                        at = (k - UNITS_A) * UNIT
                        out_b[y ^ line, place % 2, place // 2, at : at + UNIT, :] = piece

    for dy in range(3):

        @pl.when(step == dy)
        def _(dy=dy):
            for k in range(3):
                tap = 3 * dy + k
                here = tap_rows(source, edges, sizes, tap)
                part = dot_nt(here, w[(2 - k) * mid : (3 - k) * mid, :]).reshape(slopes_one.shape)
                if tap == 0:
                    slopes_one[...] = part
                else:
                    slopes_one[...] += part
                if shares:
                    share(tap, here)
            if dy == 2:
                finish_slopes(slopes_one, stats, act_one, tot_one, gain_one, shift_one, rows)


def k_weight_hidden(where, *refs):
    rows, packs = refs[:4], refs[4:8]
    subs = refs[8:12]
    keep, send, grads, extra, held = refs[12:]
    step = pl.program_id(0)
    quarter = keep.shape[2]

    @pl.when(step == 0)
    def _():
        total = None
        for k in range(4):
            n = packs[k].shape[0]
            grads[k * n : (k + 1) * n, :] = packs[k][:, :quarter].astype(F32)
            part = dot_tn(subs[k][...], packs[k][:, quarter:])
            total = part if total is None else total + part
        extra[...] = total.astype(BF16).reshape(extra.shape)

    pooled = jnp.concatenate([r[...].astype(F32) for r in rows], axis=0).astype(BF16)
    held[...] = dot_tn(pooled, grads[...].astype(BF16)).astype(BF16).reshape(held.shape)
    shard = held.shape[1]
    for x, ref in ((0, keep), (1, send)):
        more = extra[(2 * step + x) ^ where[0]]
        lines = more.shape[0] // 4
        ref[0, :shard, :] = held[x ^ (where[0] % 2)]
        for k in range(4):
            ref[0, shard:, 128 * k : 128 * (k + 1)] = more[lines * k : lines * (k + 1), :]


def k_weight_reduce(
    where, x, slopes, act, totals, sums, gain, grad, keep, send, turned, block, *, rows
):
    micros, n, mid = slopes.shape
    core, line = where[1] % 2, where[1] // 2

    @pl.when(pl.program_id(0) == 0)
    def _():
        for m in range(micros):
            a, b, c = back_terms(totals, sums, m, gain, rows)
            low = (slopes[m] * a + (act[m] * b + c)).astype(BF16)
            grad[m] = low
            turned[:, m * n : (m + 1) * n] = low.T

    total = dot(turned[...], together(x)).astype(BF16).T
    for q in range(4):
        block[q] = total[:, 128 * q : 128 * (q + 1)]
    for y in range(2):
        for out, c in ((keep, core), (send, 1 - core)):
            out[0, 0, y ^ line] = block[2 * y + c]


def k_grad_one(slopes, act, totals, sums, gain, grad, *, rows):
    for m in range(slopes.shape[0]):
        a, b, c = back_terms(totals, sums, m, gain, rows)
        grad[m] = (slopes[m] * a + (act[m] * b + c)).astype(BF16)


def k_back_reduce(grad_one, w, grad_resid, *refs, sizes):
    grad_v, grad_c = refs[-2:]
    views, lines, _ = grad_v.shape
    micros = grad_one.shape[0]
    flat = grad_v.reshape(views * lines, 128)
    at = sizes.crop_at
    n = sizes.rows
    back = dot_nt(together(grad_one), w[...])
    for m in range(micros):
        both = grad_resid[m].astype(F32) + back[m * n : (m + 1) * n]
        grad_c[m] = both[at : at + sizes.crops]
        for t in range(lines // micros):
            flat[pl.ds(micros * t + m, views, stride=lines), :] = both[:views, 128 * t : 128 * (t + 1)]


def call(kernel, name, grid, ins, outs, scratch=(), flops=0, vmem=44, where=None, aliases=None):
    spec = lambda block, index: pl.BlockSpec(block, index) if block else pl.BlockSpec(memory_space=pl.ANY)
    scalars = [] if where is None else [where]
    moved = sum(a.size * a.dtype.itemsize for a, _, _ in ins) + sum(
        math.prod(s) * jnp.dtype(t).itemsize for s, t, _, _ in outs
    )
    return pl.pallas_call(
        kernel,
        grid_spec=pltpu.PrefetchScalarGridSpec(
            num_scalar_prefetch=len(scalars),
            grid=grid,
            in_specs=[spec(b, i) for _, b, i in ins],
            out_specs=[spec(b, i) for _, _, b, i in outs],
            scratch_shapes=list(scratch),
        ),
        out_shape=[jax.ShapeDtypeStruct(s, t) for s, t, _, _ in outs],
        compiler_params=pltpu.CompilerParams(vmem_limit_bytes=vmem * MIB),
        cost_estimate=pl.CostEstimate(flops=1000, bytes_accessed=1000, transcendentals=0),
        name=name,
        input_output_aliases=aliases or {},
    )(*scalars, *[a for a, _, _ in ins])


def exact(array):
    return lax.optimization_barrier(array)


def add_low(*parts):
    total = parts[0].astype(F32)
    for part in parts[1:]:
        total = total + part.astype(F32)
    return total.astype(BF16)


def reduce_weight(grad, count, data_size, narrow_size):
    rows, cols = grad.shape
    me = lax.axis_index("dp")
    core = lax.axis_index("narrow") % 2
    blocks = grad.reshape(data_size, rows // data_size, cols)
    blocks = jnp.stack(
        [lax.dynamic_index_in_dim(blocks, me ^ j, axis=0, keepdims=False) for j in range(data_size)]
    )
    half = cols // 2
    low, high = blocks[:, :, :half], blocks[:, :, half:]
    keep = jnp.where(core == 0, low, high)
    send = jnp.where(core == 0, high, low)
    part = add_low(keep, xor_permute(send, 1, count))
    size = data_size
    for stage in bit_stages(0, data_size.bit_length() - 1):
        if len(stage) == 1:
            split = part.reshape((size // 2, 2) + part.shape[1:])
            part = add_low(split[:, 0], xor_permute(split[:, 1], stage[0] * narrow_size, count))
            size //= 2
        else:
            split = part.reshape((size // 4, 4) + part.shape[1:])
            got = [
                xor_permute(split[:, k], off * narrow_size, count)
                for k, off in ((1, stage[0]), (2, stage[1]), (3, stage[0] ^ stage[1]))
            ]
            part = add_low(split[:, 0], *got)
            size //= 4
    part = exact(part[0])
    off = 2
    while off < narrow_size:
        part = exact(add_low(part, xor_permute(part, off, count)))
        off *= 2
    other = xor_permute(part, 1, count)
    both = jnp.where(
        core == 0, jnp.concatenate([part, other], axis=1), jnp.concatenate([other, part], axis=1)
    )
    return both.astype(F32)


class Mesh84:
    core, line, x, z = 1, 2, 4, 8

    def __init__(self, count):
        self.count = count

    def send(self, array, offset):
        return xor_permute(array, offset, self.count)

    def split(self, keep, got):
        return [add_low(keep[k], got[k]) for k in range(keep.shape[0])]

    def across_z(self, parts, *others):
        sent = [after(p, *others) if others else p for p in parts[1:]]
        return [parts[0]] + [self.send(sent[k - 1], self.z * k) for k in (1, 2, 3)]

    def quarters(self, near, far, narrow):
        places = (near[0], far[0], near[1], far[1])
        pick = lambda q: lax.select_n(narrow, *(places[q ^ n] for n in range(4)))
        return jnp.concatenate([pick(q) for q in range(4)], axis=-1)


def after(value, *others):
    return lax.optimization_barrier((value, *others))[0]


def hidden_share(rows, packs, where):
    total, wide_cols = rows[0].shape
    chan = wide_cols * 4 // 5
    sub = wide_cols - chan
    emb = packs[0].shape[1] - sub
    shard = chan // 8
    extra = sub // 8 * emb // sub
    fix = lambda i, w: (0, 0)
    out = ((4, shard + extra, sub), BF16, (1, shard + extra, sub), lambda i, w: (i, 0, 0))
    return call(
        k_weight_hidden, "weight_hidden", (4,),
        [(r, (total, 2 * shard), lambda i, w: (0, i ^ (w[0] // 2))) for r in rows]
        + [(p, p.shape, fix) for p in packs]
        + [(r, (total, sub), lambda i, w: (0, chan // sub)) for r in rows],
        [out, out],
        scratch=[
            pltpu.VMEM((4 * total, sub), F32),
            pltpu.VMEM((8, sub // 8, emb), BF16),
            pltpu.VMEM((2, shard, sub), BF16),
        ],
        flops=8 * total * chan * sub,
        where=where,
    )


def spread_taps(hidden, side):
    padded = jnp.pad(hidden, ((0, 0), (1, 1), (1, 1), (0, 0)))
    pieces = [padded[:, dy : dy + side, dx : dx + side, :] for dy in range(3) for dx in range(3)]
    return jnp.concatenate(pieces, axis=-1)


def body(
    view_maps, crop_maps, image_ids, w_reduce, gain_one, shift_one, w_spatial, gain_two, shift_two,
    w_expand, gain_three, shift_three, w_hidden, gain_head, shift_head, w_embed,
):
    micros, view_rows, channels = view_maps.shape
    crop_rows = crop_maps.shape[1]
    mid = w_reduce.shape[1]
    hidden_width = w_hidden.shape[1]
    emb_width = w_embed.shape[1]
    images_dev = view_rows // (VIEWS * VSIDE * VSIDE)
    each = VIEWS + CROPS
    own = images_dev * each
    data_size, narrow_size = lax.axis_size("dp"), lax.axis_size("narrow")
    count = data_size * narrow_size
    emb_total = own * count
    pixel_count = (view_rows + crop_rows) * count
    loss_scale = 1.0 / (micros * emb_total)
    device = lax.axis_index("dp") * narrow_size + lax.axis_index("narrow")
    sizes = Sizes(view_rows, crop_rows)
    rows = sizes.rows

    pool = np.zeros((micros, own, micros, rows), np.float32)
    for m in range(micros):
        for r in range(view_rows):
            image, view = divmod(r // (VSIDE * VSIDE), VIEWS)
            pool[m, image * each + view, m, r] = 1
        for r in range(crop_rows):
            image, crop = divmod(r // (CSIDE * CSIDE), CROPS)
            pool[m, image * each + VIEWS + crop, m, sizes.crop_at + r] = 1
    pool = pool.reshape(micros * own, micros * rows)
    inv_count = np.where(np.arange(micros * own) % each < VIEWS, 1.0 / VSIDE**2, 1.0 / CSIDE**2)[:, None]
    spread = jnp.asarray(np.concatenate([pool.T, pool.T], axis=1), BF16)
    pool = jnp.asarray(pool, BF16)
    half_count = jnp.asarray(0.5 * inv_count, F32)
    inv_count = jnp.asarray(inv_count, F32)

    place = jnp.asarray(gather_order(count)) ^ device
    same = jnp.sum((image_ids[:, :, None] == image_ids[:, None, :]).astype(F32), axis=2)
    inv_pos = 1.0 / (same * each - 1.0)

    from_device = place[:, None] == jnp.arange(count, dtype=jnp.int32)[None, :]

    def by_place(values):
        blocks = values.reshape(micros, 1, count, images_dev)
        moved = jnp.sum(jnp.where(from_device[None, :, :, None], blocks, 0), axis=2)
        return jnp.repeat(moved.reshape(micros, -1), each, axis=1)

    ids_all, pos_all = by_place(image_ids), by_place(inv_pos)
    ids_own, pos_own = ids_all[:, :own, None], pos_all[:, :own, None]
    ids_all, pos_all = ids_all[:, None, :], pos_all[:, None, :]

    row = lambda v: v.reshape(1, -1)
    g1, b1, g2, b2 = row(gain_one), row(shift_one), row(gain_two), row(shift_two)
    g3, b3, gh, bh = row(gain_three), row(shift_three), row(gain_head), row(shift_head)
    reduce_all = lambda stats: all_sum(stats, count)
    flops = 2.0 * micros * rows * channels * mid

    fast = data_size == 8 and narrow_size == 4 and mid == 512 and micros == 2
    dp, narrow = lax.axis_index("dp"), lax.axis_index("narrow")
    where = jnp.stack([dp, narrow]).astype(jnp.int32)
    net = Mesh84(count)
    blk = 512
    steps = channels // blk
    fix2 = lambda *_: (0, 0)
    fix3 = lambda *_: (0, 0, 0)
    col = lambda n, *_: (0, n)
    col3 = lambda n, *_: (0, 0, n)
    row = lambda n, *_: (n, 0)
    m0 = lambda m, *_: (m, 0, 0)
    act_mid = (micros, rows, mid)
    two = lambda array: (array, array.shape, fix3)
    vec = lambda array: (array, array.shape, fix2)
    vec_block = lambda array: (array, (1, blk), col)
    tot_block = lambda array: (array, (micros, 2, blk), col3)
    stats_of = lambda width: ((micros, 2, width), F32, (micros, 2, width), fix3)

    tiles = channels // 128
    mixed = jnp.transpose(view_maps.reshape(micros, view_rows, tiles, 128), (1, 2, 0, 3))
    mixed = mixed.reshape(view_rows, micros * tiles, 128)
    lines = micros * blk // 128
    pixels, act_one, st = call(
        functools.partial(k_reduce, sizes=sizes, steps=steps), "reduce", (steps,),
        [
            (mixed, (view_rows, lines, 128), lambda n: (0, n, 0)),
            (crop_maps, (micros, crop_rows, blk), col3),
            (w_reduce, (blk, mid), row),
        ],
        [
            ((micros, rows, channels), BF16, (micros, rows, blk), col3),
            (act_mid, F32, act_mid, fix3),
            stats_of(mid),
        ],
        scratch=[pltpu.VMEM((view_rows * lines, 128), F32)],
        flops=flops,
    )
    tot_one = reduce_all(st)
    taps_scratch = [
        pltpu.VMEM((micros, rows + 2 * PAD, mid), F32),
        pltpu.VMEM((5, rows, 128), F32),
    ]
    hid_one, act_two, st = call(
        functools.partial(k_spatial, sizes=sizes, rows=pixel_count), "spatial", (3,),
        [two(act_one), two(tot_one), vec(g1), vec(b1), (w_spatial, (3 * mid, mid), row)],
        [(act_mid, BF16, act_mid, fix3), (act_mid, F32, act_mid, fix3), stats_of(mid)],
        scratch=taps_scratch,
        flops=flops * 9 * mid / channels,
    )
    tot_two = reduce_all(st)
    hid_two, st = call(
        functools.partial(k_expand, sizes=sizes, rows=pixel_count), "expand", (steps,),
        [two(act_two), two(tot_two), vec(g2), vec(b2), (w_expand, (mid, blk), col)],
        [(act_mid, BF16, act_mid, fix3), ((micros, 2, channels), F32, (micros, 2, blk), col3)],
        flops=flops,
    )
    tot_three = reduce_all(st)
    flat_own = micros * own
    pooled, head, st = call(
        functools.partial(k_pool, rows=pixel_count, steps=steps), "pool", (steps,),
        [
            two(hid_two),
            (w_expand, (mid, blk), col),
            tot_block(tot_three),
            vec_block(g3),
            vec_block(b3),
            (pixels, (micros, rows, blk), col3),
            vec(pool),
            vec(inv_count),
            (w_hidden, (blk, hidden_width), row),
        ],
        [
            ((flat_own, channels), BF16, (flat_own, blk), col),
            ((micros, own, hidden_width), F32, (micros, own, hidden_width), fix3),
            stats_of(hidden_width),
        ],
        scratch=[pltpu.VMEM((micros, rows, blk), BF16)],
        flops=flops,
    )
    tot_head = reduce_all(st)
    head_in = [two(head), two(tot_head), vec(gh), vec(bh), vec(w_embed)]
    unit_shape = (micros, own, emb_width)
    if fast:
        sub = hidden_width // 4
        pack = (flat_own, channels + sub)
        unit_low, *rows_packs = call(
            functools.partial(k_embed, count=emb_total, lines=sub // 8), "embed", (1,), head_in + [vec(pooled)],
            [(unit_shape, BF16, unit_shape, fix3)] + [(pack, BF16, pack, fix2)] * 2
            + [((flat_own, channels + 2 * sub), BF16, (flat_own, channels + 2 * sub), fix2)],
            scratch=[pltpu.VMEM((4, flat_own, sub), BF16)],
            where=where,
        )
    else:
        head_hid, unit_low = call(
            functools.partial(k_embed_only, count=emb_total), "embed", (1,), head_in,
            [
                ((micros, own, hidden_width), BF16, (micros, own, hidden_width), fix3),
                (unit_shape, BF16, unit_shape, fix3),
            ],
        )
    units = gather_all(unit_low, count)
    units = jnp.transpose(units, (1, 0, 2, 3)).reshape(micros, emb_total, emb_width)
    if fast:
        pack_own, pack_core, pack_line = (after(p, units) for p in rows_packs)
        got_core = net.send(pack_core, net.core)
        got_line = net.send(pack_line, net.line)
    loss, slopes, grad_embed, st = call(
        functools.partial(k_loss, count=emb_total, loss_scale=loss_scale, block=128), "loss", (micros,),
        [
            (units, (1, emb_total, emb_width), m0),
            (ids_all, (1, 1, emb_total), m0),
            (ids_own, (1, own, 1), m0),
            (pos_all, (1, 1, emb_total), m0),
            (pos_own, (1, own, 1), m0),
            (head, (1, own, hidden_width), m0),
            (tot_head, (1, 2, hidden_width), m0),
            vec(gh),
            vec(bh),
            vec(w_embed),
        ],
        [
            ((micros, own, 1), F32, (1, own, 1), m0),
            ((micros, own, hidden_width), F32, (1, own, hidden_width), m0),
            (unit_shape, BF16, (1, own, emb_width), m0),
            ((micros, 2, hidden_width), F32, (1, 2, hidden_width), m0),
        ],
    )
    if fast:
        got_core, got_line = (after(g, st) for g in (got_core, got_line))
        st = after(st, got_line)
        wide_cols = channels + sub
        pass_on = jnp.concatenate([got_line[:, :channels], got_line[:, wide_cols:]], axis=1)
        rows_packs = [pack_own, got_core, got_line[:, :wide_cols], net.send(pass_on, net.core)]
    sum_head = reduce_all(st)

    grad_head, *packs = call(
        functools.partial(k_head_back, count=emb_total), "head_back", (1,),
        [two(slopes), two(head), two(tot_head), two(sum_head), vec(gh), two(grad_embed)],
        [((flat_own, hidden_width), BF16, (flat_own, hidden_width), fix2)]
        + [((flat_own, hidden_width // 4 + emb_width), BF16, (flat_own, hidden_width // 4 + emb_width), fix2)]
        * (4 if fast else 0),
        where=where,
    )
    if fast:
        packs = packs[:1] + [net.send(packs[k], k) for k in (1, 2, 3)]
    grad_resid, st = call(
        functools.partial(k_back_pool, rows=pixel_count), "back_pool", (steps,),
        [
            vec(grad_head),
            two(hid_two),
            (w_expand, (mid, blk), col),
            tot_block(tot_three),
            vec_block(g3),
            vec_block(b3),
            (pixels, (micros, rows, blk), col3),
            vec(spread),
            vec(half_count),
            (w_hidden, (blk, hidden_width), row),
        ],
        [
            ((micros, rows, channels), BF16, (micros, rows, blk), col3),
            ((micros, 2, channels), F32, (micros, 2, blk), col3),
        ],
        flops=flops,
    )
    if fast:
        packs = packs[:1] + [after(g, st) for g in packs[1:]]
        wh_keep, wh_send = hidden_share(rows_packs, packs, where)
    sum_three = reduce_all(st)
    if fast:
        wh_got = net.send(after(wh_send, sum_three), net.x)
        grad_resid = after(grad_resid, wh_send, wh_keep)
    turn = (lambda n, w: n ^ w[1]) if fast else (lambda n, w: n)
    turn3 = lambda n, w: (0, 0, turn(n, w))
    turn2 = lambda n, w: (0, turn(n, w))
    w3_share = (2, 4, 2, mid // 8, blk)
    w3_out = (w3_share, BF16, (2, 4, 1, mid // 8, blk), lambda n, w: (0, 0, n // 2, 0, 0))
    slopes_two, st, *rest = call(
        functools.partial(k_back_expand, sizes=sizes, rows=pixel_count, steps=steps, shares=fast), "back_expand", (steps,),
        [
            (grad_resid, (micros, rows, blk), turn3),
            two(hid_two),
            (tot_three, (micros, 2, blk), turn3),
            (sum_three, (micros, 2, blk), turn3),
            (g3, (1, blk), turn2),
            (w_expand, (mid, blk), turn2),
            two(act_two),
            two(tot_two),
            vec(g2),
            vec(b2),
        ],
        [(act_mid, F32, act_mid, fix3), stats_of(mid)]
        + ([w3_out, w3_out] if fast else [((micros, rows, channels), BF16, (micros, rows, blk), turn3)]),
        scratch=[pltpu.VMEM((micros, rows, blk), BF16), pltpu.VMEM((mid, micros * rows), BF16)] if fast else [],
        flops=2 * flops,
        where=where,
    )
    if fast:
        w3_keep, w3_send = rest
        w3_got = net.send(w3_send, net.core)
        wh_z = net.split(wh_keep, after(wh_got, st, w3_send))
        w3_x = net.split(w3_keep, w3_got)
        st = after(st, wh_got)
    else:
        (w3_full,) = rest
    sum_two = reduce_all(st)
    if fast:
        wh_got = net.across_z(wh_z, sum_two)
        w3_got = net.send(after(w3_x[1], sum_two), net.x)
        slopes_two = after(slopes_two, *wh_z, *w3_x)
    shapes = [(2, 4, 2, UNITS_A * UNIT, 128)] * 2 + [(2, 2, 4, (9 - UNITS_A) * UNIT, 128)] * 2
    slopes_one, st, *rest = call(
        functools.partial(k_back_spatial, sizes=sizes, rows=pixel_count, shares=fast), "back_spatial", (3,),
        [
            two(slopes_two),
            two(act_two),
            two(tot_two),
            two(sum_two),
            vec(g2),
            (w_spatial, (3 * mid, mid), lambda n, *_: (2 - n, 0)),
            two(act_one),
            two(tot_one),
            vec(g1),
            vec(b1),
            two(hid_one),
        ],
        [(act_mid, F32, act_mid, fix3), stats_of(mid)]
        + ([(t, BF16, t, lambda *_: (0,) * 5) for t in shapes] if fast else [(act_mid, BF16, act_mid, fix3)]),
        scratch=taps_scratch
        + ([pltpu.VMEM((mid, micros * rows), BF16), pltpu.VMEM((4, mid, 128), BF16)] if fast else []),
        flops=2 * flops * 9 * mid / channels,
        where=where,
    )
    if fast:
        w2_keep_a, w2_send_a, w2_keep_b, w2_send_b = rest
        wh_part = exact(add_low(*(after(g, st) for g in wh_got)))
        w3_z = net.split(w3_x[0], after(w3_got, st))
        st = after(st, *wh_got, w3_got)
        first = []
        sum_one = all_sum(st, count, first.append)
        w2_got_a, w2_got_b = (net.send(after(g, *first), net.core) for g in (w2_send_a, w2_send_b))
        w2_x = net.split(w2_keep_a, w2_got_a)
        w2_y = net.split(w2_keep_b, w2_got_b)
        w2_got_a = net.send(after(w2_x[1], sum_one), net.x)
        w2_got_b = net.send(after(w2_y[1], sum_one), net.line)
        w3_got = net.across_z(w3_z, sum_one)
    else:
        sum_one = reduce_all(st)
    one_in = [two(slopes_one), two(act_one), two(tot_one), two(sum_one), vec(g1)]
    if fast:
        one_in[0] = two(after(slopes_one, *w3_z, *w2_x, *w2_y, wh_part))
        shard = channels // 8
        out = ((2, 4, 2, shard, 128), BF16, (1, 1, 2, shard, 128), lambda j, w: (j % 2, j // 2, 0, 0, 0))
        grad_one, w1_keep, w1_send = call(
            functools.partial(k_weight_reduce, rows=pixel_count), "weight_reduce", (8,),
            [(pixels, (micros, rows, shard), lambda j, w: (0, 0, j ^ w[0]))] + one_in,
            [(act_mid, BF16, act_mid, fix3), out, out],
            scratch=[pltpu.VMEM((mid, micros * rows), BF16), pltpu.VMEM((4, shard, 128), BF16)],
            flops=flops,
            where=where,
        )
        w1_got = net.send(w1_send, net.core)
        w2_got_a, w2_got_b, *w3_got, _ = exact((w2_got_a, w2_got_b, *w3_got, w1_send))
        w2_z = net.split(w2_x[0], w2_got_a)
        w2_x = net.split(w2_y[0], w2_got_b)
        w3_part = exact(add_low(*w3_got))
        w2_got_a = net.across_z(w2_z)
        w2_got_b = net.send(w2_x[1], net.x)
        w3_line = net.send(w3_part, net.line)
        grad_one = after(grad_one, *w2_z, *w2_x, w3_part)
    else:
        (grad_one,) = call(
            functools.partial(k_grad_one, rows=pixel_count), "grad_one", (1,), one_in, [(act_mid, BF16, act_mid, fix3)]
        )
    def back_reduce(first, grads, before=()):
        at = lambda n: n + first
        return call(
            functools.partial(k_back_reduce, sizes=sizes), "back_reduce", (steps // 2,),
            [
                two(grads),
                (w_reduce, (blk, mid), lambda n: (at(n), 0)),
                (grad_resid, (micros, rows, blk), lambda n: (0, 0, at(n))),
            ]
            + [(b, None, None) for b in before],
            [
                ((view_rows, micros * tiles, 128), F32, (view_rows, lines, 128), lambda n: (0, at(n), 0)),
                (crop_maps.shape, F32, (micros, crop_rows, blk), lambda n: (0, 0, at(n))),
            ],
            flops=flops / 2,
            aliases={3 + k: k for k in range(len(before))},
        )

    grad_views, grad_crops = back_reduce(0, grad_one)
    if fast:
        w1_got, w2_got_b, w3_line, *w2_got_a, grad_crops = exact((w1_got, w2_got_b, w3_line, *w2_got_a, grad_crops))
        w1_x = net.split(w1_keep, w1_got)
        w1_got = net.send(w1_x[1], net.x)
        w2_bz = net.split(w2_x[0], w2_got_b)
        w2_got_b = net.across_z(w2_bz)
        w2_a = exact(add_low(*w2_got_a))
        w2_got_a = net.send(w2_a, net.line)
        w3_part = exact(add_low(w3_part, w3_line[::-1]))
        w3_far = net.send(w3_part, net.core)
        wh_line = net.send(after(wh_part, grad_crops), net.line)
        grad_one = after(grad_one, *w1_x, *w2_bz, w2_a, w3_part)
    grad_views, grad_crops = back_reduce(steps // 2, grad_one, (grad_views, grad_crops))
    grad_views = jnp.transpose(grad_views.reshape(view_rows, tiles, micros, 128), (2, 0, 1, 3)).reshape(view_maps.shape)

    if fast:
        w1_got, w2_got_a, wh_line, w3_far, *w2_got_b, grad_crops = exact(
            (w1_got, w2_got_a, wh_line, w3_far, *w2_got_b, grad_crops)
        )
        w1_got = net.across_z(net.split(w1_x[0], w1_got))
        w2_b = exact(add_low(*w2_got_b))
        w2_a = exact(add_low(w2_a, w2_got_a[::-1]))
        wh_pair = jnp.stack([wh_part, wh_line])
        arrived = exact((*w1_got, net.send(w2_b, net.line), net.send(w2_a, net.core), net.send(wh_pair, net.core)))
        w1_part = exact(add_low(*arrived[:4]))
        w2_pair = jnp.stack([w2_b, arrived[4]])
        w2_a_far, wh_far = arrived[5:]
        w1_line, w2_b_far = exact((net.send(w1_part, net.line), net.send(w2_pair, net.core)))
        w1_part = exact(add_low(w1_part, w1_line[::-1]))
        w1_far = net.send(w1_part, net.core)
        lines = w_hidden.shape[0] // data_size
        gw_hidden = net.quarters(wh_pair[:, :lines], wh_far[:, :lines], narrow).astype(F32)
        extra = net.quarters(wh_pair[:, lines:], wh_far[:, lines:], narrow)
        extra = extra.reshape(-1, 4, 4, emb_width)
        gw_embed = jnp.transpose(extra, (1, 2, 0, 3)).reshape(-1, emb_width).astype(F32)
        gw_expand = net.quarters(w3_part, w3_far, narrow).astype(F32)
        w2 = [net.quarters(w2_a, w2_a_far, narrow), net.quarters(w2_pair, w2_b_far, narrow)]
        gw_spatial = jnp.concatenate(w2, axis=0).astype(F32)
        gw_reduce = net.quarters(w1_part, w1_far, narrow).astype(F32)
    else:
        over = lambda a, b: jnp.einsum("mri,mrj->ij", a, b, preferred_element_type=F32)
        reduce_w = lambda g: reduce_weight(g.astype(BF16), count, data_size, narrow_size)
        gw_embed = reduce_w(over(head_hid, grad_embed))
        gw_hidden = reduce_w(jnp.dot(pooled.T, grad_head, preferred_element_type=F32))
        gw_expand = reduce_w(over(hid_two, w3_full))
        at = sizes.crop_at
        real = lambda t: (t[:, :view_rows], t[:, at : at + crop_rows])
        cols = [
            spread_taps(part.reshape(-1, side, side, mid), side).reshape(micros, -1, 9, mid)
            for part, side in zip(real(rest[0]), (VSIDE, CSIDE))
        ]
        by_tap = jnp.einsum(
            "mri,mrtj->tij", jnp.concatenate(real(hid_one), axis=1), jnp.concatenate(cols, axis=1),
            preferred_element_type=F32,
        )[::-1]
        gw_spatial = reduce_w(by_tap.reshape(9 * mid, mid))
        gw_reduce = reduce_w(over(pixels, grad_one))
    gain_grad = lambda sums: jnp.sum(sums[:, 1], axis=0)
    shift_grad = lambda sums: jnp.sum(sums[:, 0], axis=0)
    return (
        loss.reshape(micros, own), grad_views, grad_crops,
        gw_reduce, gain_grad(sum_one), shift_grad(sum_one),
        gw_spatial, gain_grad(sum_two), shift_grad(sum_two),
        gw_expand, gain_grad(sum_three), shift_grad(sum_three),
        gw_hidden, gain_grad(sum_head), shift_grad(sum_head),
        gw_embed,
    )


def solution(mesh):
    rows = P(None, BOTH, None)
    return jax.shard_map(
        body,
        mesh=mesh,
        in_specs=(rows, rows) + (P(),) * 14,
        out_specs=(
            P(None, BOTH), rows, rows,
            P("dp", None), P(), P(),
            P("dp", None), P(), P(),
            P("dp", None), P(), P(),
            P("dp", None), P(), P(),
            P("dp", None),
        ),
        check_vma=False,
    )
```

```python
import functools
import math

import jax
import jax.numpy as jnp
import numpy as np
from jax import lax
from jax.experimental import pallas as pl
from jax.experimental.pallas import tpu as pltpu
from jax.sharding import PartitionSpec as P

VIEWS = 2
CROPS = 4
VSIDE = 7
CSIDE = 3
TAU_INV = 10.0
LOG2E = math.log2(math.e)
EPS = 1e-05
LEN_EPS = 1e-06
BOTH = ("dp", "narrow")
F32 = jnp.float32
BF16 = jnp.bfloat16
MIB = 1 << 20


def round_up(value, step):
    return -(-value // step) * step


def xor_permute(array, offset, count):
    return lax.ppermute(array, BOTH, [(i, i ^ offset) for i in range(count)])


def bit_stages(first, last):
    bits = [1 << b for b in range(first, last)]
    stages = [bits[:1]] if bits else []
    rest = bits[1:]
    while rest:
        stages.append(rest[:2])
        rest = rest[2:]
    return stages


def all_sum(array, count, begun=None):
    for stage in bit_stages(0, count.bit_length() - 1):
        if len(stage) == 1:
            array = array + xor_permute(array, stage[0], count)
            if begun is not None:
                begun(array)
                begun = None
        else:
            low, high = stage
            near = xor_permute(array, low, count)
            far = xor_permute(array, high, count)
            across = xor_permute(array, low ^ high, count)
            array = (array + near) + (far + across)
    return array


def gather_all(array, count):
    parts = [array]
    stages = bit_stages(0, count.bit_length() - 1)
    for stage in stages[:0:-1] + stages[:1]:
        offsets = stage if len(stage) == 1 else [stage[0], stage[1], stage[0] ^ stage[1]]
        block = jnp.stack(parts) if len(parts) > 1 else parts[0][None]
        arrived = [xor_permute(block, off, count) for off in offsets]
        parts = [p for p in parts]
        for got in arrived:
            parts.extend(got[k] for k in range(got.shape[0]))
    return jnp.stack(parts)


def gather_order(count):
    order = [0]
    stages = bit_stages(0, count.bit_length() - 1)
    for stage in stages[:0:-1] + stages[:1]:
        offsets = stage if len(stage) == 1 else [stage[0], stage[1], stage[0] ^ stage[1]]
        order = order + [o ^ off for off in offsets for o in order]
    return np.array(order, np.int32)


def dot(left, right):
    return jnp.dot(left, right, preferred_element_type=F32)


def dot_tn(left, right):
    return lax.dot_general(left, right, (((0,), (0,)), ((), ())), preferred_element_type=F32)


def dot_nt(left, right):
    return lax.dot_general(left, right, (((1,), (1,)), ((), ())), preferred_element_type=F32)


def norm_terms(totals, rows):
    means = totals[0:1] / rows
    variance = totals[1:2] / rows - means * means
    return means, lax.rsqrt(variance + EPS)


def halves(values):
    high = values.astype(BF16)
    return high, (values - high.astype(F32)).astype(BF16)


def col_sums(first, second):
    return jnp.sum(first, axis=0, keepdims=True), jnp.sum(second, axis=0, keepdims=True)


class Sizes:
    def __init__(self, view_rows, crop_rows):
        self.views, self.crops = view_rows, crop_rows
        self.crop_at = round_up(view_rows, 16)
        self.rows = self.crop_at + round_up(crop_rows, 16)

    def row_mask(self):
        row = lax.broadcasted_iota(jnp.int32, (self.rows, 128), 0)
        inside = (row < self.views) | ((row >= self.crop_at) & (row < self.crop_at + self.crops))
        return inside


def wide(mask, cols):
    return jnp.concatenate([mask] * (cols // 128), axis=1)


def fill_edges(edges_ref, sizes):
    for start, stop, at, side in (
        (0, sizes.crop_at, sizes.views, VSIDE),
        (sizes.crop_at, sizes.rows, sizes.crop_at + sizes.crops, CSIDE),
    ):
        count = stop - start
        row = lax.broadcasted_iota(jnp.int32, (count, 128), 0)
        real = row < (at - start)
        rowf = row.astype(F32) + 0.5
        line = jnp.floor(rowf * (1.0 / side))
        col = rowf - 0.5 - line * side
        in_map = line - jnp.floor((line + 0.5) * (1.0 / side)) * side
        keep = (col > 0.5, col < side - 1.5, in_map > 0.5, in_map < side - 1.5)
        for k in range(4):
            edges_ref[k, start:stop, :] = jnp.where(real & keep[k], 1.0, 0.0)
        edges_ref[4, start:stop, :] = jnp.where(real, 1.0, 0.0)


PAD = 16


def tap_block(source_ref, edges_ref, sizes, tap, width):
    dy, dx = tap // 3 - 1, tap % 3 - 1
    pieces = []
    for start, stop, side in ((0, sizes.crop_at, VSIDE), (sizes.crop_at, sizes.rows, CSIDE)):
        shift = dy * side + dx
        values = source_ref[PAD + start + shift : PAD + stop + shift, :]
        mask = None
        for cond, plane in ((dx < 0, 0), (dx > 0, 1), (dy < 0, 2), (dy > 0, 3)):
            if cond:
                edge = edges_ref[plane, start:stop, :]
                mask = edge if mask is None else mask * edge
        if mask is None:
            mask = edges_ref[4, start:stop, :]
        pieces.append((values * wide(mask, width)).astype(BF16))
    return jnp.concatenate(pieces, axis=0)


def k_reduce(xi, xc, w, x, act, stats, flat, *, sizes, steps):
    step = pl.program_id(0)
    micros, _, cols = xc.shape
    views, at = sizes.views, sizes.crop_at
    tiles = cols // 128
    flat[...] = xi[...].astype(F32).reshape(views * micros * tiles, 128)
    for m in range(micros):
        part = [flat[pl.ds(micros * t + m, views, stride=micros * tiles), :] for t in range(tiles)]
        x[m, :at, :] = jnp.concatenate(
            [jnp.concatenate(part, axis=1).astype(BF16), jnp.zeros((at - views, cols), BF16)], axis=0
        )
        tail = sizes.rows - at - sizes.crops
        x[m, at:, :] = jnp.concatenate([xc[m], jnp.zeros((tail, cols), BF16)], axis=0)
    out = dot(together(x), w[...]).reshape(act.shape)

    @pl.when(step == 0)
    def _():
        act[...] = out

    @pl.when(step > 0)
    def _():
        act[...] += out

    @pl.when(step == steps - 1)
    def _():
        put_stats(stats, act, act)


def together(ref):
    return ref[...].reshape(ref.shape[0] * ref.shape[1], ref.shape[2])


def put_stats(stats, first, second):
    for m in range(first.shape[0]):
        a, b = col_sums(first[m], first[m] * second[m])
        stats[m, 0:1, :] = a
        stats[m, 1:2, :] = b


def chunks(rows):
    step = rows // 3 if rows % 48 == 0 else rows
    return [slice(at, at + step) for at in range(0, rows, step)]


def affine(totals, m, gain, shift, rows):
    means, inv = norm_terms(totals[m], rows)
    scale = inv * gain[...]
    return scale, shift[...] - means * scale, inv, -means * inv


def silu(values):
    half = 0.5 * values
    return half + half * jnp.tanh(half)


def twice_slope(values):
    half = 0.5 * values
    turn = jnp.tanh(half)
    return (1.0 + turn) * (1.0 + half * (1.0 - turn))


def back_terms(totals, sums, m, gain, rows):
    means, inv = norm_terms(totals[m], rows)
    a = gain[...] * inv
    mean_s, mean_sn = sums[m, 0:1] / rows, sums[m, 1:2] / rows
    b = -(a * inv) * mean_sn
    return a, b, -(a * mean_s) - b * means


def set_source(source, edges, sizes):
    micros, _, width = source.shape
    fill_edges(edges, sizes)
    for m in range(micros):
        source[m, :PAD, :] = jnp.zeros((PAD, width), F32)
        source[m, PAD + sizes.rows :, :] = jnp.zeros((PAD, width), F32)


def tap_rows(source, edges, sizes, tap):
    micros, _, width = source.shape
    return jnp.concatenate([tap_block(source.at[m], edges, sizes, tap, width) for m in range(micros)], axis=0)


def k_spatial(act, totals, gain, shift, w, hid, act_two, stats, source, edges, *, sizes, rows):
    step = pl.program_id(0)
    micros, _, width = act.shape

    @pl.when(step == 0)
    def _():
        set_source(source, edges, sizes)
        for m in range(micros):
            scale, bias, _, _ = affine(totals, m, gain, shift, rows)
            hidden = silu(act[m] * scale + bias).astype(BF16)
            hid[m] = hidden
            source[m, PAD : PAD + sizes.rows, :] = hidden.astype(F32)

    for dy in range(3):

        @pl.when(step == dy)
        def _(dy=dy):
            for k in range(3):
                tap = 3 * dy + k
                part = dot(tap_rows(source, edges, sizes, tap), w[k * width : (k + 1) * width, :]).reshape(act_two.shape)
                if tap == 0:
                    act_two[...] = part
                else:
                    act_two[...] += part
            if dy == 2:
                put_stats(stats, act_two, act_two)


def k_expand(act, totals, gain, shift, w, hid, stats, *, sizes, rows):
    micros, n, width = act.shape

    @pl.when(pl.program_id(0) == 0)
    def _():
        keep = wide(sizes.row_mask(), width)
        for m in range(micros):
            scale, bias, _, _ = affine(totals, m, gain, shift, rows)
            hid[m] = jnp.where(keep, silu(act[m] * scale + bias), 0.0).astype(BF16)

    out = dot(together(hid), w[...]).reshape(micros, n, -1)
    put_stats(stats, out, out)


def k_pool(hid, w_expand, totals, gain, shift, x, pool, inv_count, w, pooled, head, stats, low, *, rows, steps):
    step = pl.program_id(0)
    micros, own, _ = head.shape
    n = x.shape[1]
    for m in range(micros):
        scale, bias, _, _ = affine(totals, m, gain, shift, rows)
        for part in chunks(n):
            act = dot(hid[m, part, :], w_expand[...])
            low[m, part, :] = silu((act * scale + bias) + x[m, part, :].astype(F32)).astype(BF16)
    low_pooled = (dot(pool[...], together(low)) * inv_count[...]).astype(BF16)
    pooled[...] = low_pooled
    part = dot(low_pooled, w[...])

    @pl.when(step == 0)
    def _():
        for m in range(micros):
            head[m] = part[m * own : (m + 1) * own]

    @pl.when(step > 0)
    def _():
        for m in range(micros):
            head[m] += part[m * own : (m + 1) * own]

    @pl.when(step == steps - 1)
    def _():
        put_stats(stats, head, head)


def head_forward(head, totals, gain, shift, w_embed, count):
    means, inv = norm_terms(totals, count)
    normed = (head - means) * inv
    pre = normed * gain + shift
    hidden = silu(pre).astype(BF16)
    embedding = dot(hidden, w_embed)
    inv_len = lax.rsqrt(jnp.sum(embedding * embedding, axis=1, keepdims=True) + LEN_EPS)
    return normed, pre, inv, hidden, embedding * inv_len, inv_len


def k_embed(where, head, totals, gain, shift, w_embed, pooled, unit_low, *packs_held, count, lines):
    packs, held = packs_held[:-1], packs_held[-1]
    micros, own, width = head.shape
    shard = 4 * lines
    hidden = []
    for m in range(micros):
        _, _, _, hid, unit, _ = head_forward(head[m], totals[m], gain[...], shift[...], w_embed[...], count)
        unit_low[m] = unit.astype(BF16)
        hidden.append(hid.astype(F32))
    both = jnp.concatenate(hidden, axis=0)
    for n in range(4):
        picked = [both[:, s * shard + n * lines : s * shard + (n + 1) * lines] for s in range(width // shard)]
        held[n] = jnp.concatenate(picked, axis=1).astype(BF16)
    chan, sub = pooled.shape[1], held.shape[2]
    for pack, places in zip(packs, ((0,), (1,), (2, 3))):
        pack[:, :chan] = pooled[...]
        for k, place in enumerate(places):
            pack[:, chan + k * sub : chan + (k + 1) * sub] = held[place ^ where[1]]


def k_embed_only(head, totals, gain, shift, w_embed, hidden, unit_low, *, count):
    for m in range(head.shape[0]):
        _, _, _, hid, unit, _ = head_forward(head[m], totals[m], gain[...], shift[...], w_embed[...], count)
        hidden[m] = hid
        unit_low[m] = unit.astype(BF16)


def k_loss(
    units, ids_all, ids_own, pos_all, pos_own, head, totals, gain, shift, w_embed,
    loss, slopes, grad_embed, stats, *, count, loss_scale, block,
):
    everyone = units[0]
    n_all = everyone.shape[0]
    n_own = head.shape[1]

    def terms(start):
        scores = dot_nt(units[0, pl.ds(start, block), :], everyone)
        return jnp.exp2((scores - 1.0) * (TAU_INV * LOG2E))

    if n_all <= 16 * block:
        total = None
        apart = lax.broadcasted_iota(jnp.int32, (block, block), 0) != lax.broadcasted_iota(jnp.int32, (block, block), 1)
        for k in range(n_all // block):
            row = terms(k * block)
            here = slice(k * block, (k + 1) * block)
            pieces = [row[:, : here.start], jnp.where(apart, row[:, here], 0.0), row[:, here.stop :]]
            row = jnp.concatenate([p for p in pieces if p.shape[1]], axis=1)
            row = jnp.sum(row.reshape(block // 8, 8, n_all), axis=0)
            total = row if total is None else total + row
        sums = jnp.sum(total, axis=0, keepdims=True)
    else:

        def add_rows(k, sums):
            start = pl.multiple_of(k * block, block)
            mine = lax.broadcasted_iota(jnp.int32, (block, n_all), 0) + start
            other = lax.broadcasted_iota(jnp.int32, (block, n_all), 1)
            return sums + jnp.sum(jnp.where(mine == other, 0.0, terms(start)), axis=0, keepdims=True)

        sums = lax.fori_loop(0, n_all // block, add_rows, jnp.zeros((1, n_all), F32))
    log_all = jnp.log(sums) + TAU_INV
    normed, pre, inv, hid, unit, inv_len = head_forward(
        head[0], totals[0], gain[...], shift[...], w_embed[...], count
    )
    low = unit.astype(BF16)
    scores = dot_nt(low, everyone) * TAU_INV
    itself = lax.broadcasted_iota(jnp.int32, (n_own, n_all), 0) == lax.broadcasted_iota(
        jnp.int32, (n_own, n_all), 1
    )
    own_sum = jnp.sum(jnp.where(itself, 0.0, jnp.exp(scores - TAU_INV)), axis=1, keepdims=True)
    log_own = jnp.log(own_sum) + TAU_INV
    positive = (ids_own[0] == ids_all[0]) & jnp.logical_not(itself)
    pos_sum = jnp.sum(jnp.where(positive, scores, 0.0), axis=1, keepdims=True)
    loss[0] = log_own - pos_sum * pos_own[0]
    by_row = jnp.where(itself, 0.0, jnp.exp(scores - log_own)) - jnp.where(positive, pos_own[0], 0.0)
    by_col = jnp.where(itself, 0.0, jnp.exp(scores - log_all)) - jnp.where(positive, pos_all[0], 0.0)
    grad_unit = (
        dot((by_row * loss_scale).astype(BF16), everyone)
        + dot((by_col * loss_scale).astype(BF16), everyone)
    ) * TAU_INV
    grad = inv_len * (grad_unit - unit * jnp.sum(unit * grad_unit, axis=1, keepdims=True))
    grad_low = grad.astype(BF16)
    grad_embed[0] = grad_low
    slope = dot_nt(grad_low, w_embed[...]) * (0.5 * twice_slope(pre))
    slopes[0] = slope
    a, b = col_sums(slope, slope * normed)
    stats[0, 0:1, :] = a
    stats[0, 1:2, :] = b


def k_head_back(where, slopes, head, totals, sums, gain, embed, grad, *packs, count):
    micros, own, width = head.shape
    rows = []
    for m in range(micros):
        a, b, c = back_terms(totals, sums, m, gain, count)
        rows.append(slopes[m] * a + head[m] * b + c)
    grad[...] = jnp.concatenate(rows, axis=0).astype(BF16)
    if packs:
        emb = jnp.concatenate([embed[m].astype(F32) for m in range(micros)], axis=0).astype(BF16)
        quarter = width // 4
        for place, pack in enumerate(packs):
            at = pl.multiple_of((place ^ where[1]) * quarter, quarter)
            pack[:, :quarter] = grad[:, pl.ds(at, quarter)]
            pack[:, quarter:] = emb


def k_back_pool(grad_head, hid, w_expand, totals, gain, shift, x, spread, half_count, w, grad_resid, stats, *, rows):
    micros, n, cols = x.shape
    pair = jnp.concatenate(halves(dot_nt(grad_head[...], w[...]) * half_count[...]), axis=0)
    for m in range(micros):
        scale, bias, inv, offset = affine(totals, m, gain, shift, rows)
        sums = None
        for part in chunks(n):
            act = dot(hid[m, part, :], w_expand[...])
            back = dot(spread[m * n + part.start : m * n + part.stop, :], pair)
            slope = back * twice_slope((act * scale + bias) + x[m, part, :].astype(F32))
            grad_resid[m, part, :] = slope.astype(BF16)
            more = col_sums(slope, slope * (act * inv + offset))
            sums = more if sums is None else (sums[0] + more[0], sums[1] + more[1])
        stats[m, 0:1, :] = sums[0]
        stats[m, 1:2, :] = sums[1]


def k_back_expand(
    where, grad_resid, hid, tot_three, sum_three, gain_three, w, act_two, tot_two, gain_two, shift_two,
    slopes, stats, *rest, sizes, rows, steps, shares,
):
    step = pl.program_id(0)
    micros, n, mid = hid.shape
    if shares:
        keep, send, low, turned = rest

        @pl.when(step == 0)
        def _():
            for m in range(micros):
                turned[:, m * n : (m + 1) * n] = hid[m].T

    else:
        (low,) = rest

    @pl.when(step == 0)
    def _():
        slopes[...] = jnp.zeros(slopes.shape, F32)

    for m in range(micros):
        a, b, c = back_terms(tot_three, sum_three, m, gain_three, rows)
        for part in chunks(n):
            act = dot(hid[m, part, :], w[...])
            grad = (grad_resid[m, part, :].astype(F32) * a + (act * b + c)).astype(BF16)
            low[m, part, :] = grad
            slopes[m, part, :] += dot_nt(grad, w[...])

    if shares:
        share = dot(turned[...], together(low)).astype(BF16)
        each = mid // 8
        for out, even in ((keep, 0), (send, 1)):

            @pl.when(step % 2 == even)
            def _(out=out):
                for shard in range(8):
                    place = shard ^ where[0]
                    out[place % 2, place // 2, 0] = share[shard * each : (shard + 1) * each]

    @pl.when(step == steps - 1)
    def _():
        finish_slopes(slopes, stats, act_two, tot_two, gain_two, shift_two, rows, wide(sizes.row_mask(), mid))


def finish_slopes(slopes, stats, act, totals, gain, shift, rows, keep=None):
    for m in range(slopes.shape[0]):
        scale, bias, inv, offset = affine(totals, m, gain, shift, rows)
        slope = slopes[m] * (0.5 * twice_slope(act[m] * scale + bias))
        if keep is not None:
            slope = jnp.where(keep, slope, 0.0)
        slopes[m] = slope
        a, b = col_sums(slope, slope * (act[m] * inv + offset))
        stats[m, 0:1, :] = a
        stats[m, 1:2, :] = b


UNIT = 64
UNITS_A = 5


def k_back_spatial(
    where, slopes, act_two, tot_two, sum_two, gain_two, w, act_one, tot_one, gain_one, shift_one, hid,
    slopes_one, stats, *rest, sizes, rows, shares,
):
    if shares:
        keep_a, send_a, keep_b, send_b, source, edges, turned, block = rest
        core, line = where[1] % 2, where[1] // 2
    else:
        grad_two, source, edges = rest
    step = pl.program_id(0)
    micros, n, mid = act_two.shape

    @pl.when(step == 0)
    def _():
        set_source(source, edges, sizes)
        for m in range(micros):
            a, b, c = back_terms(tot_two, sum_two, m, gain_two, rows)
            low = (slopes[m] * a + (act_two[m] * b + c)).astype(BF16)
            source[m, PAD : PAD + sizes.rows, :] = low.astype(F32)
            if shares:
                turned[:, m * n : (m + 1) * n] = hid[m].T
            else:
                grad_two[m] = low

    def share(tap, here):
        part = dot(turned[...], here)
        for q in range(4):
            block[q] = part[:, 128 * q : 128 * (q + 1)].astype(BF16)
        for unit in range(8 * (8 - tap), 8 * (9 - tap)):
            shard, k = divmod(unit, 9)
            place = shard ^ where[0]
            lines = slice(UNIT * (unit % 8), UNIT * (unit % 8 + 1))
            for y in range(2):
                for out_a, out_b, c in ((keep_a, keep_b, core), (send_a, send_b, 1 - core)):
                    piece = block[2 * y + c, lines, :]
                    if k < UNITS_A:
                        out_a[place % 2, place // 2, y ^ line, k * UNIT : (k + 1) * UNIT, :] = piece
                    else:
                        at = (k - UNITS_A) * UNIT
                        out_b[y ^ line, place % 2, place // 2, at : at + UNIT, :] = piece

    for dy in range(3):

        @pl.when(step == dy)
        def _(dy=dy):
            for k in range(3):
                tap = 3 * dy + k
                here = tap_rows(source, edges, sizes, tap)
                part = dot_nt(here, w[(2 - k) * mid : (3 - k) * mid, :]).reshape(slopes_one.shape)
                if tap == 0:
                    slopes_one[...] = part
                else:
                    slopes_one[...] += part
                if shares:
                    share(tap, here)
            if dy == 2:
                finish_slopes(slopes_one, stats, act_one, tot_one, gain_one, shift_one, rows)


def k_weight_hidden(where, *refs):
    rows, packs = refs[:4], refs[4:8]
    subs = refs[8:12]
    keep, send, grads, extra, held = refs[12:]
    step = pl.program_id(0)
    quarter = keep.shape[2]

    @pl.when(step == 0)
    def _():
        total = None
        for k in range(4):
            n = packs[k].shape[0]
            grads[k * n : (k + 1) * n, :] = packs[k][:, :quarter].astype(F32)
            part = dot_tn(subs[k][...], packs[k][:, quarter:])
            total = part if total is None else total + part
        extra[...] = total.astype(BF16).reshape(extra.shape)

    pooled = jnp.concatenate([r[...].astype(F32) for r in rows], axis=0).astype(BF16)
    held[...] = dot_tn(pooled, grads[...].astype(BF16)).astype(BF16).reshape(held.shape)
    shard = held.shape[1]
    for x, ref in ((0, keep), (1, send)):
        more = extra[(2 * step + x) ^ where[0]]
        lines = more.shape[0] // 4
        ref[0, :shard, :] = held[x ^ (where[0] % 2)]
        for k in range(4):
            ref[0, shard:, 128 * k : 128 * (k + 1)] = more[lines * k : lines * (k + 1), :]


def k_weight_reduce(
    where, x, slopes, act, totals, sums, gain, grad, keep, send, turned, block, *, rows
):
    micros, n, mid = slopes.shape
    core, line = where[1] % 2, where[1] // 2

    @pl.when(pl.program_id(0) == 0)
    def _():
        for m in range(micros):
            a, b, c = back_terms(totals, sums, m, gain, rows)
            low = (slopes[m] * a + (act[m] * b + c)).astype(BF16)
            grad[m] = low
            turned[:, m * n : (m + 1) * n] = low.T

    total = dot(turned[...], together(x)).astype(BF16).T
    for q in range(4):
        block[q] = total[:, 128 * q : 128 * (q + 1)]
    for y in range(2):
        for out, c in ((keep, core), (send, 1 - core)):
            out[0, 0, y ^ line] = block[2 * y + c]


def k_grad_one(slopes, act, totals, sums, gain, grad, *, rows):
    for m in range(slopes.shape[0]):
        a, b, c = back_terms(totals, sums, m, gain, rows)
        grad[m] = (slopes[m] * a + (act[m] * b + c)).astype(BF16)


def k_back_reduce(grad_one, w, grad_resid, *refs, sizes):
    grad_v, grad_c = refs[-2:]
    views, lines, _ = grad_v.shape
    micros = grad_one.shape[0]
    flat = grad_v.reshape(views * lines, 128)
    at = sizes.crop_at
    n = sizes.rows
    back = dot_nt(together(grad_one), w[...])
    for m in range(micros):
        both = grad_resid[m].astype(F32) + back[m * n : (m + 1) * n]
        grad_c[m] = both[at : at + sizes.crops]
        for t in range(lines // micros):
            flat[pl.ds(micros * t + m, views, stride=lines), :] = both[:views, 128 * t : 128 * (t + 1)]


def call(kernel, name, grid, ins, outs, scratch=(), flops=0, vmem=44, where=None, aliases=None):
    spec = lambda block, index: pl.BlockSpec(block, index) if block else pl.BlockSpec(memory_space=pl.ANY)
    scalars = [] if where is None else [where]
    moved = sum(a.size * a.dtype.itemsize for a, _, _ in ins) + sum(
        math.prod(s) * jnp.dtype(t).itemsize for s, t, _, _ in outs
    )
    return pl.pallas_call(
        kernel,
        grid_spec=pltpu.PrefetchScalarGridSpec(
            num_scalar_prefetch=len(scalars),
            grid=grid,
            in_specs=[spec(b, i) for _, b, i in ins],
            out_specs=[spec(b, i) for _, _, b, i in outs],
            scratch_shapes=list(scratch),
        ),
        out_shape=[jax.ShapeDtypeStruct(s, t) for s, t, _, _ in outs],
        compiler_params=pltpu.CompilerParams(vmem_limit_bytes=vmem * MIB),
        cost_estimate=pl.CostEstimate(flops=1000, bytes_accessed=1000, transcendentals=0),
        name=name,
        input_output_aliases=aliases or {},
    )(*scalars, *[a for a, _, _ in ins])


def exact(array):
    return lax.optimization_barrier(array)


def add_low(*parts):
    total = parts[0].astype(F32)
    for part in parts[1:]:
        total = total + part.astype(F32)
    return total.astype(BF16)


def reduce_weight(grad, count, data_size, narrow_size):
    rows, cols = grad.shape
    me = lax.axis_index("dp")
    core = lax.axis_index("narrow") % 2
    blocks = grad.reshape(data_size, rows // data_size, cols)
    blocks = jnp.stack(
        [lax.dynamic_index_in_dim(blocks, me ^ j, axis=0, keepdims=False) for j in range(data_size)]
    )
    half = cols // 2
    low, high = blocks[:, :, :half], blocks[:, :, half:]
    keep = jnp.where(core == 0, low, high)
    send = jnp.where(core == 0, high, low)
    part = add_low(keep, xor_permute(send, 1, count))
    size = data_size
    for stage in bit_stages(0, data_size.bit_length() - 1):
        if len(stage) == 1:
            split = part.reshape((size // 2, 2) + part.shape[1:])
            part = add_low(split[:, 0], xor_permute(split[:, 1], stage[0] * narrow_size, count))
            size //= 2
        else:
            split = part.reshape((size // 4, 4) + part.shape[1:])
            got = [
                xor_permute(split[:, k], off * narrow_size, count)
                for k, off in ((1, stage[0]), (2, stage[1]), (3, stage[0] ^ stage[1]))
            ]
            part = add_low(split[:, 0], *got)
            size //= 4
    part = exact(part[0])
    off = 2
    while off < narrow_size:
        part = exact(add_low(part, xor_permute(part, off, count)))
        off *= 2
    other = xor_permute(part, 1, count)
    both = jnp.where(
        core == 0, jnp.concatenate([part, other], axis=1), jnp.concatenate([other, part], axis=1)
    )
    return both.astype(F32)


class Mesh84:
    core, line, x, z = 1, 2, 4, 8

    def __init__(self, count):
        self.count = count

    def send(self, array, offset):
        return xor_permute(array, offset, self.count)

    def split(self, keep, got):
        return [add_low(keep[k], got[k]) for k in range(keep.shape[0])]

    def across_z(self, parts, *others):
        sent = [after(p, *others) if others else p for p in parts[1:]]
        return [parts[0]] + [self.send(sent[k - 1], self.z * k) for k in (1, 2, 3)]

    def quarters(self, near, far, narrow):
        places = (near[0], far[0], near[1], far[1])
        pick = lambda q: lax.select_n(narrow, *(places[q ^ n] for n in range(4)))
        return jnp.concatenate([pick(q) for q in range(4)], axis=-1)


def after(value, *others):
    return lax.optimization_barrier((value, *others))[0]


def hidden_share(rows, packs, where):
    total, wide_cols = rows[0].shape
    chan = wide_cols * 4 // 5
    sub = wide_cols - chan
    emb = packs[0].shape[1] - sub
    shard = chan // 8
    extra = sub // 8 * emb // sub
    fix = lambda i, w: (0, 0)
    out = ((4, shard + extra, sub), BF16, (1, shard + extra, sub), lambda i, w: (i, 0, 0))
    return call(
        k_weight_hidden, "weight_hidden", (4,),
        [(r, (total, 2 * shard), lambda i, w: (0, i ^ (w[0] // 2))) for r in rows]
        + [(p, p.shape, fix) for p in packs]
        + [(r, (total, sub), lambda i, w: (0, chan // sub)) for r in rows],
        [out, out],
        scratch=[
            pltpu.VMEM((4 * total, sub), F32),
            pltpu.VMEM((8, sub // 8, emb), BF16),
            pltpu.VMEM((2, shard, sub), BF16),
        ],
        flops=8 * total * chan * sub,
        where=where,
    )


def spread_taps(hidden, side):
    padded = jnp.pad(hidden, ((0, 0), (1, 1), (1, 1), (0, 0)))
    pieces = [padded[:, dy : dy + side, dx : dx + side, :] for dy in range(3) for dx in range(3)]
    return jnp.concatenate(pieces, axis=-1)


def body(
    view_maps, crop_maps, image_ids, w_reduce, gain_one, shift_one, w_spatial, gain_two, shift_two,
    w_expand, gain_three, shift_three, w_hidden, gain_head, shift_head, w_embed,
):
    micros, view_rows, channels = view_maps.shape
    crop_rows = crop_maps.shape[1]
    mid = w_reduce.shape[1]
    hidden_width = w_hidden.shape[1]
    emb_width = w_embed.shape[1]
    images_dev = view_rows // (VIEWS * VSIDE * VSIDE)
    each = VIEWS + CROPS
    own = images_dev * each
    data_size, narrow_size = lax.axis_size("dp"), lax.axis_size("narrow")
    count = data_size * narrow_size
    emb_total = own * count
    pixel_count = (view_rows + crop_rows) * count
    loss_scale = 1.0 / (micros * emb_total)
    device = lax.axis_index("dp") * narrow_size + lax.axis_index("narrow")
    sizes = Sizes(view_rows, crop_rows)
    rows = sizes.rows

    pool = np.zeros((micros, own, micros, rows), np.float32)
    for m in range(micros):
        for r in range(view_rows):
            image, view = divmod(r // (VSIDE * VSIDE), VIEWS)
            pool[m, image * each + view, m, r] = 1
        for r in range(crop_rows):
            image, crop = divmod(r // (CSIDE * CSIDE), CROPS)
            pool[m, image * each + VIEWS + crop, m, sizes.crop_at + r] = 1
    pool = pool.reshape(micros * own, micros * rows)
    inv_count = np.where(np.arange(micros * own) % each < VIEWS, 1.0 / VSIDE**2, 1.0 / CSIDE**2)[:, None]
    spread = jnp.asarray(np.concatenate([pool.T, pool.T], axis=1), BF16)
    pool = jnp.asarray(pool, BF16)
    half_count = jnp.asarray(0.5 * inv_count, F32)
    inv_count = jnp.asarray(inv_count, F32)

    place = jnp.asarray(gather_order(count)) ^ device
    same = jnp.sum((image_ids[:, :, None] == image_ids[:, None, :]).astype(F32), axis=2)
    inv_pos = 1.0 / (same * each - 1.0)

    from_device = place[:, None] == jnp.arange(count, dtype=jnp.int32)[None, :]

    def by_place(values):
        blocks = values.reshape(micros, 1, count, images_dev)
        moved = jnp.sum(jnp.where(from_device[None, :, :, None], blocks, 0), axis=2)
        return jnp.repeat(moved.reshape(micros, -1), each, axis=1)

    ids_all, pos_all = by_place(image_ids), by_place(inv_pos)
    ids_own, pos_own = ids_all[:, :own, None], pos_all[:, :own, None]
    ids_all, pos_all = ids_all[:, None, :], pos_all[:, None, :]

    row = lambda v: v.reshape(1, -1)
    g1, b1, g2, b2 = row(gain_one), row(shift_one), row(gain_two), row(shift_two)
    g3, b3, gh, bh = row(gain_three), row(shift_three), row(gain_head), row(shift_head)
    reduce_all = lambda stats: all_sum(stats, count)
    flops = 2.0 * micros * rows * channels * mid

    fast = data_size == 8 and narrow_size == 4 and mid == 512 and micros == 2
    dp, narrow = lax.axis_index("dp"), lax.axis_index("narrow")
    where = jnp.stack([dp, narrow]).astype(jnp.int32)
    net = Mesh84(count)
    blk = 512
    steps = channels // blk
    fix2 = lambda *_: (0, 0)
    fix3 = lambda *_: (0, 0, 0)
    col = lambda n, *_: (0, n)
    col3 = lambda n, *_: (0, 0, n)
    row = lambda n, *_: (n, 0)
    m0 = lambda m, *_: (m, 0, 0)
    act_mid = (micros, rows, mid)
    two = lambda array: (array, array.shape, fix3)
    vec = lambda array: (array, array.shape, fix2)
    vec_block = lambda array: (array, (1, blk), col)
    tot_block = lambda array: (array, (micros, 2, blk), col3)
    stats_of = lambda width: ((micros, 2, width), F32, (micros, 2, width), fix3)

    tiles = channels // 128
    mixed = jnp.transpose(view_maps.reshape(micros, view_rows, tiles, 128), (1, 2, 0, 3))
    mixed = mixed.reshape(view_rows, micros * tiles, 128)
    lines = micros * blk // 128
    pixels, act_one, st = call(
        functools.partial(k_reduce, sizes=sizes, steps=steps), "reduce", (steps,),
        [
            (mixed, (view_rows, lines, 128), lambda n: (0, n, 0)),
            (crop_maps, (micros, crop_rows, blk), col3),
            (w_reduce, (blk, mid), row),
        ],
        [
            ((micros, rows, channels), BF16, (micros, rows, blk), col3),
            (act_mid, F32, act_mid, fix3),
            stats_of(mid),
        ],
        scratch=[pltpu.VMEM((view_rows * lines, 128), F32)],
        flops=flops,
    )
    tot_one = reduce_all(st)
    taps_scratch = [
        pltpu.VMEM((micros, rows + 2 * PAD, mid), F32),
        pltpu.VMEM((5, rows, 128), F32),
    ]
    hid_one, act_two, st = call(
        functools.partial(k_spatial, sizes=sizes, rows=pixel_count), "spatial", (3,),
        [two(act_one), two(tot_one), vec(g1), vec(b1), (w_spatial, (3 * mid, mid), row)],
        [(act_mid, BF16, act_mid, fix3), (act_mid, F32, act_mid, fix3), stats_of(mid)],
        scratch=taps_scratch,
        flops=flops * 9 * mid / channels,
    )
    tot_two = reduce_all(st)
    hid_two, st = call(
        functools.partial(k_expand, sizes=sizes, rows=pixel_count), "expand", (steps,),
        [two(act_two), two(tot_two), vec(g2), vec(b2), (w_expand, (mid, blk), col)],
        [(act_mid, BF16, act_mid, fix3), ((micros, 2, channels), F32, (micros, 2, blk), col3)],
        flops=flops,
    )
    tot_three = reduce_all(st)
    ids_all, ids_own, pos_all, pos_own, hid_two = exact((ids_all, ids_own, pos_all, pos_own, hid_two))
    flat_own = micros * own
    pooled, head, st = call(
        functools.partial(k_pool, rows=pixel_count, steps=steps), "pool", (steps,),
        [
            two(hid_two),
            (w_expand, (mid, blk), col),
            tot_block(tot_three),
            vec_block(g3),
            vec_block(b3),
            (pixels, (micros, rows, blk), col3),
            vec(pool),
            vec(inv_count),
            (w_hidden, (blk, hidden_width), row),
        ],
        [
            ((flat_own, channels), BF16, (flat_own, blk), col),
            ((micros, own, hidden_width), F32, (micros, own, hidden_width), fix3),
            stats_of(hidden_width),
        ],
        scratch=[pltpu.VMEM((micros, rows, blk), BF16)],
        flops=flops,
    )
    tot_head = reduce_all(st)
    head_in = [two(head), two(tot_head), vec(gh), vec(bh), vec(w_embed)]
    unit_shape = (micros, own, emb_width)
    if fast:
        sub = hidden_width // 4
        pack = (flat_own, channels + sub)
        unit_low, *rows_packs = call(
            functools.partial(k_embed, count=emb_total, lines=sub // 8), "embed", (1,), head_in + [vec(pooled)],
            [(unit_shape, BF16, unit_shape, fix3)] + [(pack, BF16, pack, fix2)] * 2
            + [((flat_own, channels + 2 * sub), BF16, (flat_own, channels + 2 * sub), fix2)],
            scratch=[pltpu.VMEM((4, flat_own, sub), BF16)],
            where=where,
        )
    else:
        head_hid, unit_low = call(
            functools.partial(k_embed_only, count=emb_total), "embed", (1,), head_in,
            [
                ((micros, own, hidden_width), BF16, (micros, own, hidden_width), fix3),
                (unit_shape, BF16, unit_shape, fix3),
            ],
        )
    units = gather_all(unit_low, count)
    units = jnp.transpose(units, (1, 0, 2, 3)).reshape(micros, emb_total, emb_width)
    if fast:
        pack_own, pack_core, pack_line = (after(p, units) for p in rows_packs)
        got_core = net.send(pack_core, net.core)
        got_line = net.send(pack_line, net.line)
    loss, slopes, grad_embed, st = call(
        functools.partial(k_loss, count=emb_total, loss_scale=loss_scale, block=128), "loss", (micros,),
        [
            (units, (1, emb_total, emb_width), m0),
            (ids_all, (1, 1, emb_total), m0),
            (ids_own, (1, own, 1), m0),
            (pos_all, (1, 1, emb_total), m0),
            (pos_own, (1, own, 1), m0),
            (head, (1, own, hidden_width), m0),
            (tot_head, (1, 2, hidden_width), m0),
            vec(gh),
            vec(bh),
            vec(w_embed),
        ],
        [
            ((micros, own, 1), F32, (1, own, 1), m0),
            ((micros, own, hidden_width), F32, (1, own, hidden_width), m0),
            (unit_shape, BF16, (1, own, emb_width), m0),
            ((micros, 2, hidden_width), F32, (1, 2, hidden_width), m0),
        ],
    )
    if fast:
        got_core, got_line = (after(g, st) for g in (got_core, got_line))
        st = after(st, got_line)
        wide_cols = channels + sub
        pass_on = jnp.concatenate([got_line[:, :channels], got_line[:, wide_cols:]], axis=1)
        rows_packs = [pack_own, got_core, got_line[:, :wide_cols], net.send(pass_on, net.core)]
    sum_head = reduce_all(st)

    grad_head, *packs = call(
        functools.partial(k_head_back, count=emb_total), "head_back", (1,),
        [two(slopes), two(head), two(tot_head), two(sum_head), vec(gh), two(grad_embed)],
        [((flat_own, hidden_width), BF16, (flat_own, hidden_width), fix2)]
        + [((flat_own, hidden_width // 4 + emb_width), BF16, (flat_own, hidden_width // 4 + emb_width), fix2)]
        * (4 if fast else 0),
        where=where,
    )
    if fast:
        packs = packs[:1] + [net.send(packs[k], k) for k in (1, 2, 3)]
    grad_resid, st = call(
        functools.partial(k_back_pool, rows=pixel_count), "back_pool", (steps,),
        [
            vec(grad_head),
            two(hid_two),
            (w_expand, (mid, blk), col),
            tot_block(tot_three),
            vec_block(g3),
            vec_block(b3),
            (pixels, (micros, rows, blk), col3),
            vec(spread),
            vec(half_count),
            (w_hidden, (blk, hidden_width), row),
        ],
        [
            ((micros, rows, channels), BF16, (micros, rows, blk), col3),
            ((micros, 2, channels), F32, (micros, 2, blk), col3),
        ],
        flops=flops,
    )
    if fast:
        packs = packs[:1] + [after(g, st) for g in packs[1:]]
        wh_keep, wh_send = hidden_share(rows_packs, packs, where)
    sum_three = reduce_all(st)
    if fast:
        wh_got = net.send(after(wh_send, sum_three), net.x)
        grad_resid = after(grad_resid, wh_send, wh_keep)
    turn = (lambda n, w: n ^ w[1]) if fast else (lambda n, w: n)
    turn3 = lambda n, w: (0, 0, turn(n, w))
    turn2 = lambda n, w: (0, turn(n, w))
    w3_share = (2, 4, 2, mid // 8, blk)
    w3_out = (w3_share, BF16, (2, 4, 1, mid // 8, blk), lambda n, w: (0, 0, n // 2, 0, 0))
    slopes_two, st, *rest = call(
        functools.partial(k_back_expand, sizes=sizes, rows=pixel_count, steps=steps, shares=fast), "back_expand", (steps,),
        [
            (grad_resid, (micros, rows, blk), turn3),
            two(hid_two),
            (tot_three, (micros, 2, blk), turn3),
            (sum_three, (micros, 2, blk), turn3),
            (g3, (1, blk), turn2),
            (w_expand, (mid, blk), turn2),
            two(act_two),
            two(tot_two),
            vec(g2),
            vec(b2),
        ],
        [(act_mid, F32, act_mid, fix3), stats_of(mid)]
        + ([w3_out, w3_out] if fast else [((micros, rows, channels), BF16, (micros, rows, blk), turn3)]),
        scratch=[pltpu.VMEM((micros, rows, blk), BF16), pltpu.VMEM((mid, micros * rows), BF16)] if fast else [],
        flops=2 * flops,
        where=where,
    )
    if fast:
        w3_keep, w3_send = rest
        w3_got = net.send(w3_send, net.core)
        wh_z = net.split(wh_keep, after(wh_got, st, w3_send))
        w3_x = net.split(w3_keep, w3_got)
        st = after(st, wh_got)
    else:
        (w3_full,) = rest
    sum_two = reduce_all(st)
    if fast:
        wh_got = net.across_z(wh_z, sum_two)
        w3_got = net.send(after(w3_x[1], sum_two), net.x)
        slopes_two = after(slopes_two, *wh_z, *w3_x)
    shapes = [(2, 4, 2, UNITS_A * UNIT, 128)] * 2 + [(2, 2, 4, (9 - UNITS_A) * UNIT, 128)] * 2
    slopes_one, st, *rest = call(
        functools.partial(k_back_spatial, sizes=sizes, rows=pixel_count, shares=fast), "back_spatial", (3,),
        [
            two(slopes_two),
            two(act_two),
            two(tot_two),
            two(sum_two),
            vec(g2),
            (w_spatial, (3 * mid, mid), lambda n, *_: (2 - n, 0)),
            two(act_one),
            two(tot_one),
            vec(g1),
            vec(b1),
            two(hid_one),
        ],
        [(act_mid, F32, act_mid, fix3), stats_of(mid)]
        + ([(t, BF16, t, lambda *_: (0,) * 5) for t in shapes] if fast else [(act_mid, BF16, act_mid, fix3)]),
        scratch=taps_scratch
        + ([pltpu.VMEM((mid, micros * rows), BF16), pltpu.VMEM((4, mid, 128), BF16)] if fast else []),
        flops=2 * flops * 9 * mid / channels,
        where=where,
    )
    if fast:
        w2_keep_a, w2_send_a, w2_keep_b, w2_send_b = rest
        wh_part = exact(add_low(*(after(g, st) for g in wh_got)))
        w3_z = net.split(w3_x[0], after(w3_got, st))
        st = after(st, *wh_got, w3_got)
        first = []
        sum_one = all_sum(st, count, first.append)
        w2_got_a, w2_got_b = (net.send(after(g, *first), net.core) for g in (w2_send_a, w2_send_b))
        w2_x = net.split(w2_keep_a, w2_got_a)
        w2_y = net.split(w2_keep_b, w2_got_b)
        w2_got_a = net.send(after(w2_x[1], sum_one), net.x)
        w2_got_b = net.send(after(w2_y[1], sum_one), net.line)
        w3_got = net.across_z(w3_z, sum_one)
    else:
        sum_one = reduce_all(st)
    one_in = [two(slopes_one), two(act_one), two(tot_one), two(sum_one), vec(g1)]
    if fast:
        one_in[0] = two(after(slopes_one, *w3_z, *w2_x, *w2_y, wh_part))
        shard = channels // 8
        out = ((2, 4, 2, shard, 128), BF16, (1, 1, 2, shard, 128), lambda j, w: (j % 2, j // 2, 0, 0, 0))
        grad_one, w1_keep, w1_send = call(
            functools.partial(k_weight_reduce, rows=pixel_count), "weight_reduce", (8,),
            [(pixels, (micros, rows, shard), lambda j, w: (0, 0, j ^ w[0]))] + one_in,
            [(act_mid, BF16, act_mid, fix3), out, out],
            scratch=[pltpu.VMEM((mid, micros * rows), BF16), pltpu.VMEM((4, shard, 128), BF16)],
            flops=flops,
            where=where,
        )
        w1_got = net.send(w1_send, net.core)
        w2_got_a, w2_got_b, *w3_got, _ = exact((w2_got_a, w2_got_b, *w3_got, w1_send))
        w2_z = net.split(w2_x[0], w2_got_a)
        w2_x = net.split(w2_y[0], w2_got_b)
        w3_part = exact(add_low(*w3_got))
        w2_got_a = net.across_z(w2_z)
        w2_got_b = net.send(w2_x[1], net.x)
        w3_line = net.send(w3_part, net.line)
        grad_one = after(grad_one, *w2_z, *w2_x, w3_part)
    else:
        (grad_one,) = call(
            functools.partial(k_grad_one, rows=pixel_count), "grad_one", (1,), one_in, [(act_mid, BF16, act_mid, fix3)]
        )
    def back_reduce(first, grads, before=()):
        at = lambda n: n + first
        return call(
            functools.partial(k_back_reduce, sizes=sizes), "back_reduce", (steps // 2,),
            [
                two(grads),
                (w_reduce, (blk, mid), lambda n: (at(n), 0)),
                (grad_resid, (micros, rows, blk), lambda n: (0, 0, at(n))),
            ]
            + [(b, None, None) for b in before],
            [
                ((view_rows, micros * tiles, 128), F32, (view_rows, lines, 128), lambda n: (0, at(n), 0)),
                (crop_maps.shape, F32, (micros, crop_rows, blk), lambda n: (0, 0, at(n))),
            ],
            flops=flops / 2,
            aliases={3 + k: k for k in range(len(before))},
        )

    grad_views, grad_crops = back_reduce(0, grad_one)
    if fast:
        w1_got, w2_got_b, w3_line, *w2_got_a, grad_crops = exact((w1_got, w2_got_b, w3_line, *w2_got_a, grad_crops))
        w1_x = net.split(w1_keep, w1_got)
        w1_got = net.send(w1_x[1], net.x)
        w2_bz = net.split(w2_x[0], w2_got_b)
        w2_got_b = net.across_z(w2_bz)
        w2_a = exact(add_low(*w2_got_a))
        w2_got_a = net.send(w2_a, net.line)
        w3_part = exact(add_low(w3_part, w3_line[::-1]))
        w3_far = net.send(w3_part, net.core)
        wh_line = net.send(after(wh_part, grad_crops), net.line)
        grad_one = after(grad_one, *w1_x, *w2_bz, w2_a, w3_part)
    grad_views, grad_crops = back_reduce(steps // 2, grad_one, (grad_views, grad_crops))
    grad_views = jnp.transpose(grad_views.reshape(view_rows, tiles, micros, 128), (2, 0, 1, 3)).reshape(view_maps.shape)

    if fast:
        w1_got, w2_got_a, wh_line, w3_far, *w2_got_b, grad_crops = exact(
            (w1_got, w2_got_a, wh_line, w3_far, *w2_got_b, grad_crops)
        )
        w1_got = net.across_z(net.split(w1_x[0], w1_got))
        w2_b = exact(add_low(*w2_got_b))
        w2_a = exact(add_low(w2_a, w2_got_a[::-1]))
        wh_pair = jnp.stack([wh_part, wh_line])
        arrived = exact((*w1_got, net.send(w2_b, net.line), net.send(w2_a, net.core), net.send(wh_pair, net.core)))
        w1_part = exact(add_low(*arrived[:4]))
        w2_pair = jnp.stack([w2_b, arrived[4]])
        w2_a_far, wh_far = arrived[5:]
        w1_line, w2_b_far = exact((net.send(w1_part, net.line), net.send(w2_pair, net.core)))
        w1_part = exact(add_low(w1_part, w1_line[::-1]))
        w1_far = net.send(w1_part, net.core)
        lines = w_hidden.shape[0] // data_size
        gw_hidden = net.quarters(wh_pair[:, :lines], wh_far[:, :lines], narrow).astype(F32)
        extra = net.quarters(wh_pair[:, lines:], wh_far[:, lines:], narrow)
        extra = extra.reshape(-1, 4, 4, emb_width)
        gw_embed = jnp.transpose(extra, (1, 2, 0, 3)).reshape(-1, emb_width).astype(F32)
        gw_expand = net.quarters(w3_part, w3_far, narrow).astype(F32)
        w2 = [net.quarters(w2_a, w2_a_far, narrow), net.quarters(w2_pair, w2_b_far, narrow)]
        gw_spatial = jnp.concatenate(w2, axis=0).astype(F32)
        gw_reduce = net.quarters(w1_part, w1_far, narrow).astype(F32)
    else:
        over = lambda a, b: jnp.einsum("mri,mrj->ij", a, b, preferred_element_type=F32)
        reduce_w = lambda g: reduce_weight(g.astype(BF16), count, data_size, narrow_size)
        gw_embed = reduce_w(over(head_hid, grad_embed))
        gw_hidden = reduce_w(jnp.dot(pooled.T, grad_head, preferred_element_type=F32))
        gw_expand = reduce_w(over(hid_two, w3_full))
        at = sizes.crop_at
        real = lambda t: (t[:, :view_rows], t[:, at : at + crop_rows])
        cols = [
            spread_taps(part.reshape(-1, side, side, mid), side).reshape(micros, -1, 9, mid)
            for part, side in zip(real(rest[0]), (VSIDE, CSIDE))
        ]
        by_tap = jnp.einsum(
            "mri,mrtj->tij", jnp.concatenate(real(hid_one), axis=1), jnp.concatenate(cols, axis=1),
            preferred_element_type=F32,
        )[::-1]
        gw_spatial = reduce_w(by_tap.reshape(9 * mid, mid))
        gw_reduce = reduce_w(over(pixels, grad_one))
    gain_grad = lambda sums: jnp.sum(sums[:, 1], axis=0)
    shift_grad = lambda sums: jnp.sum(sums[:, 0], axis=0)
    return (
        loss.reshape(micros, own), grad_views, grad_crops,
        gw_reduce, gain_grad(sum_one), shift_grad(sum_one),
        gw_spatial, gain_grad(sum_two), shift_grad(sum_two),
        gw_expand, gain_grad(sum_three), shift_grad(sum_three),
        gw_hidden, gain_grad(sum_head), shift_grad(sum_head),
        gw_embed,
    )


def solution(mesh):
    rows = P(None, BOTH, None)
    return jax.shard_map(
        body,
        mesh=mesh,
        in_specs=(rows, rows) + (P(),) * 14,
        out_specs=(
            P(None, BOTH), rows, rows,
            P("dp", None), P(), P(),
            P("dp", None), P(), P(),
            P("dp", None), P(), P(),
            P("dp", None), P(), P(),
            P("dp", None),
        ),
        check_vma=False,
    )
```
